32 devices in a mesh: seq: 16 (over z, y, x), batch: 2 (over core).
Axes of the slice: x: 2, y: 2, z: 4, core: 2. Of those that a mesh axis runs over, the one named last changes fastest.
Arguments:
- inputs: bfloat16 [2, 16384, 768], P('batch', 'seq'), may hold values from -6 to 6
- selection: int32 [2, 256, 16], P('batch', 'seq'), may hold values from 0 to 255, as said below
- cotangent: bfloat16 [2, 16384, 768], P('batch', 'seq'), may hold values from -6 to 6
- ln1_gain: bfloat16 [768], P(('seq', 'batch')), may hold values from 0.5 to 1.5
- ln1_bias: bfloat16 [768], P(('seq', 'batch')), may hold values from -1 to 1
- w_qkv: bfloat16 [768, 2304], P(('seq', 'batch')), may hold values from -0.21875 to 0.21875
- w_out: bfloat16 [768, 768], P(('seq', 'batch')), may hold values from -1.75 to 1.75
- ln2_gain: bfloat16 [768], P(('seq', 'batch')), may hold values from 0.5 to 1.5
- ln2_bias: bfloat16 [768], P(('seq', 'batch')), may hold values from -1 to 1
- w_up: bfloat16 [768, 3072], P(('seq', 'batch')), may hold values from -0.21875 to 0.21875
- w_down: bfloat16 [3072, 768], P(('seq', 'batch')), may hold values from -0.109375 to 0.109375
Outputs:
- output: bfloat16 [2, 16384, 768], P('batch', 'seq')
- input_grad: float32 [2, 16384, 768], P('batch', 'seq')
- grad_ln1_gain: float32 [768], P(('seq', 'batch'))
- grad_ln1_bias: float32 [768], P(('seq', 'batch'))
- grad_qkv: float32 [768, 2304], P(('seq', 'batch'))
- grad_out: float32 [768, 768], P(('seq', 'batch'))
- grad_ln2_gain: float32 [768], P(('seq', 'batch'))
- grad_ln2_bias: float32 [768], P(('seq', 'batch'))
- grad_up: float32 [768, 3072], P(('seq', 'batch'))
- grad_down: float32 [3072, 768], P(('seq', 'batch'))
The draws below stay inside these ranges and needn't reach their ends.
Inputs may be any that keep to these rules, and one draw needn't show every extreme that they name: For query block b of a sequence the 16 entries of selection are distinct and exactly min(b, 16) of them are below b.
All inputs are finite; a program needn't handle non-finite values.
Results may differ from the reference program's by a relative error of at most 0.01.
Values may be sent and summed in bfloat16 or wider, within the bound.
No kernel may reach another device: no remote copies, remote signals or barrier semaphores. Data moves between devices by JAX's collectives and lax.ppermute only.
A program may use at most 192 MiB of HBM per device.

```python
from functools import partial
import jax
import jax.numpy as jnp
from jax import lax

D = 768
HEADS = 12
HEAD = 64
FF = 3072
BLOCK = 64
TOPK = 16
SEQUENCE_COUNT = 2
LEN = 16384
NB = 256
BLOCKS_PER_CHIPSET = 16


def draw_selection(key, part):
    key = jax.random.fold_in(key, 7)
    key_reward, key_jitter = jax.random.split(key)
    holder_count = NB // BLOCKS_PER_CHIPSET
    holder_reward = jax.random.randint(key_reward, (SEQUENCE_COUNT, 1, holder_count), 0, 3 * 16384)
    holder_reward = jnp.repeat(holder_reward, BLOCKS_PER_CHIPSET, axis=2)
    jitter_sample = jax.random.randint(key_jitter, (SEQUENCE_COUNT, NB, NB), 0, 16384)
    candidate_block = jnp.arange(NB, dtype=jnp.int32)[None, None, :]
    query_block = jnp.arange(NB, dtype=jnp.int32)[None, :, None]
    rank_order = (jitter_sample + holder_reward) * 1024 + candidate_block
    is_valid = candidate_block < query_block
    rank_order = jnp.where(is_valid, rank_order, candidate_block - NB)
    unused, picked = lax.top_k(rank_order, TOPK)
    return picked.astype(jnp.int32)


def block_levels(key, shape, cuts, smallest, top_value):
    gain = 1.0
    for axis_at, blocks in cuts:
        draws = jax.random.uniform(jax.random.fold_in(jax.random.fold_in(key, 6), axis_at), (blocks,), jnp.float32, smallest / len(cuts), top_value / len(cuts))
        gain = gain * jnp.repeat(jnp.exp(draws), shape[axis_at] // blocks).reshape((-1,) + (1,) * (len(shape) - 1 - axis_at))
    return gain


def noise(stream_key, shape, deviation, limit, cuts=(), kind=jnp.bfloat16):
    factor_of = block_levels(stream_key, shape, cuts, -0.22, 0.18) if cuts else 1.0
    values = jax.random.normal(stream_key, shape, jnp.float32) * deviation * factor_of
    return jnp.minimum(jnp.maximum(values, -limit), limit).astype(kind)


def setup_inputs(seed: int = 0) -> dict:
    streams_of = jax.random.split(jax.random.key(seed), 12)
    return {
        "inputs": noise(streams_of[0], (SEQUENCE_COUNT, LEN, D), 1.0, 6.0, ((0, 2), (1, 16))),
        "selection": draw_selection(jax.random.fold_in(streams_of[11], 71), 0),
        "cotangent": noise(streams_of[2], (SEQUENCE_COUNT, LEN, D), 1.0, 6.0, ((0, 2), (1, 16))),
        "ln1_gain": jnp.clip(1.0 + 0.1 * jax.random.normal(streams_of[3], (D,), jnp.float32), 0.5, 1.5).astype(jnp.bfloat16),
        "ln1_bias": noise(streams_of[4], (D,), 0.2, 1.0, ((0, 32),)),
        "w_qkv": noise(streams_of[5], (D, 3 * D), D ** -0.5, 0.21875, ((0, 32),)),
        "w_out": noise(streams_of[6], (D, D), (D // 64) ** -0.5, 1.75, ((0, 32),)),
        "ln2_gain": jnp.clip(1.0 + 0.1 * jax.random.normal(streams_of[7], (D,), jnp.float32), 0.5, 1.5).astype(jnp.bfloat16),
        "ln2_bias": noise(streams_of[8], (D,), 0.2, 1.0, ((0, 32),)),
        "w_up": noise(streams_of[9], (D, FF), D ** -0.5, 0.21875, ((0, 32),)),
        "w_down": noise(streams_of[10], (FF, D), FF ** -0.5, 0.109375, ((0, 32),)),
    }


@jax.custom_vjp
def low(v):
    return lax.optimization_barrier(v.astype(jnp.bfloat16)).astype(jnp.float32)

@jax.custom_vjp
def low_back(v):
    return v

def low_keep(v):
    return (low(v), None)

def low_pass(kept, grad):
    return (grad,)

def back_keep(v):
    return (v, None)

def back_low(kept, grad):
    return (low(grad),)
low.defvjp(low_keep, low_pass)
low_back.defvjp(back_keep, back_low)

def matmul(left_side, right_side):
    return jnp.dot(left_side, right_side, precision=lax.Precision.HIGHEST)

def layer_norm(values, norm_gain, offset):
    center = values - lax.optimization_barrier(jnp.mean(values, axis=-1, keepdims=True))
    spread = lax.optimization_barrier(jnp.mean(center * center, axis=-1, keepdims=True))
    return center * lax.rsqrt(spread + 1e-05) * norm_gain + offset

def attend_group(pooled, group_data):
    pooled_keys, pooled_values = pooled
    queries, keys_now, values_now, keys_prev, values_prev, chosen, first_block = group_data
    row_total = queries.shape[0]
    blocks = row_total // BLOCK
    query4 = queries.reshape(blocks, BLOCK, HEADS, HEAD)
    key_blocks = jnp.concatenate([keys_prev[None], keys_now.reshape(blocks, BLOCK, D)], 0)
    value_blocks = jnp.concatenate([values_prev[None], values_now.reshape(blocks, BLOCK, D)], 0)
    keys_win = jnp.concatenate([key_blocks[:-1], key_blocks[1:]], 1).reshape(blocks, 2 * BLOCK, HEADS, HEAD)
    values_win = jnp.concatenate([value_blocks[:-1], value_blocks[1:]], 1).reshape(blocks, 2 * BLOCK, HEADS, HEAD)
    key_pick = pooled_keys[chosen].reshape(blocks, TOPK, HEADS, HEAD)
    value_pick = pooled_values[chosen].reshape(blocks, TOPK, HEADS, HEAD)
    near_scores = jnp.einsum('bqhe,bkhe->bhqk', query4, keys_win, precision=lax.Precision.HIGHEST)
    far_scores = jnp.einsum('bqhe,bshe->bhqs', query4, key_pick, precision=lax.Precision.HIGHEST)
    scores = low_back(jnp.concatenate([near_scores, far_scores], -1) * HEAD ** (-0.5))
    block_ids = first_block + jnp.arange(blocks, dtype=jnp.int32)
    query_pos = block_ids[:, None] * BLOCK + jnp.arange(BLOCK, dtype=jnp.int32)[None, :]
    key_pos = (block_ids[:, None] - 1) * BLOCK + jnp.arange(2 * BLOCK, dtype=jnp.int32)[None, :]
    near_allowed = (key_pos[:, None, :] <= query_pos[:, :, None]) & (key_pos[:, None, :] > query_pos[:, :, None] - BLOCK) & (key_pos[:, None, :] >= 0)
    far_allowed = jnp.broadcast_to((chosen < block_ids[:, None])[:, None, :], (blocks, BLOCK, TOPK))
    allowed = jnp.concatenate([near_allowed, far_allowed], -1)[:, None]
    masked = jnp.where(allowed, scores, -1e+30)
    row_max = lax.optimization_barrier(jnp.max(masked, axis=-1, keepdims=True))
    weights = jnp.exp(masked - row_max)
    attn_probs = low(weights / lax.optimization_barrier(jnp.sum(weights, axis=-1, keepdims=True)))
    mixed_out = jnp.einsum('bhqk,bkhe->bqhe', attn_probs[..., :2 * BLOCK], values_win, precision=lax.Precision.HIGHEST)
    mixed_out = mixed_out + jnp.einsum('bhqs,bshe->bqhe', attn_probs[..., 2 * BLOCK:], value_pick, precision=lax.Precision.HIGHEST)
    return mixed_out.reshape(row_total, D)

def attention(queries, keys_all, values_all, chosen):
    group_rows = 512
    group_count = LEN // group_rows
    per_group = group_rows // BLOCK
    pooled_keys = low(lax.optimization_barrier(jnp.mean(keys_all.reshape(NB, BLOCK, D), axis=1)))
    pooled_values = low(lax.optimization_barrier(jnp.mean(values_all.reshape(NB, BLOCK, D), axis=1)))
    zero_rows = jnp.zeros((BLOCK, D), jnp.float32)
    keys_shift = jnp.concatenate([zero_rows, keys_all], 0)[:LEN]
    values_shift = jnp.concatenate([zero_rows, values_all], 0)[:LEN]
    scanned = (queries.reshape(group_count, group_rows, D), keys_all.reshape(group_count, group_rows, D), values_all.reshape(group_count, group_rows, D), keys_shift.reshape(group_count, group_rows, D)[:, :BLOCK], values_shift.reshape(group_count, group_rows, D)[:, :BLOCK], chosen.reshape(group_count, per_group, TOPK), jnp.arange(group_count, dtype=jnp.int32) * per_group)
    group_out = lax.map(jax.checkpoint(partial(attend_group, (pooled_keys, pooled_values))), scanned)
    return group_out.reshape(LEN, D)

def block_layer(params, inputs, chosen):
    gain_one, bias_one, w_qkv, w_out, gain_two, bias_two, w_up, w_down = params
    normed = low(layer_norm(inputs, gain_one, bias_one))
    mixed = low_back(low(matmul(normed, w_qkv)))
    attended = low_back(low(attention(mixed[:, :D], mixed[:, D:2 * D], mixed[:, 2 * D:], chosen)))
    after_attn = inputs + low_back(matmul(attended, w_out))
    normed_two = low(layer_norm(after_attn, gain_two, bias_two))
    hidden = low_back(matmul(normed_two, w_up))
    active = low(jax.nn.gelu(hidden, approximate=True))
    return after_attn + low_back(matmul(active, w_down))

def reference(inputs, selection, cotangent, ln1_gain, ln1_bias, w_qkv, w_out, ln2_gain, ln2_bias, w_up, w_down):
    params = tuple((item.astype(jnp.float32) for item in (ln1_gain, ln1_bias, w_qkv, w_out, ln2_gain, ln2_bias, w_up, w_down)))

    def forward(weights, tokens):

        def per_sequence(seq_pair):
            return block_layer(weights, seq_pair[0], seq_pair[1])
        return lax.map(jax.checkpoint(per_sequence), (tokens, selection))
    result, pullback = jax.vjp(forward, params, inputs.astype(jnp.float32))
    gradients, grad_in = pullback(cotangent.astype(jnp.float32))
    return (result.astype(jnp.bfloat16), grad_in, gradients[0], gradients[1], gradients[2], gradients[3], gradients[4], gradients[5], gradients[6], gradients[7])
```

```python
from functools import partial

import jax
import jax.numpy as jnp
from jax import lax
from jax.experimental import pallas as pl
from jax.experimental.pallas import tpu as pltpu
from jax.sharding import PartitionSpec as P

HEADS = 12
HEAD = 64
BLOCK = 64
TOPK = 16
QUAD = 4 * HEAD
FOLD = BLOCK + TOPK
NEG = -1e30


def dot_nn(a, b):
    return lax.dot_general(a, b, (((1,), (0,)), ((), ())), preferred_element_type=jnp.float32)


def dot_nt(a, b):
    return lax.dot_general(a, b, (((1,), (1,)), ((), ())), preferred_element_type=jnp.float32)


def dot_tn(a, b):
    return lax.dot_general(a, b, (((0,), (0,)), ((), ())), preferred_element_type=jnp.float32)


def spread_heads(rows):
    lane = lax.broadcasted_iota(jnp.int32, rows.shape, 1) // HEAD
    zero = jnp.zeros_like(rows)
    return jnp.concatenate([jnp.where(lane == h, rows, zero) for h in range(4)], 0)


def gather_heads(full):
    lane = lax.broadcasted_iota(jnp.int32, (BLOCK, QUAD), 1) // HEAD
    out = full[:BLOCK]
    for h in range(1, 4):
        out = jnp.where(lane == h, full[h * BLOCK : (h + 1) * BLOCK], out)
    return out


def prev_side():
    k = lax.broadcasted_iota(jnp.int32, (BLOCK, QUAD), 0)
    q = lax.broadcasted_iota(jnp.int32, (BLOCK, QUAD), 1) % BLOCK
    return k > q


def unfold(near, far, prev):
    zero = jnp.zeros_like(near)
    both = [jnp.where(prev, near, zero), jnp.where(prev, zero, near), far]
    return jnp.concatenate(both, 0).astype(jnp.bfloat16)


def attend_kernel(
    first_ref, sel_ref, bias_ref, pool_ref, prev_ref, cur_ref, att_ref, probs_ref, picks_ref
):
    c = pl.program_id(0)
    width = HEADS * HEAD

    @pl.when(c == 0)
    def _():
        pool_rows = pool_ref.shape[0]
        ids = lax.broadcasted_iota(jnp.int32, (sel_ref.shape[0], pool_rows), 1)
        one_hot = (ids == sel_ref[...]).astype(jnp.float32).astype(jnp.bfloat16)
        picks_ref[...] = dot_nn(one_hot, pool_ref[:, width:]).astype(jnp.bfloat16)

    prev = prev_side()
    edge = jnp.where((c == 0) & (first_ref[0] == 1), NEG, 0.0)
    picked = picks_ref[pl.ds(pl.multiple_of(c * TOPK, TOPK), TOPK), :]
    for g in range(HEADS // 4):
        lanes = slice(g * QUAD, (g + 1) * QUAD)
        klanes = slice(width + g * QUAD, width + (g + 1) * QUAD)
        vlanes = slice(2 * width + g * QUAD, 2 * width + (g + 1) * QUAD)
        plk = slice(g * QUAD, (g + 1) * QUAD)
        plv = slice(width + g * QUAD, width + (g + 1) * QUAD)
        keys = jnp.concatenate([prev_ref[:, klanes], cur_ref[:, klanes], picked[:, plk]], 0)
        values = jnp.concatenate([prev_ref[:, vlanes], cur_ref[:, vlanes], picked[:, plv]], 0)
        wide_q = spread_heads(cur_ref[:, lanes])
        scores = dot_nt(keys, wide_q) * HEAD ** (-0.5)
        near = jnp.where(prev, scores[:BLOCK] + edge, scores[BLOCK : 2 * BLOCK])
        far = scores[2 * BLOCK :] + bias_ref[...]
        folded = jnp.concatenate([near, far], 0)
        top = jnp.max(folded, axis=0, keepdims=True)
        weights = jnp.exp(folded - top)
        probs = weights * (1.0 / jnp.sum(weights, axis=0, keepdims=True))
        probs_ref[0, g] = probs
        full = unfold(probs[:BLOCK], probs[BLOCK:], prev)
        att_ref[:, lanes] = gather_heads(dot_tn(full, values)).astype(jnp.bfloat16)


def attend(mixed, sel_col, bias_col, first, blocks, pool_rows):
    width = HEADS * HEAD
    base = pool_rows // BLOCK
    return pl.pallas_call(
        attend_kernel,
        grid_spec=pltpu.PrefetchScalarGridSpec(
            num_scalar_prefetch=1,
            grid=(blocks,),
            in_specs=[
                pl.BlockSpec((blocks * TOPK, 1), lambda c, f: (0, 0)),
                pl.BlockSpec((TOPK, 1), lambda c, f: (c, 0)),
                pl.BlockSpec((pool_rows, 3 * width), lambda c, f: (0, 0)),
                pl.BlockSpec((BLOCK, 3 * width), lambda c, f: (base + c, 0)),
                pl.BlockSpec((BLOCK, 3 * width), lambda c, f: (base + c + 1, 0)),
            ],
            out_specs=[
                pl.BlockSpec((BLOCK, width), lambda c, f: (c, 0)),
                pl.BlockSpec((1, HEADS // 4, FOLD, QUAD), lambda c, f: (c, 0, 0, 0)),
                pl.BlockSpec((blocks * TOPK, 2 * width), lambda c, f: (0, 0)),
            ],
        ),
        out_shape=[
            jax.ShapeDtypeStruct((blocks * BLOCK, width), jnp.bfloat16),
            jax.ShapeDtypeStruct((blocks, HEADS // 4, FOLD, QUAD), jnp.float32),
            jax.ShapeDtypeStruct((blocks * TOPK, 2 * width), jnp.bfloat16),
        ],
        compiler_params=pltpu.CompilerParams(vmem_limit_bytes=32 * 1024 * 1024),
        name="attend",
    )(first, sel_col, bias_col, mixed, mixed, mixed)


def attend_back_kernel(
    blocks, sel_ref, prev_ref, cur_ref, picks_ref, probs_ref, datt_ref, out_ref, carry, dpicks
):
    i = pl.program_id(0)
    width = HEADS * HEAD

    @pl.when(i == 0)
    def _():
        carry[...] = jnp.zeros_like(carry)

    @pl.when(i < blocks)
    def _():
        prev = prev_side()
        row = pl.multiple_of(i * TOPK, TOPK)
        for g in range(HEADS // 4):
            lanes = slice(g * QUAD, (g + 1) * QUAD)
            klanes = slice(width + g * QUAD, width + (g + 1) * QUAD)
            vlanes = slice(2 * width + g * QUAD, 2 * width + (g + 1) * QUAD)
            keys = jnp.concatenate([prev_ref[:, klanes], cur_ref[:, klanes], picks_ref[:, lanes]], 0)
            values = jnp.concatenate(
                [prev_ref[:, vlanes], cur_ref[:, vlanes], picks_ref[:, klanes]], 0
            )
            wide_q = spread_heads(cur_ref[:, lanes])
            wide_d = spread_heads(datt_ref[:, lanes])
            probs = probs_ref[0, g]
            dprobs = dot_nt(values, wide_d)
            near = jnp.where(prev, dprobs[:BLOCK], dprobs[BLOCK : 2 * BLOCK])
            folded = jnp.concatenate([near, dprobs[2 * BLOCK :]], 0)
            inner = jnp.sum(probs * folded, axis=0, keepdims=True)
            dscores = probs * (folded - inner) * HEAD ** (-0.5)
            full_p = unfold(probs[:BLOCK], probs[BLOCK:], prev)
            full_d = unfold(dscores[:BLOCK], dscores[BLOCK:], prev)
            dvals = dot_nn(full_p, wide_d)
            dkeys = dot_nn(full_d, wide_q)
            dq = gather_heads(dot_tn(full_d, keys))
            out_ref[:, lanes] = carry[:, lanes].astype(jnp.bfloat16)
            out_ref[:, klanes] = (carry[:, klanes] + dkeys[:BLOCK]).astype(jnp.bfloat16)
            out_ref[:, vlanes] = (carry[:, vlanes] + dvals[:BLOCK]).astype(jnp.bfloat16)
            carry[:, lanes] = dq
            carry[:, klanes] = dkeys[BLOCK : 2 * BLOCK]
            carry[:, vlanes] = dvals[BLOCK : 2 * BLOCK]
            dpicks[pl.ds(row, TOPK), lanes] = dkeys[2 * BLOCK :].astype(jnp.bfloat16)
            dpicks[pl.ds(row, TOPK), klanes] = dvals[2 * BLOCK :].astype(jnp.bfloat16)

    @pl.when(i == blocks)
    def _():
        out_ref[...] = carry[...].astype(jnp.bfloat16)

    @pl.when(i > blocks)
    def _():
        ids = lax.broadcasted_iota(jnp.int32, (BLOCK, blocks * TOPK), 0) + (i - blocks - 1) * BLOCK
        one_hot = (ids == sel_ref[...]).astype(jnp.float32).astype(jnp.bfloat16)
        out_ref[:, :width] = jnp.zeros((BLOCK, width), jnp.bfloat16)
        out_ref[:, width:] = dot_nn(one_hot, dpicks[...]).astype(jnp.bfloat16)


def attend_back(mixed, sel_row, picks, probs, datt, blocks, pool_rows):
    width = HEADS * HEAD
    base = pool_rows // BLOCK
    last = blocks - 1

    def query_block(i):
        return jnp.minimum(i, last)

    return pl.pallas_call(
        partial(attend_back_kernel, blocks),
        grid=(blocks + 1 + base,),
        in_specs=[
            pl.BlockSpec((1, blocks * TOPK), lambda i: (0, 0)),
            pl.BlockSpec((BLOCK, 3 * width), lambda i: (base + query_block(i), 0)),
            pl.BlockSpec((BLOCK, 3 * width), lambda i: (base + query_block(i) + 1, 0)),
            pl.BlockSpec((TOPK, 2 * width), lambda i: (query_block(i), 0)),
            pl.BlockSpec((1, HEADS // 4, FOLD, QUAD), lambda i: (query_block(i), 0, 0, 0)),
            pl.BlockSpec((BLOCK, width), lambda i: (query_block(i), 0)),
        ],
        out_specs=pl.BlockSpec(
            (BLOCK, 3 * width), lambda i: (jnp.where(i > blocks, i - blocks - 1, base + i), 0)
        ),
        out_shape=jax.ShapeDtypeStruct((pool_rows + (blocks + 1) * BLOCK, 3 * width), jnp.bfloat16),
        scratch_shapes=[
            pltpu.VMEM((BLOCK, 3 * width), jnp.float32),
            pltpu.VMEM((blocks * TOPK, 2 * width), jnp.bfloat16),
        ],
        compiler_params=pltpu.CompilerParams(vmem_limit_bytes=32 * 1024 * 1024),
        name="attend_back",
    )(sel_row, mixed, mixed, picks, probs, datt)


def standardize(values):
    center = values - jnp.mean(values, axis=-1, keepdims=True)
    spread = jnp.mean(center * center, axis=-1, keepdims=True)
    scale = lax.rsqrt(spread + 1e-05)
    return center * scale, scale


def standardize_back(unit, scale, dunit):
    return scale * (
        dunit
        - jnp.mean(dunit, axis=-1, keepdims=True)
        - unit * jnp.mean(dunit * unit, axis=-1, keepdims=True)
    )


def shift_seq(value, distance):
    size = lax.axis_size("seq")
    route = [(i - distance, i) for i in range(size) if 0 <= i - distance < size]
    return lax.ppermute(value, "seq", route)


def gather_small(rows):
    size = lax.axis_size("seq")
    return lax.all_to_all(jnp.tile(rows, (size, 1)), "seq", 0, 0, tiled=True)


def scatter_small(rows):
    size = lax.axis_size("seq")
    parts = lax.all_to_all(rows, "seq", 0, 0, tiled=True)
    return jnp.sum(parts.reshape(size, -1, rows.shape[1]).astype(jnp.float32), axis=0)


BOTH = ("seq", "batch")


def local(
    inputs, selection, cotangent, ln1_gain, ln1_bias, w_qkv, w_out, ln2_gain, ln2_bias, w_up, w_down
):
    bf16, f32 = jnp.bfloat16, jnp.float32
    tokens_low = inputs[0]
    chosen = selection[0]
    count, width = tokens_low.shape
    blocks = count // BLOCK
    pool_rows = blocks * lax.axis_size("seq")
    at = lax.axis_index("seq")

    vectors = lax.all_gather(
        jnp.stack([ln1_gain, ln1_bias, ln2_gain, ln2_bias]), BOTH, axis=1, tiled=True
    ).astype(f32)
    gain_one, bias_one, gain_two, bias_two = vectors
    mat_qkv = lax.all_gather(w_qkv, BOTH, axis=0, tiled=True)
    mat_out = lax.all_gather(w_out, BOTH, axis=0, tiled=True)
    mat_up = lax.all_gather(w_up, BOTH, axis=0, tiled=True)
    mat_down = lax.all_gather(w_down, BOTH, axis=0, tiled=True)

    tokens = tokens_low.astype(f32)
    unit, unit_scale = standardize(tokens)
    unit_halo, _ = standardize(shift_seq(tokens_low[-BLOCK:], 1).astype(f32))
    unit_pool = gather_small(jnp.mean(unit.reshape(blocks, BLOCK, width), axis=1).astype(bf16))
    unit_ext = jnp.concatenate([unit_pool.astype(f32), unit_halo, unit], 0)
    normed = (unit_ext * gain_one + bias_one).astype(bf16)
    mixed = dot_nn(normed, mat_qkv).astype(bf16)

    block_ids = at * blocks + jnp.arange(blocks, dtype=jnp.int32)
    flat = chosen.reshape(blocks * TOPK)
    far_bias = jnp.where(chosen < block_ids[:, None], 0.0, NEG).reshape(blocks * TOPK, 1)
    first = (at == 0).astype(jnp.int32)[None]
    attended, probs, picks = attend(mixed, flat[:, None], far_bias, first, blocks, pool_rows)

    after = tokens + dot_nn(attended, mat_out)
    unit_two, scale_two = standardize(after)
    normed_two = (unit_two * gain_two + bias_two).astype(bf16)
    hidden = dot_nn(normed_two, mat_up)
    active, gelu_back = jax.vjp(partial(jax.nn.gelu, approximate=True), hidden)
    active = active.astype(bf16)
    output = (after + dot_nn(active, mat_down)).astype(bf16)

    upstream = cotangent[0]
    dhidden = gelu_back(dot_nt(upstream, mat_down))[0].astype(bf16)
    grad_down = dot_tn(active, upstream).astype(bf16)
    grad_up = dot_tn(normed_two, dhidden).astype(bf16)
    dnormed_two = dot_nt(dhidden, mat_up)
    grad_gain_two = jnp.sum(dnormed_two * unit_two, axis=0)
    grad_bias_two = jnp.sum(dnormed_two, axis=0)
    dafter = upstream.astype(f32) + standardize_back(unit_two, scale_two, dnormed_two * gain_two)
    dafter_low = dafter.astype(bf16)
    grad_out = dot_tn(attended, dafter_low).astype(bf16)
    dattended = dot_nt(dafter_low, mat_out).astype(bf16)

    dmixed = attend_back(mixed, flat[None, :], picks, probs, dattended, blocks, pool_rows)
    grad_qkv = dot_tn(normed, dmixed).astype(bf16)
    dnormed = dot_nt(dmixed, mat_qkv)
    grad_gain_one = jnp.sum(dnormed * unit_ext, axis=0)
    grad_bias_one = jnp.sum(dnormed, axis=0)
    from_pool = scatter_small(dnormed[:pool_rows].astype(bf16)) * (1.0 / BLOCK)
    from_next = shift_seq(dnormed[pool_rows : pool_rows + BLOCK].astype(bf16), -1).astype(f32)
    dtoken = (
        dnormed[pool_rows + BLOCK :]
        + jnp.repeat(from_pool, BLOCK, axis=0)
        + jnp.pad(from_next, ((count - BLOCK, 0), (0, 0)))
    )
    input_grad = dafter + standardize_back(unit, unit_scale, dtoken * gain_one)

    columns = jnp.stack([grad_gain_one, grad_bias_one, grad_gain_two, grad_bias_two], 1)
    columns = jnp.pad(columns.astype(bf16), ((0, 0), (0, 124)))

    def scatter(value):
        return lax.psum_scatter(value, BOTH, scatter_dimension=0, tiled=True).astype(f32)

    own_down = scatter(grad_down)
    own_up = scatter(grad_up)
    own_qkv = scatter(jnp.concatenate([grad_qkv, grad_out, columns], 1))
    split = 3 * width
    tail = own_qkv[:, split + width :]
    return (
        output[None],
        input_grad[None],
        tail[:, 0],
        tail[:, 1],
        own_qkv[:, :split],
        own_qkv[:, split : split + width],
        tail[:, 2],
        tail[:, 3],
        own_up,
        own_down,
    )


def solution(mesh):
    tokens = P("batch", "seq", None)
    vector = P(BOTH)
    matrix = P(BOTH, None)
    return jax.shard_map(
        local,
        mesh=mesh,
        in_specs=(
            tokens,
            tokens,
            tokens,
            vector,
            vector,
            matrix,
            matrix,
            vector,
            vector,
            matrix,
            matrix,
        ),
        out_specs=(
            tokens,
            tokens,
            vector,
            vector,
            matrix,
            matrix,
            vector,
            vector,
            matrix,
            matrix,
        ),
        check_vma=False,
    )
```

```python
from functools import partial

import jax
import jax.numpy as jnp
from jax import lax
from jax.experimental import pallas as pl
from jax.experimental.pallas import tpu as pltpu
from jax.sharding import PartitionSpec as P

HEADS = 12
HEAD = 64
BLOCK = 64
TOPK = 16
QUAD = 4 * HEAD
FOLD = BLOCK + TOPK
NEG = -1e30


def dot_nn(a, b):
    return lax.dot_general(a, b, (((1,), (0,)), ((), ())), preferred_element_type=jnp.float32)


def dot_nt(a, b):
    return lax.dot_general(a, b, (((1,), (1,)), ((), ())), preferred_element_type=jnp.float32)


def dot_tn(a, b):
    return lax.dot_general(a, b, (((0,), (0,)), ((), ())), preferred_element_type=jnp.float32)


def spread_heads(rows):
    lane = lax.broadcasted_iota(jnp.int32, rows.shape, 1) // HEAD
    zero = jnp.zeros_like(rows)
    return jnp.concatenate([jnp.where(lane == h, rows, zero) for h in range(4)], 0)


def gather_heads(full):
    lane = lax.broadcasted_iota(jnp.int32, (BLOCK, QUAD), 1) // HEAD
    out = full[:BLOCK]
    for h in range(1, 4):
        out = jnp.where(lane == h, full[h * BLOCK : (h + 1) * BLOCK], out)
    return out


def prev_side():
    k = lax.broadcasted_iota(jnp.int32, (BLOCK, QUAD), 0)
    q = lax.broadcasted_iota(jnp.int32, (BLOCK, QUAD), 1) % BLOCK
    return k > q


def unfold(near, far, prev):
    zero = jnp.zeros_like(near)
    both = [jnp.where(prev, near, zero), jnp.where(prev, zero, near), far]
    return jnp.concatenate(both, 0).astype(jnp.bfloat16)


HALF = HEADS // 2 * HEAD


def load_quad(own_ref, other_ref, part, g):
    at = part * HALF
    if g == 0:
        return own_ref[:, at : at + QUAD]
    if g == 1:
        return jnp.concatenate(
            [own_ref[:, at + QUAD : at + HALF], other_ref[:, at : at + HALF - QUAD]], 1
        )
    return other_ref[:, at + HALF - QUAD : at + HALF]


def join_quads(quads):
    own = jnp.concatenate([quads[0], quads[1][:, : HALF - QUAD]], 1)
    other = jnp.concatenate([quads[1][:, HALF - QUAD :], quads[2]], 1)
    return own, other


def attend_kernel(
    info_ref,
    sel_ref,
    bias_ref,
    pool_own,
    prev_own,
    cur_own,
    pool_other,
    prev_other,
    cur_other,
    att_ref,
    probs_ref,
    picks_ref,
):
    c = pl.program_id(0)
    core = info_ref[1]

    @pl.when(c == 0)
    def _():
        pool_rows = pool_own.shape[0]
        ids = lax.broadcasted_iota(jnp.int32, (sel_ref.shape[0], pool_rows), 1)
        one_hot = (ids == sel_ref[...]).astype(jnp.float32).astype(jnp.bfloat16)
        picks_ref[0] = dot_nn(one_hot, pool_own[:, HALF:]).astype(jnp.bfloat16)
        picks_ref[1] = dot_nn(one_hot, pool_other[:, HALF:]).astype(jnp.bfloat16)

    prev = prev_side()
    edge = jnp.where((c == 0) & (info_ref[0] == 1), NEG, 0.0)
    rows = pl.ds(pl.multiple_of(c * TOPK, TOPK), TOPK)
    pick_own, pick_other = picks_ref.at[0, rows], picks_ref.at[1, rows]
    outs = []
    for g in range(HEADS // 4):
        keys, values = [
            jnp.concatenate(
                [
                    load_quad(prev_own, prev_other, part, g),
                    load_quad(cur_own, cur_other, part, g),
                    load_quad(pick_own, pick_other, part - 1, g),
                ],
                0,
            )
            for part in (1, 2)
        ]
        wide_q = spread_heads(load_quad(cur_own, cur_other, 0, g))
        scores = dot_nt(keys, wide_q) * HEAD ** (-0.5)
        near = jnp.where(prev, scores[:BLOCK] + edge, scores[BLOCK : 2 * BLOCK])
        far = scores[2 * BLOCK :] + bias_ref[...]
        folded = jnp.concatenate([near, far], 0)
        top = jnp.max(folded, axis=0, keepdims=True)
        weights = jnp.exp(folded - top)
        probs = weights * (1.0 / jnp.sum(weights, axis=0, keepdims=True))
        probs_ref[0, g] = probs
        full = unfold(probs[:BLOCK], probs[BLOCK:], prev)
        outs.append(gather_heads(dot_tn(full, values)).astype(jnp.bfloat16))
    own, other = join_quads(outs)
    att_ref[:, pl.ds(pl.multiple_of(core * HALF, 128), HALF)] = own
    att_ref[:, pl.ds(pl.multiple_of((1 - core) * HALF, 128), HALF)] = other


def attend(mixed_own, mixed_other, sel_col, bias_col, info, blocks, pool_rows):
    width = HEADS * HEAD
    base = pool_rows // BLOCK
    mixed_specs = [
        pl.BlockSpec((pool_rows, 3 * HALF), lambda c, f: (0, 0)),
        pl.BlockSpec((BLOCK, 3 * HALF), lambda c, f: (base + c, 0)),
        pl.BlockSpec((BLOCK, 3 * HALF), lambda c, f: (base + c + 1, 0)),
    ]
    return pl.pallas_call(
        attend_kernel,
        grid_spec=pltpu.PrefetchScalarGridSpec(
            num_scalar_prefetch=1,
            grid=(blocks,),
            in_specs=[
                pl.BlockSpec((blocks * TOPK, 1), lambda c, f: (0, 0)),
                pl.BlockSpec((TOPK, 1), lambda c, f: (c, 0)),
            ]
            + mixed_specs * 2,
            out_specs=[
                pl.BlockSpec((BLOCK, width), lambda c, f: (c, 0)),
                pl.BlockSpec((1, HEADS // 4, FOLD, QUAD), lambda c, f: (c, 0, 0, 0)),
                pl.BlockSpec((2, blocks * TOPK, 2 * HALF), lambda c, f: (0, 0, 0)),
            ],
        ),
        out_shape=[
            jax.ShapeDtypeStruct((blocks * BLOCK, width), jnp.bfloat16),
            jax.ShapeDtypeStruct((blocks, HEADS // 4, FOLD, QUAD), jnp.float32),
            jax.ShapeDtypeStruct((2, blocks * TOPK, 2 * HALF), jnp.bfloat16),
        ],
        compiler_params=pltpu.CompilerParams(vmem_limit_bytes=32 * 1024 * 1024),
        cost_estimate=pl.CostEstimate(
            flops=12_000_000_000, bytes_accessed=12_000_000, transcendentals=1_000_000
        ),
        name="attend",
    )(info, sel_col, bias_col, *[mixed_own] * 3, *[mixed_other] * 3)


def attend_back_kernel(
    blocks,
    info_ref,
    sel_ref,
    prev_own,
    cur_own,
    prev_other,
    cur_other,
    picks_ref,
    probs_ref,
    datt_ref,
    out_own,
    out_other,
    carry,
    dpicks,
):
    i = pl.program_id(0)
    core = info_ref[1]

    @pl.when(i == 0)
    def _():
        carry[...] = jnp.zeros_like(carry)

    @pl.when(i < blocks)
    def _():
        prev = prev_side()
        rows = pl.ds(pl.multiple_of(i * TOPK, TOPK), TOPK)
        datt_own = datt_ref.at[:, pl.ds(pl.multiple_of(core * HALF, 128), HALF)]
        datt_other = datt_ref.at[:, pl.ds(pl.multiple_of((1 - core) * HALF, 128), HALF)]
        grads = []
        for g in range(HEADS // 4):
            keys, values = [
                jnp.concatenate(
                    [
                        load_quad(prev_own, prev_other, part, g),
                        load_quad(cur_own, cur_other, part, g),
                        load_quad(picks_ref.at[0], picks_ref.at[1], part - 1, g),
                    ],
                    0,
                )
                for part in (1, 2)
            ]
            wide_q = spread_heads(load_quad(cur_own, cur_other, 0, g))
            wide_d = spread_heads(load_quad(datt_own, datt_other, 0, g))
            probs = probs_ref[0, g]
            dprobs = dot_nt(values, wide_d)
            near = jnp.where(prev, dprobs[:BLOCK], dprobs[BLOCK : 2 * BLOCK])
            folded = jnp.concatenate([near, dprobs[2 * BLOCK :]], 0)
            inner = jnp.sum(probs * folded, axis=0, keepdims=True)
            dscores = probs * (folded - inner) * HEAD ** (-0.5)
            full_p = unfold(probs[:BLOCK], probs[BLOCK:], prev)
            full_d = unfold(dscores[:BLOCK], dscores[BLOCK:], prev)
            dvals = dot_nn(full_p, wide_d)
            dkeys = dot_nn(full_d, wide_q)
            dq = gather_heads(dot_tn(full_d, keys))
            grads.append((dq, dkeys, dvals))
        for part in range(3):
            lanes = slice(part * HALF, (part + 1) * HALF)
            halves = join_quads([grad[part] for grad in grads])
            for side, out_ref in enumerate((out_own, out_other)):
                half = halves[side]
                if part == 0:
                    out_ref[:, lanes] = carry[side, :, lanes].astype(jnp.bfloat16)
                    carry[side, :, lanes] = half
                else:
                    out_ref[:, lanes] = (carry[side, :, lanes] + half[:BLOCK]).astype(jnp.bfloat16)
                    carry[side, :, lanes] = half[BLOCK : 2 * BLOCK]
                    picked = slice((part - 1) * HALF, part * HALF)
                    dpicks[side, rows, picked] = half[2 * BLOCK :].astype(jnp.bfloat16)

    @pl.when(i == blocks)
    def _():
        out_own[...] = carry[0].astype(jnp.bfloat16)
        out_other[...] = carry[1].astype(jnp.bfloat16)

    @pl.when(i > blocks)
    def _():
        ids = lax.broadcasted_iota(jnp.int32, (BLOCK, blocks * TOPK), 0) + (i - blocks - 1) * BLOCK
        one_hot = (ids == sel_ref[...]).astype(jnp.float32).astype(jnp.bfloat16)
        for side, out_ref in enumerate((out_own, out_other)):
            out_ref[:, :HALF] = jnp.zeros((BLOCK, HALF), jnp.bfloat16)
            out_ref[:, HALF:] = dot_nn(one_hot, dpicks[side]).astype(jnp.bfloat16)


def attend_back(mixed_own, mixed_other, sel_row, info, picks, probs, datt, blocks, pool_rows):
    width = HEADS * HEAD
    base = pool_rows // BLOCK

    def query_block(i):
        return jnp.minimum(i, blocks - 1)

    def out_block(i, f):
        return (jnp.where(i > blocks, i - blocks - 1, base + i), 0)

    mixed_specs = [
        pl.BlockSpec((BLOCK, 3 * HALF), lambda i, f: (base + query_block(i), 0)),
        pl.BlockSpec((BLOCK, 3 * HALF), lambda i, f: (base + query_block(i) + 1, 0)),
    ]
    rows = pool_rows + (blocks + 1) * BLOCK
    return pl.pallas_call(
        partial(attend_back_kernel, blocks),
        grid_spec=pltpu.PrefetchScalarGridSpec(
            num_scalar_prefetch=1,
            grid=(blocks + 1 + base,),
            in_specs=[pl.BlockSpec((1, blocks * TOPK), lambda i, f: (0, 0))]
            + mixed_specs * 2
            + [
                pl.BlockSpec((2, TOPK, 2 * HALF), lambda i, f: (0, query_block(i), 0)),
                pl.BlockSpec(
                    (1, HEADS // 4, FOLD, QUAD), lambda i, f: (query_block(i), 0, 0, 0)
                ),
                pl.BlockSpec((BLOCK, width), lambda i, f: (query_block(i), 0)),
            ],
            out_specs=[pl.BlockSpec((BLOCK, 3 * HALF), out_block)] * 2,
            scratch_shapes=[
                pltpu.VMEM((2, BLOCK, 3 * HALF), jnp.float32),
                pltpu.VMEM((2, blocks * TOPK, 2 * HALF), jnp.bfloat16),
            ],
        ),
        out_shape=[jax.ShapeDtypeStruct((rows, 3 * HALF), jnp.bfloat16)] * 2,
        compiler_params=pltpu.CompilerParams(vmem_limit_bytes=32 * 1024 * 1024),
        cost_estimate=pl.CostEstimate(
            flops=20_000_000_000, bytes_accessed=18_000_000, transcendentals=0
        ),
        name="attend_back",
    )(info, sel_row, *[mixed_own] * 2, *[mixed_other] * 2, picks, probs, datt)


def standardize(values):
    center = values - jnp.mean(values, axis=-1, keepdims=True)
    spread = jnp.mean(center * center, axis=-1, keepdims=True)
    scale = lax.rsqrt(spread + 1e-05)
    return center * scale, scale


def standardize_back(unit, scale, dunit):
    return scale * (
        dunit
        - jnp.mean(dunit, axis=-1, keepdims=True)
        - unit * jnp.mean(dunit * unit, axis=-1, keepdims=True)
    )


def shift_seq(value, distance):
    size = lax.axis_size("seq")
    route = [(i - distance, i) for i in range(size) if 0 <= i - distance < size]
    return lax.ppermute(value, "seq", route)


BOTH = ("seq", "batch")

def flip_route(axis_size, bit):
    return [(i, i ^ bit) for i in range(axis_size)]

def ring_route(size, stride, steps):
    return [(i, (i + stride * steps) % size) for i in range(size)]

def swap(value, axis, bit):
    return lax.ppermute(value, axis, flip_route(lax.axis_size(axis), bit))

def in_order(bit, own, other):
    return jnp.stack([jnp.where(bit == 0, own, other), jnp.where(bit == 0, other, own)])

def gather_seq(slab, cut):
    size = lax.axis_size("seq")
    at = lax.axis_index("seq")
    layers = size // 4
    z, y, x = at // 4, at // 2 % 2, at % 2
    got = [slab] + [lax.ppermute(slab, "seq", ring_route(size, 4, k)) for k in range(1, layers)]
    stack = jnp.stack(got)
    line = jnp.concatenate([lax.dynamic_slice_in_dim(stack, (z - k) % layers, 1, 0) for k in range(layers)], 0)
    first, second = line[:, :, :cut], line[:, :, cut:]
    first_x = swap(first, "seq", 1)
    second_y = swap(second, "seq", 2)
    first = in_order(x, first, first_x)
    second = in_order(y, second, second_y)
    first_y = swap(first, "seq", 2)
    second_x = swap(second, "seq", 1)
    first = in_order(y, first, first_y)
    second = in_order(x, second, second_x)
    rows = size * slab.shape[0]
    first = jnp.transpose(first, (2, 0, 1, 3, 4)).reshape(rows, cut)
    second = jnp.transpose(second, (2, 1, 0, 3, 4)).reshape(rows, slab.shape[1] - cut)
    return jnp.concatenate([first, second], 1)

def pick(value, index, axis):
    return lax.dynamic_index_in_dim(value, index, axis, keepdims=False)

def add(a, b):
    return (a.astype(jnp.float32) + b.astype(jnp.float32)).astype(jnp.bfloat16)

def scatter_seq(full, cut):
    size = lax.axis_size("seq")
    at = lax.axis_index("seq")
    layers = size // 4
    z, y, x = at // 4, at // 2 % 2, at % 2
    grid = full.reshape(layers, 2, 2, -1, full.shape[1])
    first, second = grid[..., :cut], grid[..., cut:]
    first_got = swap(pick(first, 1 - x, 2), "seq", 1)
    second_got = swap(pick(second, 1 - y, 1), "seq", 2)
    first = add(pick(first, x, 2), first_got)
    second = add(pick(second, y, 1), second_got)
    first_got = swap(pick(first, 1 - y, 1), "seq", 2)
    second_got = swap(pick(second, 1 - x, 1), "seq", 1)
    line = jnp.concatenate([add(pick(first, y, 1), first_got), add(pick(second, x, 1), second_got)], -1)
    total = pick(line, z, 0).astype(jnp.float32)
    for k in range(1, layers):
        got = lax.ppermute(pick(line, (z + k) % layers, 0), "seq", ring_route(size, 4, k))
        total = total + got.astype(jnp.float32)
    return total


def paired():
    return lax.axis_size("batch") == 2 and lax.axis_size("seq") % 4 == 0


def side_index():
    return lax.axis_index("batch") % 2


def halves_of(matrix, groups):
    rows, columns = matrix.shape
    parts = matrix.reshape(rows, groups, 2, columns // (2 * groups))
    return jnp.transpose(parts, (2, 0, 1, 3)).reshape(2, rows, columns // 2)


def whole_of(halves, groups):
    _, rows, columns = halves.shape
    parts = halves.reshape(2, rows, groups, columns // groups)
    return jnp.transpose(parts, (1, 2, 0, 3)).reshape(rows, 2 * columns)


def gather_slab(halves):
    side = side_index()
    mine, theirs = pick(halves, side, 0), pick(halves, 1 - side, 0)
    got = swap(theirs, "batch", 1)
    return in_order(side, mine, got).reshape(-1, halves.shape[2])


def gather_halves(halves, cut):
    if paired():
        own = gather_seq(gather_slab(halves), cut)
        return own, swap(own, "batch", 1)
    full = lax.all_gather(halves, BOTH, axis=1, tiled=True)
    return pick(full, side_index(), 0), pick(full, 1 - side_index(), 0)


def scatter_halves(own, other, cut):
    side = side_index()
    if paired():
        mixed = add(own, swap(other, "batch", 1))
        total = scatter_seq(mixed, cut)
        total = total.reshape(2, -1, total.shape[1])
        got = swap(pick(total, 1 - side, 0), "batch", 1)
        return in_order(side, pick(total, side, 0), got)
    full = in_order(side, own, other)
    return lax.psum_scatter(full, BOTH, scatter_dimension=1, tiled=True).astype(jnp.float32)


def everyone(rows):
    size = lax.axis_size("seq")
    return lax.all_to_all(jnp.broadcast_to(rows, (size,) + rows.shape), "seq", 0, 0)


def gather_vectors(vectors):
    return lax.all_gather(vectors, BOTH, axis=1, tiled=True).astype(jnp.float32)


def local(
    inputs, selection, cotangent, ln1_gain, ln1_bias, w_qkv, w_out, ln2_gain, ln2_bias, w_up, w_down
):
    bf16, f32 = jnp.bfloat16, jnp.float32
    tokens_low = inputs[0]
    chosen = selection[0]
    count, width = tokens_low.shape
    blocks = count // BLOCK
    size = lax.axis_size("seq")
    pool_rows = blocks * size
    at = lax.axis_index("seq")
    side = side_index()
    vectors = jnp.stack([ln1_gain, ln1_bias, ln2_gain, ln2_bias])

    own_qkv, other_qkv = gather_halves(halves_of(w_qkv, 3), 512)
    out_up = jnp.concatenate([halves_of(w_out, 1), halves_of(w_up, 1)], 2)
    own_ou, other_ou = gather_halves(out_up, 1024)
    mat_down = lax.all_gather(w_down, BOTH, axis=0, tiled=True)
    mat_out = whole_of(in_order(side, own_ou[:, : width // 2], other_ou[:, : width // 2]), 1)
    mat_up = whole_of(in_order(side, own_ou[:, width // 2 :], other_ou[:, width // 2 :]), 1)

    tokens = tokens_low.astype(f32)
    unit, unit_scale = standardize(tokens)
    unit_halo, _ = standardize(shift_seq(tokens_low[-BLOCK:], 1).astype(f32))
    pooled = jnp.mean(unit.reshape(blocks, BLOCK, width), axis=1).astype(bf16)
    if paired():
        chip = in_order(side, vectors, swap(vectors, "batch", 1))
        chip = jnp.transpose(chip, (1, 0, 2)).reshape(1, -1)
        span = chip.shape[1]
        chip = jnp.pad(chip, ((0, 7), (0, width - span)))
        got = everyone(jnp.concatenate([pooled, chip], 0))
        unit_pool = got[:, :blocks].reshape(pool_rows, width)
        vectors = got[:, blocks, :span].reshape(size, 4, span // 4)
        vectors = jnp.transpose(vectors, (1, 0, 2)).reshape(4, width).astype(f32)
    else:
        unit_pool = lax.all_gather(pooled, "seq", axis=0, tiled=True)
        vectors = lax.all_gather(vectors, BOTH, axis=1, tiled=True).astype(f32)
    gain_one, bias_one, gain_two, bias_two = vectors
    unit_ext = jnp.concatenate([unit_pool.astype(f32), unit_halo, unit], 0)
    normed = (unit_ext * gain_one + bias_one).astype(bf16)
    mixed_own = dot_nn(normed, own_qkv).astype(bf16)
    mixed_other = dot_nn(normed, other_qkv).astype(bf16)

    block_ids = at * blocks + jnp.arange(blocks, dtype=jnp.int32)
    flat = chosen.reshape(blocks * TOPK)
    far_bias = jnp.where(chosen < block_ids[:, None], 0.0, NEG).reshape(blocks * TOPK, 1)
    info = jnp.stack([(at == 0).astype(jnp.int32), side])
    attended, probs, picks = attend(
        mixed_own, mixed_other, flat[:, None], far_bias, info, blocks, pool_rows
    )

    after = tokens + dot_nn(attended, mat_out)
    unit_two, scale_two = standardize(after)
    normed_two = (unit_two * gain_two + bias_two).astype(bf16)
    hidden = dot_nn(normed_two, mat_up)
    active, gelu_back = jax.vjp(partial(jax.nn.gelu, approximate=True), hidden)
    active = active.astype(bf16)
    output = (after + dot_nn(active, mat_down)).astype(bf16)

    upstream = cotangent[0]
    dhidden = gelu_back(dot_nt(upstream, mat_down))[0].astype(bf16)
    grad_down = dot_tn(active, upstream).astype(bf16)
    grad_up = in_order(side, *jnp.split(dot_tn(normed_two, dhidden).astype(bf16), 2, axis=1))
    dnormed_two = dot_nt(dhidden, mat_up)
    grad_gain_two = jnp.sum(dnormed_two * unit_two, axis=0)
    grad_bias_two = jnp.sum(dnormed_two, axis=0)
    dafter = upstream.astype(f32) + standardize_back(unit_two, scale_two, dnormed_two * gain_two)
    dafter_low = dafter.astype(bf16)
    grad_out = in_order(side, *jnp.split(dot_tn(attended, dafter_low).astype(bf16), 2, axis=1))
    dattended = dot_nt(dafter_low, mat_out).astype(bf16)
    own_down = lax.psum_scatter(grad_down, BOTH, scatter_dimension=0, tiled=True).astype(f32)
    sum_up = scatter_halves(grad_up[0], grad_up[1], 768)

    dmixed_own, dmixed_other = attend_back(
        mixed_own, mixed_other, flat[None, :], info, picks, probs, dattended, blocks, pool_rows
    )
    grad_other = dot_tn(normed, dmixed_other).astype(bf16)
    grad_own = dot_tn(normed, dmixed_own).astype(bf16)
    dnormed = dot_nt(dmixed_own, own_qkv) + dot_nt(dmixed_other, other_qkv)
    grad_gain_one = jnp.sum(dnormed * unit_ext, axis=0)
    grad_bias_one = jnp.sum(dnormed, axis=0)
    vector_grads = jnp.stack([grad_gain_one, grad_bias_one, grad_gain_two, grad_bias_two])
    from_next = shift_seq(dnormed[pool_rows : pool_rows + BLOCK].astype(bf16), -1).astype(f32)
    own_qo = jnp.concatenate([grad_own, grad_out[0]], 1)
    other_qo = jnp.concatenate([grad_other, grad_out[1]], 1)
    sum_qo = scatter_halves(own_qo, other_qo, 768)
    dpool = dnormed[:pool_rows].astype(bf16)
    if paired():
        spread = jnp.transpose(vector_grads.reshape(4, size, -1), (1, 0, 2)).reshape(size, 1, -1)
        spread = jnp.pad(spread.astype(bf16), ((0, 0), (0, 7), (0, width - spread.shape[2])))
        send = jnp.concatenate([dpool.reshape(size, blocks, width), spread], 1)
        got = jnp.sum(lax.all_to_all(send, "seq", 0, 0).astype(f32), axis=0)
        from_pool = got[:blocks]
        chip = got[blocks, :span].reshape(4, 2, -1)
        vector_sums = pick(chip, side, 1) + swap(pick(chip, 1 - side, 1), "batch", 1)
    else:
        from_pool = lax.psum_scatter(dpool, "seq", scatter_dimension=0, tiled=True).astype(f32)
        vector_sums = lax.psum_scatter(vector_grads, BOTH, scatter_dimension=1, tiled=True)
    dtoken = (
        dnormed[pool_rows + BLOCK :]
        + jnp.repeat(from_pool * (1.0 / BLOCK), BLOCK, axis=0)
        + jnp.pad(from_next, ((count - BLOCK, 0), (0, 0)))
    )
    input_grad = dafter + standardize_back(unit, unit_scale, dtoken * gain_one)

    split = 3 * width // 2
    return (
        output[None],
        input_grad[None],
        vector_sums[0],
        vector_sums[1],
        whole_of(sum_qo[:, :, :split], 3),
        whole_of(sum_qo[:, :, split:], 1),
        vector_sums[2],
        vector_sums[3],
        whole_of(sum_up, 1),
        own_down,
    )


def solution(mesh):
    tokens = P("batch", "seq", None)
    vector = P(BOTH)
    matrix = P(BOTH, None)
    return jax.shard_map(
        local,
        mesh=mesh,
        in_specs=(
            tokens,
            tokens,
            tokens,
            vector,
            vector,
            matrix,
            matrix,
            vector,
            vector,
            matrix,
            matrix,
        ),
        out_specs=(
            tokens,
            tokens,
            vector,
            vector,
            matrix,
            matrix,
            vector,
            vector,
            matrix,
            matrix,
        ),
        check_vma=False,
    )
```

```python
from functools import partial

import jax
import jax.numpy as jnp
from jax import lax
from jax.experimental import pallas as pl
from jax.experimental.pallas import tpu as pltpu
from jax.sharding import PartitionSpec as P

HEADS = 12
HEAD = 64
BLOCK = 64
TOPK = 16
QUAD = 4 * HEAD
FOLD = BLOCK + TOPK
NEG = -1e30


def dot_nn(a, b):
    return lax.dot_general(a, b, (((1,), (0,)), ((), ())), preferred_element_type=jnp.float32)


def dot_nt(a, b):
    return lax.dot_general(a, b, (((1,), (1,)), ((), ())), preferred_element_type=jnp.float32)


def dot_tn(a, b):
    return lax.dot_general(a, b, (((0,), (0,)), ((), ())), preferred_element_type=jnp.float32)


def spread_heads(rows):
    lane = lax.broadcasted_iota(jnp.int32, rows.shape, 1) // HEAD
    zero = jnp.zeros_like(rows)
    return jnp.concatenate([jnp.where(lane == h, rows, zero) for h in range(4)], 0)


def gather_heads(full):
    lane = lax.broadcasted_iota(jnp.int32, (BLOCK, QUAD), 1) // HEAD
    out = full[:BLOCK]
    for h in range(1, 4):
        out = jnp.where(lane == h, full[h * BLOCK : (h + 1) * BLOCK], out)
    return out


def prev_side():
    k = lax.broadcasted_iota(jnp.int32, (BLOCK, QUAD), 0)
    q = lax.broadcasted_iota(jnp.int32, (BLOCK, QUAD), 1) % BLOCK
    return k > q


def unfold(near, far, prev):
    zero = jnp.zeros_like(near)
    both = [jnp.where(prev, near, zero), jnp.where(prev, zero, near), far]
    return jnp.concatenate(both, 0).astype(jnp.bfloat16)


HALF = HEADS // 2 * HEAD


def load_quad(own_ref, other_ref, part, g):
    at = part * HALF
    if g == 0:
        return own_ref[:, at : at + QUAD]
    if g == 1:
        return jnp.concatenate(
            [own_ref[:, at + QUAD : at + HALF], other_ref[:, at : at + HALF - QUAD]], 1
        )
    return other_ref[:, at + HALF - QUAD : at + HALF]


def join_quads(quads):
    own = jnp.concatenate([quads[0], quads[1][:, : HALF - QUAD]], 1)
    other = jnp.concatenate([quads[1][:, HALF - QUAD :], quads[2]], 1)
    return own, other


def attend_kernel(
    info_ref,
    sel_ref,
    bias_ref,
    pool_own,
    prev_own,
    cur_own,
    pool_other,
    prev_other,
    cur_other,
    att_ref,
    probs_ref,
    picks_ref,
):
    c = pl.program_id(0)
    core = info_ref[1]

    @pl.when(c == 0)
    def _():
        pool_rows = pool_own.shape[0]
        ids = lax.broadcasted_iota(jnp.int32, (sel_ref.shape[0], pool_rows), 1)
        one_hot = (ids == sel_ref[...]).astype(jnp.float32).astype(jnp.bfloat16)
        picks_ref[0] = dot_nn(one_hot, pool_own[:, HALF:]).astype(jnp.bfloat16)
        picks_ref[1] = dot_nn(one_hot, pool_other[:, HALF:]).astype(jnp.bfloat16)

    prev = prev_side()
    edge = jnp.where((c == 0) & (info_ref[0] == 1), NEG, 0.0)
    rows = pl.ds(pl.multiple_of(c * TOPK, TOPK), TOPK)
    pick_own, pick_other = picks_ref.at[0, rows], picks_ref.at[1, rows]
    outs = []
    for g in range(HEADS // 4):
        keys, values = [
            jnp.concatenate(
                [
                    load_quad(prev_own, prev_other, part, g),
                    load_quad(cur_own, cur_other, part, g),
                    load_quad(pick_own, pick_other, part - 1, g),
                ],
                0,
            )
            for part in (1, 2)
        ]
        wide_q = spread_heads(load_quad(cur_own, cur_other, 0, g))
        scores = dot_nt(keys, wide_q) * HEAD ** (-0.5)
        near = jnp.where(prev, scores[:BLOCK] + edge, scores[BLOCK : 2 * BLOCK])
        far = scores[2 * BLOCK :] + bias_ref[...]
        folded = jnp.concatenate([near, far], 0)
        top = jnp.max(folded, axis=0, keepdims=True)
        weights = jnp.exp(folded - top)
        probs = weights * (1.0 / jnp.sum(weights, axis=0, keepdims=True))
        probs_ref[0, g] = probs
        full = unfold(probs[:BLOCK], probs[BLOCK:], prev)
        outs.append(gather_heads(dot_tn(full, values)).astype(jnp.bfloat16))
    own, other = join_quads(outs)
    att_ref[:, pl.ds(pl.multiple_of(core * HALF, 128), HALF)] = own
    att_ref[:, pl.ds(pl.multiple_of((1 - core) * HALF, 128), HALF)] = other


def attend(mixed_own, mixed_other, sel_col, bias_col, info, blocks, pool_rows):
    width = HEADS * HEAD
    halo = blocks + pool_rows // BLOCK
    mixed_specs = [
        pl.BlockSpec((pool_rows, 3 * HALF), lambda c, f: (blocks * BLOCK // pool_rows, 0)),
        pl.BlockSpec((BLOCK, 3 * HALF), lambda c, f: (jnp.where(c == 0, halo, c - 1), 0)),
        pl.BlockSpec((BLOCK, 3 * HALF), lambda c, f: (c, 0)),
    ]
    return pl.pallas_call(
        attend_kernel,
        grid_spec=pltpu.PrefetchScalarGridSpec(
            num_scalar_prefetch=1,
            grid=(blocks,),
            in_specs=[
                pl.BlockSpec((blocks * TOPK, 1), lambda c, f: (0, 0)),
                pl.BlockSpec((TOPK, 1), lambda c, f: (c, 0)),
            ]
            + mixed_specs * 2,
            out_specs=[
                pl.BlockSpec((BLOCK, width), lambda c, f: (c, 0)),
                pl.BlockSpec((1, HEADS // 4, FOLD, QUAD), lambda c, f: (c, 0, 0, 0)),
                pl.BlockSpec((2, blocks * TOPK, 2 * HALF), lambda c, f: (0, 0, 0)),
            ],
        ),
        out_shape=[
            jax.ShapeDtypeStruct((blocks * BLOCK, width), jnp.bfloat16),
            jax.ShapeDtypeStruct((blocks, HEADS // 4, FOLD, QUAD), jnp.float32),
            jax.ShapeDtypeStruct((2, blocks * TOPK, 2 * HALF), jnp.bfloat16),
        ],
        compiler_params=pltpu.CompilerParams(vmem_limit_bytes=32 * 1024 * 1024),
        cost_estimate=pl.CostEstimate(
            flops=12_000_000_000, bytes_accessed=12_000_000, transcendentals=1_000_000
        ),
        name="attend",
    )(info, sel_col, bias_col, *[mixed_own] * 3, *[mixed_other] * 3)


def attend_back_kernel(
    blocks,
    info_ref,
    sel_ref,
    prev_own,
    cur_own,
    prev_other,
    cur_other,
    picks_ref,
    probs_ref,
    datt_ref,
    out_own,
    out_other,
    carry,
    dpicks,
):
    i = pl.program_id(0)
    core = info_ref[1]

    @pl.when(i == 0)
    def _():
        carry[...] = jnp.zeros_like(carry)

    @pl.when(i < blocks)
    def _():
        prev = prev_side()
        rows = pl.ds(pl.multiple_of(i * TOPK, TOPK), TOPK)
        datt_own = datt_ref.at[:, pl.ds(pl.multiple_of(core * HALF, 128), HALF)]
        datt_other = datt_ref.at[:, pl.ds(pl.multiple_of((1 - core) * HALF, 128), HALF)]
        grads = []
        for g in range(HEADS // 4):
            keys, values = [
                jnp.concatenate(
                    [
                        load_quad(prev_own, prev_other, part, g),
                        load_quad(cur_own, cur_other, part, g),
                        load_quad(picks_ref.at[0], picks_ref.at[1], part - 1, g),
                    ],
                    0,
                )
                for part in (1, 2)
            ]
            wide_q = spread_heads(load_quad(cur_own, cur_other, 0, g))
            wide_d = spread_heads(load_quad(datt_own, datt_other, 0, g))
            probs = probs_ref[0, g]
            dprobs = dot_nt(values, wide_d)
            near = jnp.where(prev, dprobs[:BLOCK], dprobs[BLOCK : 2 * BLOCK])
            folded = jnp.concatenate([near, dprobs[2 * BLOCK :]], 0)
            inner = jnp.sum(probs * folded, axis=0, keepdims=True)
            dscores = probs * (folded - inner) * HEAD ** (-0.5)
            full_p = unfold(probs[:BLOCK], probs[BLOCK:], prev)
            full_d = unfold(dscores[:BLOCK], dscores[BLOCK:], prev)
            dvals = dot_nn(full_p, wide_d)
            dkeys = dot_nn(full_d, wide_q)
            dq = gather_heads(dot_tn(full_d, keys))
            grads.append((dq, dkeys, dvals))
        for part in range(3):
            lanes = slice(part * HALF, (part + 1) * HALF)
            halves = join_quads([grad[part] for grad in grads])
            for side, out_ref in enumerate((out_own, out_other)):
                half = halves[side]
                if part == 0:
                    out_ref[:, lanes] = carry[side, :, lanes].astype(jnp.bfloat16)
                    carry[side, :, lanes] = half
                else:
                    out_ref[:, lanes] = (carry[side, :, lanes] + half[:BLOCK]).astype(jnp.bfloat16)
                    carry[side, :, lanes] = half[BLOCK : 2 * BLOCK]
                    picked = slice((part - 1) * HALF, part * HALF)
                    dpicks[side, rows, picked] = half[2 * BLOCK :].astype(jnp.bfloat16)

    @pl.when(i == blocks)
    def _():
        out_own[...] = carry[0].astype(jnp.bfloat16)
        out_other[...] = carry[1].astype(jnp.bfloat16)

    @pl.when(i > blocks)
    def _():
        ids = lax.broadcasted_iota(jnp.int32, (BLOCK, blocks * TOPK), 0) + (i - blocks - 1) * BLOCK
        one_hot = (ids == sel_ref[...]).astype(jnp.float32).astype(jnp.bfloat16)
        for side, out_ref in enumerate((out_own, out_other)):
            out_ref[:, :HALF] = jnp.zeros((BLOCK, HALF), jnp.bfloat16)
            out_ref[:, HALF:] = dot_nn(one_hot, dpicks[side]).astype(jnp.bfloat16)


def attend_back(mixed_own, mixed_other, sel_row, info, picks, probs, datt, blocks, pool_rows):
    width = HEADS * HEAD
    base = pool_rows // BLOCK

    def query_block(i):
        return jnp.minimum(i, blocks - 1)

    def before_block(i, f):
        return (jnp.where(i == 0, blocks + base, query_block(i) - 1), 0)

    def out_block(i, f):
        row = jnp.where(i == 0, blocks + base, i - 1)
        return (jnp.where(i > blocks, i - 1, row), 0)

    mixed_specs = [
        pl.BlockSpec((BLOCK, 3 * HALF), before_block),
        pl.BlockSpec((BLOCK, 3 * HALF), lambda i, f: (query_block(i), 0)),
    ]
    rows = pool_rows + (blocks + 1) * BLOCK
    return pl.pallas_call(
        partial(attend_back_kernel, blocks),
        grid_spec=pltpu.PrefetchScalarGridSpec(
            num_scalar_prefetch=1,
            grid=(blocks + 1 + base,),
            in_specs=[pl.BlockSpec((1, blocks * TOPK), lambda i, f: (0, 0))]
            + mixed_specs * 2
            + [
                pl.BlockSpec((2, TOPK, 2 * HALF), lambda i, f: (0, query_block(i), 0)),
                pl.BlockSpec(
                    (1, HEADS // 4, FOLD, QUAD), lambda i, f: (query_block(i), 0, 0, 0)
                ),
                pl.BlockSpec((BLOCK, width), lambda i, f: (query_block(i), 0)),
            ],
            out_specs=[pl.BlockSpec((BLOCK, 3 * HALF), out_block)] * 2,
            scratch_shapes=[
                pltpu.VMEM((2, BLOCK, 3 * HALF), jnp.float32),
                pltpu.VMEM((2, blocks * TOPK, 2 * HALF), jnp.bfloat16),
            ],
        ),
        out_shape=[jax.ShapeDtypeStruct((rows, 3 * HALF), jnp.bfloat16)] * 2,
        compiler_params=pltpu.CompilerParams(vmem_limit_bytes=32 * 1024 * 1024),
        cost_estimate=pl.CostEstimate(
            flops=20_000_000_000, bytes_accessed=18_000_000, transcendentals=0
        ),
        name="attend_back",
    )(info, sel_row, *[mixed_own] * 2, *[mixed_other] * 2, picks, probs, datt)


def standardize(values):
    center = values - jnp.mean(values, axis=-1, keepdims=True)
    spread = jnp.mean(center * center, axis=-1, keepdims=True)
    scale = lax.rsqrt(spread + 1e-05)
    return center * scale, scale


def standardize_back(unit, scale, dunit):
    return scale * (
        dunit
        - jnp.mean(dunit, axis=-1, keepdims=True)
        - unit * jnp.mean(dunit * unit, axis=-1, keepdims=True)
    )


ROWS = 256
CHUNK = 512
MIB = 1024 * 1024


def params(mib):
    return pltpu.CompilerParams(vmem_limit_bytes=mib * MIB)


def shape(rows, columns, dtype=jnp.bfloat16):
    return jax.ShapeDtypeStruct((rows, columns), dtype)


def cost(flops, moved):
    return pl.CostEstimate(flops=flops, bytes_accessed=moved, transcendentals=0)


def lanes_at(index, size):
    return pl.ds(pl.multiple_of(index * size, 128), size)


def pool_kernel(tokens_ref, out_ref):
    for b in range(out_ref.shape[0]):
        unit, _ = standardize(tokens_ref[b * BLOCK : (b + 1) * BLOCK].astype(jnp.float32))
        out_ref[b : b + 1] = jnp.mean(unit, axis=0, keepdims=True)


def pool(tokens):
    rows, width = tokens.shape
    return pl.pallas_call(
        pool_kernel,
        out_shape=shape(rows // BLOCK, width, jnp.float32),
        compiler_params=params(16),
        cost_estimate=cost(2_000_000_000, 6_000_000),
        name="pool",
    )(tokens)


def project_kernel(
    tokens_ref, pool_ref, halo_ref, vec_ref, own_ref, other_ref, normed_ref, unit_ref, m_own, m_other
):
    j = pl.program_id(0)

    @pl.when(j == 0)
    def _():
        gain, bias = vec_ref[0:1], vec_ref[1:2]
        start = 0
        for ref in (tokens_ref, pool_ref, halo_ref):
            for r in range(0, ref.shape[0], BLOCK):
                unit = ref[r : r + BLOCK].astype(jnp.float32)
                if ref is not pool_ref:
                    unit, _ = standardize(unit)
                rows = slice(start, start + BLOCK)
                unit_ref[rows] = unit.astype(jnp.bfloat16)
                normed_ref[rows] = (unit * gain + bias).astype(jnp.bfloat16)
                start += BLOCK

    @pl.when(j < 3)
    def _():
        m_own[...] = dot_nn(normed_ref[...], own_ref[...]).astype(jnp.bfloat16)

    @pl.when(j >= 3)
    def _():
        m_other[...] = dot_nn(normed_ref[...], other_ref[...]).astype(jnp.bfloat16)


def project(tokens, unit_pool, halo, vectors, own, other):
    width = tokens.shape[1]
    total = tokens.shape[0] + unit_pool.shape[0] + halo.shape[0]

    def first(j):
        return (0, jnp.minimum(j, 2))

    def second(j):
        return (0, jnp.maximum(j - 3, 0))

    whole = lambda j: (0, 0)
    return pl.pallas_call(
        project_kernel,
        grid=(6,),
        in_specs=[
            pl.BlockSpec(tokens.shape, whole),
            pl.BlockSpec(unit_pool.shape, whole),
            pl.BlockSpec(halo.shape, whole),
            pl.BlockSpec(vectors.shape, whole),
            pl.BlockSpec((width, HALF), first),
            pl.BlockSpec((width, HALF), second),
        ],
        out_specs=[
            pl.BlockSpec((total, width), whole),
            pl.BlockSpec((total, width), whole),
            pl.BlockSpec((total, HALF), first),
            pl.BlockSpec((total, HALF), second),
        ],
        out_shape=[
            shape(total, width),
            shape(total, width),
            shape(total, 3 * HALF),
            shape(total, 3 * HALF),
        ],
        compiler_params=params(40),
        cost_estimate=cost(6_000_000_000, 12_000_000),
        name="project",
    )(tokens, unit_pool, halo, vectors, own, other)


def after_kernel(info_ref, att_ref, own_ref, other_ref, tokens_ref, vec_ref, after_ref, normed_ref):
    core = info_ref[1]
    half = own_ref.shape[1]
    after_ref[:, lanes_at(core, half)] = dot_nn(att_ref[...], own_ref[...])
    after_ref[:, lanes_at(1 - core, half)] = dot_nn(att_ref[...], other_ref[...])
    after = tokens_ref[...].astype(jnp.float32) + after_ref[...]
    after_ref[...] = after
    unit, _ = standardize(after)
    normed_ref[...] = (unit * vec_ref[2:3] + vec_ref[3:4]).astype(jnp.bfloat16)


def out_columns(own):
    width = own.shape[0]
    half = width // 2
    return pl.BlockSpec((width, half), lambda i, f: (0, own.shape[1] // half - 1))


def after_attention(attended, own, other, tokens, vectors, info):
    count, width = tokens.shape
    row = pl.BlockSpec((ROWS, width), lambda i, f: (i, 0))
    return pl.pallas_call(
        after_kernel,
        grid_spec=pltpu.PrefetchScalarGridSpec(
            num_scalar_prefetch=1,
            grid=(count // ROWS,),
            in_specs=[
                row,
                out_columns(own),
                out_columns(other),
                row,
                pl.BlockSpec(vectors.shape, lambda i, f: (0, 0)),
            ],
            out_specs=[row, row],
        ),
        out_shape=[shape(count, width, jnp.float32), shape(count, width)],
        compiler_params=params(24),
        cost_estimate=cost(2_000_000_000, 10_000_000),
        name="after_attention",
    )(info, attended, own, other, tokens, vectors)


def up_kernel(
    info_ref, n2_ref, dy_ref, own_ref, other_ref, active_ref, slope_ref, gd_own, gd_other, grad_ref
):
    j = pl.program_id(0)
    core = info_ref[1]
    side = gd_own.shape[1]
    half = pl.num_programs(0) // 2
    weight = jnp.where(j < half, own_ref[...], other_ref[...])
    root = (2.0 / 3.141592653589793) ** 0.5
    for r in range(0, n2_ref.shape[0], ROWS):
        rows = slice(r, r + ROWS)
        u = dot_nn(n2_ref[rows], weight)
        square = u * u
        t = jnp.tanh(root * u * (1.0 + 0.044715 * square))
        upper = 0.5 * (1.0 + t)
        active_ref[rows] = (u * upper).astype(jnp.bfloat16)
        bend = 0.5 * u * (1.0 - t * t) * (root * (1.0 + 3.0 * 0.044715 * square))
        slope_ref[rows] = (upper + bend).astype(jnp.bfloat16)
    grad_ref[...] = dot_tn(active_ref[...], dy_ref[...]).astype(jnp.bfloat16)
    gd_own[...] = grad_ref[:, lanes_at(core, side)]
    gd_other[...] = grad_ref[:, lanes_at(1 - core, side)]


def ff_maps(hidden):
    steps = hidden // CHUNK
    half = steps // 2
    own = lambda j, f: (0, jnp.minimum(j, half - 1))
    other = lambda j, f: (0, jnp.maximum(j - half, 0))
    place = lambda j, f: lax.rem(f[1] * half + j, steps)
    return steps, own, other, place


def up_project(normed_two, upstream, own, other, info, hidden):
    count, width = normed_two.shape
    steps, first, second, place = ff_maps(hidden)
    whole = pl.BlockSpec((count, width), lambda j, f: (0, 0))
    columns = pl.BlockSpec((count, CHUNK), lambda j, f: (0, place(j, f)))
    rows = pl.BlockSpec((CHUNK, width // 2), lambda j, f: (place(j, f), 0))
    return pl.pallas_call(
        up_kernel,
        grid_spec=pltpu.PrefetchScalarGridSpec(
            num_scalar_prefetch=1,
            grid=(steps,),
            in_specs=[
                whole,
                whole,
                pl.BlockSpec((width, CHUNK), first),
                pl.BlockSpec((width, CHUNK), second),
            ],
            out_specs=[
                columns,
                columns,
                rows,
                rows,
            ],
            scratch_shapes=[pltpu.VMEM((CHUNK, width), jnp.bfloat16)],
        ),
        out_shape=[
            shape(count, hidden),
            shape(count, hidden),
            shape(hidden, width // 2),
            shape(hidden, width // 2),
        ],
        compiler_params=params(40),
        cost_estimate=cost(14_000_000_000, 25_000_000),
        name="up_project",
    )(info, normed_two, upstream, own, other)


def down_kernel(
    info_ref,
    n2_ref,
    dy_ref,
    slope_ref,
    down_ref,
    own_ref,
    other_ref,
    dn2_ref,
    g_own,
    g_other,
    dh_ref,
):
    j = pl.program_id(0)
    half = pl.num_programs(0) // 2
    weight = jnp.where(j < half, own_ref[...], other_ref[...])

    @pl.when(j == 0)
    def _():
        dn2_ref[...] = jnp.zeros_like(dn2_ref)

    for r in range(0, n2_ref.shape[0], ROWS):
        rows = slice(r, r + ROWS)
        dactive = dot_nt(dy_ref[rows], down_ref[...])
        dh = (dactive * slope_ref[rows].astype(jnp.float32)).astype(jnp.bfloat16)
        dh_ref[rows] = dh
        dn2_ref[rows] += dot_nt(dh, weight)
    grad = dot_tn(n2_ref[...], dh_ref[...]).astype(jnp.bfloat16)

    @pl.when(j < half)
    def _():
        g_own[...] = grad

    @pl.when(j >= half)
    def _():
        g_other[...] = grad


def down_back(normed_two, upstream, slope, mat_down, own, other, info, hidden):
    count, width = normed_two.shape
    steps, first, second, place = ff_maps(hidden)
    whole = pl.BlockSpec((count, width), lambda j, f: (0, 0))
    return pl.pallas_call(
        down_kernel,
        grid_spec=pltpu.PrefetchScalarGridSpec(
            num_scalar_prefetch=1,
            grid=(steps,),
            in_specs=[
                whole,
                whole,
                pl.BlockSpec((count, CHUNK), lambda j, f: (0, place(j, f))),
                pl.BlockSpec((CHUNK, width), lambda j, f: (place(j, f), 0)),
                pl.BlockSpec((width, CHUNK), first),
                pl.BlockSpec((width, CHUNK), second),
            ],
            out_specs=[
                whole,
                pl.BlockSpec((width, CHUNK), first),
                pl.BlockSpec((width, CHUNK), second),
            ],
            scratch_shapes=[pltpu.VMEM((count, CHUNK), jnp.bfloat16)],
        ),
        out_shape=[
            shape(count, width, jnp.float32),
            shape(width, hidden // 2),
            shape(width, hidden // 2),
        ],
        compiler_params=params(40),
        cost_estimate=cost(20_000_000_000, 25_000_000),
        name="down_back",
    )(info, normed_two, upstream, slope, mat_down, own, other)


def after_back_kernel(
    info_ref,
    after_ref,
    dn2_ref,
    dy_ref,
    att_ref,
    vec_ref,
    own_ref,
    other_ref,
    dafter_ref,
    datt_ref,
    go_own,
    go_other,
    sums_ref,
    acc,
    low,
):
    i = pl.program_id(0)
    core = info_ref[1]
    half = own_ref.shape[1]

    @pl.when(i == 0)
    def _():
        sums_ref[...] = jnp.zeros_like(sums_ref)
        acc[...] = jnp.zeros_like(acc)

    unit, scale = standardize(after_ref[...])
    dn2 = dn2_ref[...]
    sums_ref[0:1] += jnp.sum(dn2 * unit, axis=0, keepdims=True)
    sums_ref[1:2] += jnp.sum(dn2, axis=0, keepdims=True)
    dafter = dy_ref[...].astype(jnp.float32) + standardize_back(unit, scale, dn2 * vec_ref[2:3])
    dafter_ref[...] = dafter
    low[...] = dafter.astype(jnp.bfloat16)
    datt = dot_nt(low[:, lanes_at(core, half)], own_ref[...])
    datt += dot_nt(low[:, lanes_at(1 - core, half)], other_ref[...])
    datt_ref[...] = datt.astype(jnp.bfloat16)
    acc[...] += dot_tn(att_ref[...], low[...])

    @pl.when(i == pl.num_programs(0) - 1)
    def _():
        go_own[...] = acc[:, lanes_at(core, half)].astype(jnp.bfloat16)
        go_other[...] = acc[:, lanes_at(1 - core, half)].astype(jnp.bfloat16)


def after_back(after, dn2, upstream, attended, vectors, own, other, info):
    count, width = after.shape
    row = pl.BlockSpec((ROWS, width), lambda i, f: (i, 0))
    return pl.pallas_call(
        after_back_kernel,
        grid_spec=pltpu.PrefetchScalarGridSpec(
            num_scalar_prefetch=1,
            grid=(count // ROWS,),
            in_specs=[
                row,
                row,
                row,
                row,
                pl.BlockSpec(vectors.shape, lambda i, f: (0, 0)),
                out_columns(own),
                out_columns(other),
            ],
            out_specs=[
                row,
                row,
                pl.BlockSpec((width, width // 2), lambda i, f: (0, 0)),
                pl.BlockSpec((width, width // 2), lambda i, f: (0, 0)),
                pl.BlockSpec((8, width), lambda i, f: (0, 0)),
            ],
            scratch_shapes=[
                pltpu.VMEM((width, width), jnp.float32),
                pltpu.VMEM((ROWS, width), jnp.bfloat16),
            ],
        ),
        out_shape=[
            shape(count, width, jnp.float32),
            shape(count, width),
            shape(width, width // 2),
            shape(width, width // 2),
            shape(8, width, jnp.float32),
        ],
        compiler_params=params(32),
        cost_estimate=cost(4_000_000_000, 16_000_000),
        name="after_back",
    )(info, after, dn2, upstream, attended, vectors, own, other)


def project_back_kernel(dm_own, dm_other, own_ref, other_ref, unit_ref, dn_ref, sums_ref):
    @pl.when(pl.program_id(0) == 0)
    def _():
        sums_ref[...] = jnp.zeros_like(sums_ref)

    dn = dot_nt(dm_own[...], own_ref[...]) + dot_nt(dm_other[...], other_ref[...])
    dn_ref[...] = dn
    sums_ref[0:1] += jnp.sum(dn * unit_ref[...].astype(jnp.float32), axis=0, keepdims=True)
    sums_ref[1:2] += jnp.sum(dn, axis=0, keepdims=True)


def project_back(dm_own, dm_other, own, other, unit):
    total, width = unit.shape
    groups = total // BLOCK
    rows = BLOCK * max(n for n in range(1, 8) if groups % n == 0)
    row = lambda i: (i, 0)
    whole = pl.BlockSpec((width, 3 * HALF), lambda i: (0, 0))
    return pl.pallas_call(
        project_back_kernel,
        grid=(total // rows,),
        in_specs=[
            pl.BlockSpec((rows, 3 * HALF), row),
            pl.BlockSpec((rows, 3 * HALF), row),
            whole,
            whole,
            pl.BlockSpec((rows, width), row),
        ],
        out_specs=[pl.BlockSpec((rows, width), row), pl.BlockSpec((8, width), lambda i: (0, 0))],
        out_shape=[shape(total, width, jnp.float32), shape(8, width, jnp.float32)],
        compiler_params=params(32),
        cost_estimate=cost(6_000_000_000, 16_000_000),
        name="project_back",
    )(dm_own, dm_other, own, other, unit)


def input_kernel(tokens_ref, dn_ref, dafter_ref, pool_ref, next_ref, vec_ref, out_ref):
    i = pl.program_id(0)
    gain = vec_ref[0:1]
    per = tokens_ref.shape[0] // BLOCK
    last = (i == pl.num_programs(0) - 1).astype(jnp.float32)
    for b in range(per):
        rows = slice(b * BLOCK, (b + 1) * BLOCK)
        unit, scale = standardize(tokens_ref[rows].astype(jnp.float32))
        dn = dn_ref[rows] + pool_ref[pl.ds(i * per + b, 1)] * (1.0 / BLOCK)
        if b == per - 1:
            dn += next_ref[...].astype(jnp.float32) * last
        out_ref[rows] = dafter_ref[rows] + standardize_back(unit, scale, dn * gain)


def input_back(tokens, dnormed, dafter, from_pool, from_next, vectors):
    count, width = tokens.shape
    row = pl.BlockSpec((ROWS, width), lambda i: (i, 0))
    whole = lambda i: (0, 0)
    return pl.pallas_call(
        input_kernel,
        grid=(count // ROWS,),
        in_specs=[
            row,
            row,
            row,
            pl.BlockSpec(from_pool.shape, whole),
            pl.BlockSpec(from_next.shape, whole),
            pl.BlockSpec(vectors.shape, whole),
        ],
        out_specs=row,
        out_shape=shape(count, width, jnp.float32),
        compiler_params=params(24),
        cost_estimate=cost(3_000_000_000, 12_000_000),
        name="input_back",
    )(tokens, dnormed, dafter, from_pool, from_next, vectors)


def output_kernel(after_ref, active_ref, down_ref, out_ref):
    value = after_ref[...] + dot_nn(active_ref[...], down_ref[...])
    out_ref[...] = value.astype(jnp.bfloat16)


def layer_output(after, active, mat_down):
    count, width = after.shape
    hidden = active.shape[1]
    row = lambda i: (i, 0)
    return pl.pallas_call(
        output_kernel,
        grid=(count // ROWS,),
        in_specs=[
            pl.BlockSpec((ROWS, width), row),
            pl.BlockSpec((ROWS, hidden), row),
            pl.BlockSpec((hidden, width), lambda i: (0, 0)),
        ],
        out_specs=pl.BlockSpec((ROWS, width), row),
        out_shape=shape(count, width),
        compiler_params=params(32),
        cost_estimate=cost(6_000_000_000, 16_000_000),
        name="layer_output",
    )(after, active, mat_down)


def shift_seq(value, distance):
    size = lax.axis_size("seq")
    route = [(i - distance, i) for i in range(size) if 0 <= i - distance < size]
    return lax.ppermute(value, "seq", route)


BOTH = ("seq", "batch")


def follows(value, *earlier):
    return lax.optimization_barrier((value, earlier))[0]


def flip_route(size, bit):
    return [(i, i ^ bit) for i in range(size)]


def ring_route(size, stride, steps):
    return [(i, (i + stride * steps) % size) for i in range(size)]


def swap(value, axis, bit):
    return lax.ppermute(value, axis, flip_route(lax.axis_size(axis), bit))


def in_order(bit, own, other):
    return jnp.stack([jnp.where(bit == 0, own, other), jnp.where(bit == 0, other, own)])


def pick(value, index, axis):
    return lax.dynamic_index_in_dim(value, index, axis, keepdims=False)


def add(a, b):
    return (a.astype(jnp.float32) + b.astype(jnp.float32)).astype(jnp.bfloat16)


def place():
    at = lax.axis_index("seq")
    return at // 4, at // 2 % 2, at % 2


def send_line(slab):
    size = lax.axis_size("seq")
    return [lax.ppermute(slab, "seq", ring_route(size, 4, k)) for k in range(1, size // 4)]


def join_line(slab, got):
    z = place()[0]
    stack = jnp.stack([slab] + got)
    layers = stack.shape[0]
    parts = [lax.dynamic_slice_in_dim(stack, (z - k) % layers, 1, 0) for k in range(layers)]
    return jnp.concatenate(parts, 0)


def send_near(line, cut):
    first, second = line[:, :, :cut], line[:, :, cut:]
    return first, second, swap(first, "seq", 1), swap(second, "seq", 2)


def join_near(first, second, first_got, second_got):
    _, y, x = place()
    return in_order(x, first, first_got), in_order(y, second, second_got)


def send_far(first, second):
    return swap(first, "seq", 2), swap(second, "seq", 1)


def join_far(first, second, first_got, second_got):
    _, y, x = place()
    first = jnp.transpose(in_order(y, first, first_got), (2, 0, 1, 3, 4))
    second = jnp.transpose(in_order(x, second, second_got), (2, 1, 0, 3, 4))
    rows = first.shape[3] * lax.axis_size("seq")
    return first.reshape(rows, -1), second.reshape(rows, -1)


def split_grid(full, cut, axis=4):
    grid = full.reshape(lax.axis_size("seq") // 4, 2, 2, -1, full.shape[1])
    return jnp.split(grid, [cut], axis)


def drop_near(first, second):
    _, y, x = place()
    return pick(first, 1 - x, 2), pick(second, 1 - y, 1)


def keep_near(first, second, first_got, second_got):
    _, y, x = place()
    return add(pick(first, x, 2), first_got), add(pick(second, y, 1), second_got)


def drop_far(first, second):
    _, y, x = place()
    return pick(first, 1 - y, 1), pick(second, 1 - x, 1)


def keep_far(first, second, first_got, second_got, axis=2):
    _, y, x = place()
    parts = [add(pick(first, y, 1), first_got), add(pick(second, x, 1), second_got)]
    return jnp.concatenate(parts, axis)


def swap_near(dropped):
    return swap(dropped[0], "seq", 1), swap(dropped[1], "seq", 2)


def swap_far(dropped):
    return swap(dropped[0], "seq", 2), swap(dropped[1], "seq", 1)


def scatter_line(line):
    z = place()[0]
    size = lax.axis_size("seq")
    layers = size // 4
    got = [
        lax.ppermute(pick(line, (z + k) % layers, 0), "seq", ring_route(size, 4, k))
        for k in range(1, layers)
    ]
    return pick(line, z, 0), got


def sum_line(own, got):
    return sum((g.astype(jnp.float32) for g in got), own.astype(jnp.float32))


def paired():
    return lax.axis_size("batch") == 2 and lax.axis_size("seq") % 4 == 0


def side_index():
    return lax.axis_index("batch") % 2


def halves_of(matrix, groups):
    rows, columns = matrix.shape
    parts = matrix.reshape(rows, groups, 2, columns // (2 * groups))
    return jnp.transpose(parts, (2, 0, 1, 3)).reshape(2, rows, columns // 2)


def whole_of(halves, groups):
    _, rows, columns = halves.shape
    parts = halves.reshape(2, rows, groups, columns // groups)
    return jnp.transpose(parts, (1, 2, 0, 3)).reshape(rows, 2 * columns)


def rows_of_side(total):
    side = side_index()
    total = total.reshape(2, -1, total.shape[1])
    got = swap(pick(total, 1 - side, 0), "batch", 1)
    return in_order(side, pick(total, side, 0), got)


def local(
    inputs, selection, cotangent, ln1_gain, ln1_bias, w_qkv, w_out, ln2_gain, ln2_bias, w_up, w_down
):
    bf16, f32 = jnp.bfloat16, jnp.float32
    tokens = inputs[0]
    chosen = selection[0]
    upstream = cotangent[0]
    count, width = tokens.shape
    hidden = w_up.shape[1]
    blocks = count // BLOCK
    size = lax.axis_size("seq")
    pool_rows = blocks * size
    at = lax.axis_index("seq")
    side = side_index()
    fast = paired()

    half_qkv = halves_of(w_qkv, 3)
    half_uo = jnp.concatenate([halves_of(w_up, 1), halves_of(w_out, 1)], 2)
    vectors = jnp.stack([ln1_gain, ln1_bias, ln2_gain, ln2_bias])
    if fast:
        columns = jnp.pad(vectors.T, ((0, 0), (0, 124)))
        columns = jnp.broadcast_to(columns, (2,) + columns.shape)
        bundle = jnp.concatenate([columns, half_qkv, half_uo], 2)
        got = swap(pick(bundle, 1 - side, 0), "batch", 1)
        slab = in_order(side, pick(bundle, side, 0), got).reshape(-1, bundle.shape[2])
        third = width // 3
        per = slab.shape[0] // 3
        pooled = pool(tokens).astype(bf16).reshape(per, 3, third)
        pooled = jnp.transpose(pooled, (1, 0, 2)).reshape(-1, third)
        front = third + 128
        edge = 128 + half_qkv.shape[2]
        slab_q = jnp.concatenate([pooled, slab[:, :edge]], 1)
        slab_u = slab[:, edge:]
        line_got = send_line(slab_q)
        halo = shift_seq(follows(tokens[-BLOCK:], slab_q), 1)
        line_got_u = send_line(follows(slab_u, halo))
        line_q = join_line(slab_q, line_got)
        near = send_near(line_q, 768)
        wide_q = join_near(*near)
        far = send_far(*wide_q)
        line_u = join_line(slab_u, follows(line_got_u, wide_q))
        near_u = send_near(line_u, 1024)
        first, second = join_far(*wide_q, *far)
        own_qkv = jnp.concatenate([first[:, front:], second], 1)
        other_qkv = swap(own_qkv, "batch", 1)
        unit_pool = jnp.transpose(first[:, :third].reshape(size, 3, per, third), (0, 2, 1, 3))
        unit_pool = unit_pool.reshape(pool_rows, width)
        vectors = first[:, third : third + 4].T.astype(f32)
        wide_u = join_near(*follows(near_u, own_qkv))
        far_u = send_far(*wide_u)
        other_qkv = follows(other_qkv, wide_u)
    else:
        gathered = lax.all_gather(half_qkv, BOTH, axis=1, tiled=True)
        own_qkv, other_qkv = pick(gathered, side, 0), pick(gathered, 1 - side, 0)
        gathered = lax.all_gather(half_uo, BOTH, axis=1, tiled=True)
        own_uo, other_uo = pick(gathered, side, 0), pick(gathered, 1 - side, 0)
        halo = shift_seq(tokens[-BLOCK:], 1)
        unit_pool = lax.all_gather(pool(tokens).astype(bf16), "seq", axis=0, tiled=True)
        vectors = lax.all_gather(vectors, BOTH, axis=1, tiled=True).astype(f32)
    mat_down = lax.all_gather(w_down, BOTH, axis=0, tiled=True)
    vectors = jnp.pad(vectors, ((0, 4), (0, 0)))

    normed, unit, mixed_own, mixed_other = project(
        tokens, unit_pool, halo, vectors, own_qkv, other_qkv
    )
    if fast:
        own_uo = jnp.concatenate(join_far(*wide_u, *follows(far_u, mixed_own)), 1)
        other_uo = swap(own_uo, "batch", 1)
        mixed_own = follows(mixed_own, own_uo)

    block_ids = at * blocks + jnp.arange(blocks, dtype=jnp.int32)
    flat = chosen.reshape(blocks * TOPK)
    far_bias = jnp.where(chosen < block_ids[:, None], 0.0, NEG).reshape(blocks * TOPK, 1)
    info = jnp.stack([(at == 0).astype(jnp.int32), side])
    attended, probs, picks = attend(
        mixed_own, mixed_other, flat[:, None], far_bias, info, blocks, pool_rows
    )
    after, normed_two = after_attention(attended, own_uo, other_uo, tokens, vectors, info)
    active, slope, down_own, down_other = up_project(
        normed_two, upstream, own_uo, other_uo, info, hidden
    )
    if fast:
        down_got = swap(down_other, "batch", 1)
        slope = follows(slope, down_other)
    dn2, up_own, up_other = down_back(
        normed_two, upstream, slope, mat_down, own_uo, other_uo, info, hidden
    )
    if fast:
        up_got = swap(up_other, "batch", 1)
        grid_d = split_grid(add(down_own, follows(down_got, dn2)), hidden // size // 2, 3)
        drop_d = drop_near(*grid_d)
        near_d = swap_near(drop_d)
        dn2 = follows(dn2, drop_d)
    dafter, dattended, out_own, out_other, sums_two = after_back(
        after, dn2, upstream, attended, vectors, own_uo, other_uo, info
    )
    if fast:
        out_got = swap(out_other, "batch", 1)
        kept_d = keep_near(*grid_d, *follows(near_d, dattended))
        drop_d = drop_far(*kept_d)
        far_d = swap_far(drop_d)
        up_sum = add(up_own, follows(up_got, dattended))
        out_sum = add(out_own, follows(out_got, drop_d))
        grid_u = split_grid(jnp.concatenate([up_sum, out_sum], 1), 1024)
        drop_u = drop_near(*grid_u)
        near_u = swap_near(drop_u)
        dattended = follows(dattended, drop_u)

    dmixed_own, dmixed_other = attend_back(
        mixed_own, mixed_other, flat[None, :], info, picks, probs, dattended, blocks, pool_rows
    )
    if fast:
        line_d = keep_far(*kept_d, *follows(far_d, dmixed_own), axis=1)
        line_d, got_d = scatter_line(line_d)
        kept_u = keep_near(*grid_u, *follows(near_u, dmixed_own))
        drop_u = drop_far(*kept_u)
        far_u = swap_far(drop_u)
        dmixed_other, dmixed_own = follows((dmixed_other, dmixed_own), drop_u, line_d)
    grad_other = dot_tn(normed, dmixed_other).astype(bf16)
    if fast:
        grad_got = swap(grad_other, "batch", 1)
        dmixed_own = follows(dmixed_own, grad_other)
    grad_own = dot_tn(normed, dmixed_own).astype(bf16)
    if fast:
        grid_q = split_grid(add(grad_own, grad_got), 512)
        drop_q = drop_near(*grid_q)
        near_q = swap_near(drop_q)
        line_u = keep_far(*kept_u, *follows(far_u, drop_q))
        line_u, got_u = scatter_line(line_u)
        dmixed_own = follows(dmixed_own, line_u)
    dnormed, sums_one = project_back(dmixed_own, dmixed_other, own_qkv, other_qkv, unit)
    vector_grads = jnp.concatenate([sums_one[:2], sums_two[:2]], 0)
    from_next = shift_seq(dnormed[count + pool_rows :].astype(bf16), -1)
    dpool = dnormed[count : count + pool_rows].astype(bf16)
    if fast:
        kept_q = keep_near(*grid_q, *follows(near_q, dnormed))
        drop_q = drop_far(*kept_q)
        far_q = swap_far(drop_q)
        spread = jnp.transpose(vector_grads.reshape(4, size, -1), (1, 0, 2)).reshape(size, 1, -1)
        span = spread.shape[2]
        spread = jnp.pad(spread.astype(bf16), ((0, 0), (0, 7), (0, width - span)))
        send = jnp.concatenate([dpool.reshape(size, blocks, width), spread], 1)
        pool_got = lax.all_to_all(send, "seq", 0, 0)
        sum_down = rows_of_side(sum_line(line_d, follows(got_d, drop_q)))
        output = layer_output(follows(after, drop_q, send), active, mat_down)
        line_q = keep_far(*kept_q, *follows(far_q, output))
        line_q, got_q = scatter_line(line_q)
        got = jnp.sum(follows(pool_got, line_q).astype(f32), axis=0)
        from_pool = got[:blocks]
        chip = got[blocks, :span].reshape(4, 2, -1)
        vector_sums = pick(chip, side, 1) + swap(pick(chip, 1 - side, 1), "batch", 1)
        sum_uo = rows_of_side(sum_line(line_u, follows(got_u, line_q)))
    else:
        from_pool = lax.psum_scatter(dpool, "seq", scatter_dimension=0, tiled=True).astype(f32)
        vector_sums = lax.psum_scatter(vector_grads, BOTH, scatter_dimension=1, tiled=True)
        output = layer_output(after, active, mat_down)
    input_grad = input_back(tokens, dnormed, dafter, from_pool, from_next, vectors)
    if fast:
        sum_qkv = rows_of_side(sum_line(line_q, follows(got_q, input_grad)))
    else:

        def scatter(own, other):
            full = in_order(side, own, other)
            sums = lax.psum_scatter(full, BOTH, scatter_dimension=1, tiled=True)
            return sums.astype(f32)

        sum_uo = scatter(
            jnp.concatenate([up_own, out_own], 1), jnp.concatenate([up_other, out_other], 1)
        )
        sum_qkv = scatter(grad_own, grad_other)
        sum_down = scatter(down_own, down_other)

    split = hidden // 2
    return (
        output[None],
        input_grad[None],
        vector_sums[0],
        vector_sums[1],
        whole_of(sum_qkv, 3),
        whole_of(sum_uo[:, :, split:], 1),
        vector_sums[2],
        vector_sums[3],
        whole_of(sum_uo[:, :, :split], 1),
        whole_of(sum_down, 1),
    )


def solution(mesh):
    tokens = P("batch", "seq", None)
    vector = P(BOTH)
    matrix = P(BOTH, None)
    return jax.shard_map(
        local,
        mesh=mesh,
        in_specs=(
            tokens,
            tokens,
            tokens,
            vector,
            vector,
            matrix,
            matrix,
            vector,
            vector,
            matrix,
            matrix,
        ),
        out_specs=(
            tokens,
            tokens,
            vector,
            vector,
            matrix,
            matrix,
            vector,
            vector,
            matrix,
            matrix,
        ),
        check_vma=False,
    )
```

```python
from functools import partial

import jax
import jax.numpy as jnp
from jax import lax
from jax.experimental import pallas as pl
from jax.experimental.pallas import tpu as pltpu
from jax.sharding import PartitionSpec as P

HEADS = 12
HEAD = 64
BLOCK = 64
TOPK = 16
QUAD = 4 * HEAD
FOLD = BLOCK + TOPK
NEG = -1e30


def dot_nn(a, b):
    return lax.dot_general(a, b, (((1,), (0,)), ((), ())), preferred_element_type=jnp.float32)


def dot_nt(a, b):
    return lax.dot_general(a, b, (((1,), (1,)), ((), ())), preferred_element_type=jnp.float32)


def dot_tn(a, b):
    return lax.dot_general(a, b, (((0,), (0,)), ((), ())), preferred_element_type=jnp.float32)


def spread_heads(rows):
    lane = lax.broadcasted_iota(jnp.int32, rows.shape, 1) // HEAD
    zero = jnp.zeros_like(rows)
    return jnp.concatenate([jnp.where(lane == h, rows, zero) for h in range(4)], 0)


def gather_heads(full):
    lane = lax.broadcasted_iota(jnp.int32, (BLOCK, QUAD), 1) // HEAD
    out = full[:BLOCK]
    for h in range(1, 4):
        out = jnp.where(lane == h, full[h * BLOCK : (h + 1) * BLOCK], out)
    return out


def prev_side():
    k = lax.broadcasted_iota(jnp.int32, (BLOCK, QUAD), 0)
    q = lax.broadcasted_iota(jnp.int32, (BLOCK, QUAD), 1) % BLOCK
    return k > q


def unfold(near, far, prev):
    zero = jnp.zeros_like(near)
    both = [jnp.where(prev, near, zero), jnp.where(prev, zero, near), far]
    return jnp.concatenate(both, 0).astype(jnp.bfloat16)


HALF = HEADS // 2 * HEAD
PAIR = 2 * BLOCK


def load_quad(own_ref, other_ref, rows, part, g):
    at = part * HALF
    if g == 0:
        return own_ref[rows, at : at + QUAD]
    if g == 1:
        return jnp.concatenate(
            [own_ref[rows, at + QUAD : at + HALF], other_ref[rows, at : at + HALF - QUAD]], 1
        )
    return other_ref[rows, at + HALF - QUAD : at + HALF]


def join_quads(quads):
    own = jnp.concatenate([quads[0], quads[1][:, : HALF - QUAD]], 1)
    other = jnp.concatenate([quads[1][:, HALF - QUAD :], quads[2]], 1)
    return own, other


CHAINS = [(b, g) for b in range(2) for g in range(HEADS // 4)]


def load_keys(prev, cur, picks, part, b, g):
    every = slice(None)
    before = load_quad(*prev, every, part, g) if b == 0 else load_quad(*cur, slice(0, BLOCK), part, g)
    here = load_quad(*cur, slice(b * BLOCK, (b + 1) * BLOCK), part, g)
    picked = load_quad(*picks, slice(b * TOPK, (b + 1) * TOPK), part - 1, g)
    return jnp.concatenate([before, here, picked], 0)


def attend_kernel(
    info_ref,
    sel_ref,
    bias_ref,
    pool_own,
    prev_own,
    cur_own,
    pool_other,
    prev_other,
    cur_other,
    att_ref,
    probs_ref,
    picks_ref,
):
    c = pl.program_id(0)
    core = info_ref[1]

    @pl.when(c == 0)
    def _():
        pool_rows = pool_own.shape[0]
        ids = lax.broadcasted_iota(jnp.int32, (sel_ref.shape[0], pool_rows), 1)
        one_hot = (ids == sel_ref[...]).astype(jnp.float32).astype(jnp.bfloat16)
        picks_ref[0] = dot_nn(one_hot, pool_own[:, HALF:]).astype(jnp.bfloat16)
        picks_ref[1] = dot_nn(one_hot, pool_other[:, HALF:]).astype(jnp.bfloat16)

    side = prev_side()
    edge = jnp.where((c == 0) & (info_ref[0] == 1), NEG, 0.0)
    rows = pl.ds(pl.multiple_of(c * 2 * TOPK, 2 * TOPK), 2 * TOPK)
    prev, cur = (prev_own, prev_other), (cur_own, cur_other)
    picks = (picks_ref.at[0, rows], picks_ref.at[1, rows])
    scored, values, fulls, outs = [], [], [], []
    for b, g in CHAINS:
        keys = load_keys(prev, cur, picks, 1, b, g)
        values.append(load_keys(prev, cur, picks, 2, b, g))
        wide_q = spread_heads(load_quad(*cur, slice(b * BLOCK, (b + 1) * BLOCK), 0, g))
        scored.append(dot_nt(keys, wide_q))
    for n, (b, g) in enumerate(CHAINS):
        scores = scored[n] * HEAD ** (-0.5)
        before = scores[:BLOCK] + edge if b == 0 else scores[:BLOCK]
        near = jnp.where(side, before, scores[BLOCK : 2 * BLOCK])
        far = scores[2 * BLOCK :] + bias_ref[b * TOPK : (b + 1) * TOPK]
        folded = jnp.concatenate([near, far], 0)
        top = jnp.max(folded, axis=0, keepdims=True)
        weights = jnp.exp(folded - top)
        probs = weights * (1.0 / jnp.sum(weights, axis=0, keepdims=True))
        probs_ref[b, g] = probs
        fulls.append(unfold(probs[:BLOCK], probs[BLOCK:], side))
    for n, (b, g) in enumerate(CHAINS):
        outs.append(gather_heads(dot_tn(fulls[n], values[n])).astype(jnp.bfloat16))
    for b in range(2):
        own, other = join_quads(outs[b * (HEADS // 4) : (b + 1) * (HEADS // 4)])
        here = slice(b * BLOCK, (b + 1) * BLOCK)
        att_ref[here, pl.ds(pl.multiple_of(core * HALF, 128), HALF)] = own
        att_ref[here, pl.ds(pl.multiple_of((1 - core) * HALF, 128), HALF)] = other


def attend(mixed_own, mixed_other, sel_col, bias_col, info, blocks, pool_rows):
    width = HEADS * HEAD
    halo = mixed_own.shape[0] // BLOCK - 1
    mixed_specs = [
        pl.BlockSpec((pool_rows, 3 * HALF), lambda c, f: (blocks * BLOCK // pool_rows, 0)),
        pl.BlockSpec((BLOCK, 3 * HALF), lambda c, f: (jnp.where(c == 0, halo, 2 * c - 1), 0)),
        pl.BlockSpec((PAIR, 3 * HALF), lambda c, f: (c, 0)),
    ]
    return pl.pallas_call(
        attend_kernel,
        grid_spec=pltpu.PrefetchScalarGridSpec(
            num_scalar_prefetch=1,
            grid=(blocks // 2,),
            in_specs=[
                pl.BlockSpec((blocks * TOPK, 1), lambda c, f: (0, 0)),
                pl.BlockSpec((2 * TOPK, 1), lambda c, f: (c, 0)),
            ]
            + mixed_specs * 2,
            out_specs=[
                pl.BlockSpec((PAIR, width), lambda c, f: (c, 0)),
                pl.BlockSpec((2, HEADS // 4, FOLD, QUAD), lambda c, f: (c, 0, 0, 0)),
                pl.BlockSpec((2, blocks * TOPK, 2 * HALF), lambda c, f: (0, 0, 0)),
            ],
        ),
        out_shape=[
            jax.ShapeDtypeStruct((blocks * BLOCK, width), jnp.bfloat16),
            jax.ShapeDtypeStruct((blocks, HEADS // 4, FOLD, QUAD), jnp.float32),
            jax.ShapeDtypeStruct((2, blocks * TOPK, 2 * HALF), jnp.bfloat16),
        ],
        compiler_params=pltpu.CompilerParams(vmem_limit_bytes=32 * 1024 * 1024),
        cost_estimate=pl.CostEstimate(
            flops=12_000_000_000, bytes_accessed=12_000_000, transcendentals=1_000_000
        ),
        name="attend",
    )(info, sel_col, bias_col, *[mixed_own] * 3, *[mixed_other] * 3)


def attend_back_kernel(
    pairs,
    info_ref,
    sel_ref,
    prev_own,
    cur_own,
    prev_other,
    cur_other,
    picks_ref,
    probs_ref,
    datt_ref,
    out_own,
    out_other,
    carry,
    dpicks,
):
    i = pl.program_id(0)
    core = info_ref[1]
    outs = (out_own, out_other)

    @pl.when(i == 0)
    def _():
        carry[...] = jnp.zeros_like(carry)

    @pl.when(i < pairs)
    def _():
        side = prev_side()
        datt = (
            datt_ref.at[:, pl.ds(pl.multiple_of(core * HALF, 128), HALF)],
            datt_ref.at[:, pl.ds(pl.multiple_of((1 - core) * HALF, 128), HALF)],
        )
        prev, cur = (prev_own, prev_other), (cur_own, cur_other)
        picks = (picks_ref.at[0], picks_ref.at[1])
        wide_qs, wide_ds, firsts, full_ps, full_ds = [], [], [], [], []
        for b, g in CHAINS:
            here = slice(b * BLOCK, (b + 1) * BLOCK)
            wide_qs.append(spread_heads(load_quad(*cur, here, 0, g)))
            wide_ds.append(spread_heads(load_quad(*datt, here, 0, g)))
            firsts.append(dot_nt(load_keys(prev, cur, picks, 2, b, g), wide_ds[-1]))
        for n, (b, g) in enumerate(CHAINS):
            probs, dprobs = probs_ref[b, g], firsts[n]
            near = jnp.where(side, dprobs[:BLOCK], dprobs[BLOCK : 2 * BLOCK])
            folded = jnp.concatenate([near, dprobs[2 * BLOCK :]], 0)
            inner = jnp.sum(probs * folded, axis=0, keepdims=True)
            dscores = probs * (folded - inner) * HEAD ** (-0.5)
            full_ps.append(unfold(probs[:BLOCK], probs[BLOCK:], side))
            full_ds.append(unfold(dscores[:BLOCK], dscores[BLOCK:], side))
        grads = []
        for n, (b, g) in enumerate(CHAINS):
            dvals = dot_nn(full_ps[n], wide_ds[n])
            dkeys = dot_nn(full_ds[n], wide_qs[n])
            dq = gather_heads(dot_tn(full_ds[n], load_keys(prev, cur, picks, 1, b, g)))
            grads.append((dq, dkeys, dvals))
        for part in range(3):
            lanes = slice(part * HALF, (part + 1) * HALF)
            a = join_quads([grad[part] for grad in grads[: HEADS // 4]])
            b = join_quads([grad[part] for grad in grads[HEADS // 4 :]])
            for s, out_ref in enumerate(outs):
                if part == 0:
                    out_ref[:, lanes] = carry[s, :, lanes].astype(jnp.bfloat16)
                    carry[s, :BLOCK, lanes] = a[s]
                    carry[s, BLOCK:, lanes] = b[s]
                else:
                    out_ref[:BLOCK, lanes] = carry[s, :BLOCK, lanes].astype(jnp.bfloat16)
                    low = carry[s, BLOCK:, lanes] + a[s][:BLOCK]
                    out_ref[BLOCK:, lanes] = low.astype(jnp.bfloat16)
                    carry[s, :BLOCK, lanes] = a[s][BLOCK : 2 * BLOCK] + b[s][:BLOCK]
                    carry[s, BLOCK:, lanes] = b[s][BLOCK : 2 * BLOCK]
                    both = jnp.concatenate([a[s][2 * BLOCK :], b[s][2 * BLOCK :]], 0)
                    rows = pl.ds(pl.multiple_of(i * 2 * TOPK, 2 * TOPK), 2 * TOPK)
                    picked = slice((part - 1) * HALF, part * HALF)
                    dpicks[s, rows, picked] = both.astype(jnp.bfloat16)

    @pl.when(i == pairs)
    def _():
        out_own[...] = carry[0].astype(jnp.bfloat16)
        out_other[...] = carry[1].astype(jnp.bfloat16)

    @pl.when(i > pairs)
    def _():
        ids = lax.broadcasted_iota(jnp.int32, (PAIR, 2 * pairs * TOPK), 0) + (i - pairs - 1) * PAIR
        one_hot = (ids == sel_ref[...]).astype(jnp.float32).astype(jnp.bfloat16)
        for s, out_ref in enumerate(outs):
            out_ref[:, :HALF] = jnp.zeros((PAIR, HALF), jnp.bfloat16)
            out_ref[:, HALF:] = dot_nn(one_hot, dpicks[s]).astype(jnp.bfloat16)


def attend_back(mixed_own, mixed_other, sel_row, info, picks, probs, datt, blocks, pool_rows):
    width = HEADS * HEAD
    pairs = blocks // 2
    total = mixed_own.shape[0]
    halo = total // BLOCK - 1

    def pair(i):
        return jnp.minimum(i, pairs - 1)

    def before_block(i, f):
        return (jnp.where(i == 0, halo, 2 * pair(i) - 1), 0)

    def out_block(i, f):
        return (jnp.where(i == 0, total // PAIR - 1, i - 1), 0)

    mixed_specs = [
        pl.BlockSpec((BLOCK, 3 * HALF), before_block),
        pl.BlockSpec((PAIR, 3 * HALF), lambda i, f: (pair(i), 0)),
    ]
    return pl.pallas_call(
        partial(attend_back_kernel, pairs),
        grid_spec=pltpu.PrefetchScalarGridSpec(
            num_scalar_prefetch=1,
            grid=(pairs + 1 + pool_rows // PAIR,),
            in_specs=[pl.BlockSpec((1, blocks * TOPK), lambda i, f: (0, 0))]
            + mixed_specs * 2
            + [
                pl.BlockSpec((2, 2 * TOPK, 2 * HALF), lambda i, f: (0, pair(i), 0)),
                pl.BlockSpec((2, HEADS // 4, FOLD, QUAD), lambda i, f: (pair(i), 0, 0, 0)),
                pl.BlockSpec((PAIR, width), lambda i, f: (pair(i), 0)),
            ],
            out_specs=[pl.BlockSpec((PAIR, 3 * HALF), out_block)] * 2,
            scratch_shapes=[
                pltpu.VMEM((2, PAIR, 3 * HALF), jnp.float32),
                pltpu.VMEM((2, blocks * TOPK, 2 * HALF), jnp.bfloat16),
            ],
        ),
        out_shape=[jax.ShapeDtypeStruct((total, 3 * HALF), jnp.bfloat16)] * 2,
        compiler_params=pltpu.CompilerParams(vmem_limit_bytes=32 * 1024 * 1024),
        cost_estimate=pl.CostEstimate(
            flops=20_000_000_000, bytes_accessed=18_000_000, transcendentals=0
        ),
        name="attend_back",
    )(info, sel_row, *[mixed_own] * 2, *[mixed_other] * 2, picks, probs, datt)


def standardize(values):
    center = values - jnp.mean(values, axis=-1, keepdims=True)
    spread = jnp.mean(center * center, axis=-1, keepdims=True)
    scale = lax.rsqrt(spread + 1e-05)
    return center * scale, scale


def standardize_back(unit, scale, dunit):
    return scale * (
        dunit
        - jnp.mean(dunit, axis=-1, keepdims=True)
        - unit * jnp.mean(dunit * unit, axis=-1, keepdims=True)
    )


ROWS = 256
CHUNK = 768
GROUP = 48
MIB = 1024 * 1024


def params(mib):
    return pltpu.CompilerParams(vmem_limit_bytes=mib * MIB)


def shape(rows, columns, dtype=jnp.bfloat16):
    return jax.ShapeDtypeStruct((rows, columns), dtype)


def cost(flops, moved):
    return pl.CostEstimate(flops=flops, bytes_accessed=moved, transcendentals=0)


def lanes_at(index, size):
    return pl.ds(pl.multiple_of(index * size, 128), size)


def pool_kernel(tokens_ref, unit_ref, out_ref):
    for b in range(out_ref.shape[0]):
        rows = slice(b * BLOCK, (b + 1) * BLOCK)
        unit, _ = standardize(tokens_ref[rows].astype(jnp.float32))
        unit_ref[rows] = unit
        out_ref[b : b + 1] = jnp.mean(unit, axis=0, keepdims=True)


def pool(tokens):
    rows, width = tokens.shape
    return pl.pallas_call(
        pool_kernel,
        out_shape=[shape(rows, width, jnp.float32), shape(rows // BLOCK, width, jnp.float32)],
        compiler_params=params(24),
        cost_estimate=cost(2_000_000_000, 6_000_000),
        name="pool",
    )(tokens)


def normal_kernel(own_ref, pool_ref, halo_ref, vec_ref, normed_ref, unit_ref):
    gain, bias = vec_ref[0:1], vec_ref[1:2]
    start = 0
    for ref in (own_ref, pool_ref, halo_ref):
        for r in range(0, ref.shape[0], BLOCK):
            unit = ref[r : r + BLOCK].astype(jnp.float32)
            if ref is halo_ref:
                unit, _ = standardize(unit)
                rows = slice(start, start + BLOCK)
                unit_ref[rows] = jnp.zeros(unit.shape, jnp.bfloat16)
                normed_ref[rows] = jnp.zeros(unit.shape, jnp.bfloat16)
                start += BLOCK
            rows = slice(start, start + BLOCK)
            unit_ref[rows] = unit.astype(jnp.bfloat16)
            normed_ref[rows] = (unit * gain + bias).astype(jnp.bfloat16)
            start += BLOCK


def normal(unit_own, unit_pool, halo, vectors):
    width = unit_own.shape[1]
    total = unit_own.shape[0] + unit_pool.shape[0] + 2 * halo.shape[0]
    return pl.pallas_call(
        normal_kernel,
        out_shape=[shape(total, width), shape(total, width)],
        compiler_params=params(24),
        cost_estimate=cost(2_000_000_000, 10_000_000),
        name="normal",
    )(unit_own, unit_pool, halo, vectors)


def mlp_kernel(
    info_ref,
    att_ref,
    tokens_ref,
    dy_ref,
    vec_ref,
    out_own,
    out_other,
    up_own,
    up_other,
    down_ref,
    output_ref,
    dafter_ref,
    datt_ref,
    gd_own,
    gd_other,
    gu_own,
    gu_other,
    sums_ref,
    after_ref,
    n2_ref,
    active_ref,
    dh_ref,
    dn2_ref,
    total_ref,
    grad_ref,
    acc,
    low,
):
    i = pl.program_id(0)
    core = info_ref[1]
    side = out_own.shape[1]
    count, width = n2_ref.shape
    row_steps = count // ROWS
    steps = pl.num_programs(0) - 2 * row_steps
    half = steps // 2
    j = i - row_steps

    @pl.when(i < row_steps)
    def _():
        rows = pl.ds(pl.multiple_of(i * ROWS, ROWS), ROWS)
        after_ref[rows, lanes_at(core, side)] = dot_nn(att_ref[rows], out_own[...])
        after_ref[rows, lanes_at(1 - core, side)] = dot_nn(att_ref[rows], out_other[...])
        after = tokens_ref[...].astype(jnp.float32) + after_ref[rows]
        after_ref[rows] = after
        unit, _ = standardize(after)
        n2_ref[rows] = (unit * vec_ref[2:3] + vec_ref[3:4]).astype(jnp.bfloat16)
        dn2_ref[rows] = jnp.zeros((ROWS, width), jnp.float32)
        total_ref[rows] = after

    @pl.when((j >= 0) & (j < steps))
    def _():
        weight = jnp.where(j < half, up_own[...], up_other[...])
        down = down_ref[...]
        root = (2.0 / 3.141592653589793) ** 0.5

        def first(r):
            rows = slice(r, r + ROWS)
            return rows, dot_nn(n2_ref[rows], weight), dot_nt(dy_ref[rows], down)

        def second(rows, u, dactive):
            square = u * u
            t = jnp.tanh(u * (root + (0.044715 * root) * square))
            upper = 0.5 + 0.5 * t
            active = u * upper
            bend = active * ((1.0 - t) * (root + (3.0 * 0.044715 * root) * square))
            active = active.astype(jnp.bfloat16)
            dh = (dactive * (upper + bend)).astype(jnp.bfloat16)
            active_ref[rows] = active
            dh_ref[rows] = dh
            dn2_ref[rows] += dot_nt(dh, weight)
            total_ref[rows] += dot_nn(active, down)

        waiting = first(0)
        for r in range(ROWS, count, ROWS):
            coming = first(r)
            second(*waiting)
            waiting = coming
        second(*waiting)
        grad_ref[...] = dot_tn(active_ref[...], dy_ref[...]).astype(jnp.bfloat16)
        per = gd_own.shape[1] // side
        for s in range(gd_own.shape[0] // GROUP):
            for g in range(per):
                rows = slice((s * per + g) * GROUP, (s * per + g + 1) * GROUP)
                to = (slice(s * GROUP, (s + 1) * GROUP), slice(g * side, (g + 1) * side))
                gd_own[to] = grad_ref[rows, lanes_at(core, side)]
                gd_other[to] = grad_ref[rows, lanes_at(1 - core, side)]
        grad = dot_tn(n2_ref[...], dh_ref[...]).astype(jnp.bfloat16)

        @pl.when(j < half)
        def _():
            gu_own[:, lanes_at(j, CHUNK)] = grad

        @pl.when(j >= half)
        def _():
            gu_other[:, lanes_at(j - half, CHUNK)] = grad

    @pl.when(j == steps)
    def _():
        sums_ref[...] = jnp.zeros_like(sums_ref)
        acc[...] = jnp.zeros_like(acc)

    @pl.when(j >= steps)
    def _():
        rows = pl.ds(pl.multiple_of((j - steps) * ROWS, ROWS), ROWS)
        output_ref[...] = total_ref[rows].astype(jnp.bfloat16)
        unit, scale = standardize(after_ref[rows])
        dn2 = dn2_ref[rows]
        sums_ref[0:1] += jnp.sum(dn2 * unit, axis=0, keepdims=True)
        sums_ref[1:2] += jnp.sum(dn2, axis=0, keepdims=True)
        dafter = dy_ref[rows].astype(jnp.float32)
        dafter += standardize_back(unit, scale, dn2 * vec_ref[2:3])
        dafter_ref[...] = dafter
        low[...] = dafter.astype(jnp.bfloat16)
        datt = dot_nt(low[:, lanes_at(core, side)], out_own[...])
        datt += dot_nt(low[:, lanes_at(1 - core, side)], out_other[...])
        datt_ref[...] = datt.astype(jnp.bfloat16)
        acc[...] += dot_tn(att_ref[rows], low[...])

    @pl.when(i == pl.num_programs(0) - 1)
    def _():
        at = gu_own.shape[1] - side
        gu_own[:, at:] = acc[:, lanes_at(core, side)].astype(jnp.bfloat16)
        gu_other[:, at:] = acc[:, lanes_at(1 - core, side)].astype(jnp.bfloat16)


def ff_maps(hidden, before):
    steps = hidden // CHUNK
    half = steps // 2
    step = lambda i: jnp.clip(i - before, 0, steps - 1)
    own = lambda i, f: (0, jnp.minimum(step(i), half - 1))
    other = lambda i, f: (0, jnp.maximum(step(i) - half, 0))
    place = lambda i, f: lax.rem(f[1] * half + step(i), steps)
    return steps, own, other, place


def out_columns(own):
    width = own.shape[0]
    half = width // 2
    return pl.BlockSpec((width, half), lambda i, f: (0, own.shape[1] // half - 1))


def mlp(attended, tokens, upstream, vectors, own, other, mat_down, info):
    count, width = tokens.shape
    hidden = mat_down.shape[0]
    row_steps = count // ROWS
    steps, first, second, place = ff_maps(hidden, row_steps)
    whole = lambda i, f: (0, 0)
    once = pl.Buffered(1)
    full = pl.BlockSpec((count, width), whole, pipeline_mode=once)
    grads = pl.BlockSpec(own.shape, whole, pipeline_mode=once)
    low_grads = pl.BlockSpec((CHUNK // 4, 2 * width), lambda i, f: (place(i, f), 0))
    row = pl.BlockSpec((ROWS, width), lambda i, f: (jnp.maximum(i - row_steps - steps, 0), 0))
    f32 = jnp.float32
    return pl.pallas_call(
        mlp_kernel,
        grid_spec=pltpu.PrefetchScalarGridSpec(
            num_scalar_prefetch=1,
            grid=(2 * row_steps + steps,),
            in_specs=[
                full,
                pl.BlockSpec((ROWS, width), lambda i, f: (jnp.minimum(i, row_steps - 1), 0)),
                full,
                pl.BlockSpec(vectors.shape, whole),
                out_columns(own),
                out_columns(other),
                pl.BlockSpec((width, CHUNK), first),
                pl.BlockSpec((width, CHUNK), second),
                pl.BlockSpec((CHUNK, width), lambda i, f: (place(i, f), 0)),
            ],
            out_specs=[
                row,
                row,
                row,
                low_grads,
                low_grads,
                grads,
                grads,
                pl.BlockSpec((8, width), whole),
            ],
            scratch_shapes=[
                pltpu.VMEM((count, width), f32),
                pltpu.VMEM((count, width), jnp.bfloat16),
                pltpu.VMEM((count, CHUNK), jnp.bfloat16),
                pltpu.VMEM((count, CHUNK), jnp.bfloat16),
                pltpu.VMEM((count, width), f32),
                pltpu.VMEM((count, width), f32),
                pltpu.VMEM((CHUNK, width), jnp.bfloat16),
                pltpu.VMEM((width, width), f32),
                pltpu.VMEM((ROWS, width), jnp.bfloat16),
            ],
        ),
        out_shape=[
            shape(count, width),
            shape(count, width, f32),
            shape(count, width),
            shape(hidden // 4, 2 * width),
            shape(hidden // 4, 2 * width),
            shape(*own.shape),
            shape(*own.shape),
            shape(8, width, f32),
        ],
        compiler_params=params(58),
        cost_estimate=cost(40_000_000_000, 30_000_000),
        name="mlp",
    )(info, attended, tokens, upstream, vectors, own, other, own, other, mat_down)


def project_back_kernel(dm_own, dm_other, own_ref, other_ref, unit_ref, dn_ref, sums_ref):
    @pl.when(pl.program_id(0) == 0)
    def _():
        sums_ref[...] = jnp.zeros_like(sums_ref)

    dn = dot_nt(dm_own[...], own_ref[...]) + dot_nt(dm_other[...], other_ref[...])
    dn_ref[...] = dn
    sums_ref[0:1] += jnp.sum(dn * unit_ref[...].astype(jnp.float32), axis=0, keepdims=True)
    sums_ref[1:2] += jnp.sum(dn, axis=0, keepdims=True)


def project_back(dm_own, dm_other, own, other, unit):
    total, width = unit.shape
    rows = total // 4
    row = lambda i: (i, 0)
    whole = pl.BlockSpec((width, 3 * HALF), lambda i: (0, 0))
    return pl.pallas_call(
        project_back_kernel,
        grid=(total // rows,),
        in_specs=[
            pl.BlockSpec((rows, 3 * HALF), row),
            pl.BlockSpec((rows, 3 * HALF), row),
            whole,
            whole,
            pl.BlockSpec((rows, width), row),
        ],
        out_specs=[pl.BlockSpec((rows, width), row), pl.BlockSpec((8, width), lambda i: (0, 0))],
        out_shape=[shape(total, width, jnp.float32), shape(8, width, jnp.float32)],
        compiler_params=params(32),
        cost_estimate=cost(6_000_000_000, 16_000_000),
        name="project_back",
    )(dm_own, dm_other, own, other, unit)


def input_kernel(tokens_ref, dn_ref, dafter_ref, pool_ref, next_ref, vec_ref, out_ref):
    i = pl.program_id(0)
    gain = vec_ref[0:1]
    per = tokens_ref.shape[0] // BLOCK
    last = (i == pl.num_programs(0) - 1).astype(jnp.float32)
    for b in range(per):
        rows = slice(b * BLOCK, (b + 1) * BLOCK)
        unit, scale = standardize(tokens_ref[rows].astype(jnp.float32))
        dn = dn_ref[rows] + pool_ref[pl.ds(i * per + b, 1)] * (1.0 / BLOCK)
        if b == per - 1:
            dn += next_ref[...].astype(jnp.float32) * last
        out_ref[rows] = dafter_ref[rows] + standardize_back(unit, scale, dn * gain)


def input_back(tokens, dnormed, dafter, from_pool, from_next, vectors):
    count, width = tokens.shape
    row = pl.BlockSpec((ROWS, width), lambda i: (i, 0))
    whole = lambda i: (0, 0)
    return pl.pallas_call(
        input_kernel,
        grid=(count // ROWS,),
        in_specs=[
            row,
            row,
            row,
            pl.BlockSpec(from_pool.shape, whole),
            pl.BlockSpec(from_next.shape, whole),
            pl.BlockSpec(vectors.shape, whole),
        ],
        out_specs=row,
        out_shape=shape(count, width, jnp.float32),
        compiler_params=params(24),
        cost_estimate=cost(3_000_000_000, 12_000_000),
        name="input_back",
    )(tokens, dnormed, dafter, from_pool, from_next, vectors)


def shift_seq(value, distance):
    size = lax.axis_size("seq")
    route = [(i - distance, i) for i in range(size) if 0 <= i - distance < size]
    return lax.ppermute(value, "seq", route)


BOTH = ("seq", "batch")


def follows(value, *earlier):
    return lax.optimization_barrier((value, earlier))[0]


def flip_route(size, bit):
    return [(i, i ^ bit) for i in range(size)]


def ring_route(size, stride, steps):
    return [(i, (i + stride * steps) % size) for i in range(size)]


def swap(value, axis, bit):
    return lax.ppermute(value, axis, flip_route(lax.axis_size(axis), bit))


def in_order(bit, own, other):
    return jnp.stack([jnp.where(bit == 0, own, other), jnp.where(bit == 0, other, own)])


def pick(value, index, axis):
    return lax.dynamic_index_in_dim(value, index, axis, keepdims=False)


def add(a, b):
    return (a.astype(jnp.float32) + b.astype(jnp.float32)).astype(jnp.bfloat16)


def place():
    at = lax.axis_index("seq")
    return at // 4, at // 2 % 2, at % 2


def send_line(slab):
    size = lax.axis_size("seq")
    return [lax.ppermute(slab, "seq", ring_route(size, 4, k)) for k in range(1, size // 4)]


def join_line(slab, got):
    z = place()[0]
    stack = jnp.stack([slab] + got)
    layers = stack.shape[0]
    parts = [lax.dynamic_slice_in_dim(stack, (z - k) % layers, 1, 0) for k in range(layers)]
    return jnp.concatenate(parts, 0)


def send_near(line, cut):
    first, second = line[:, :, :cut], line[:, :, cut:]
    return first, second, swap(first, "seq", 1), swap(second, "seq", 2)


def join_near(first, second, first_got, second_got):
    _, y, x = place()
    return in_order(x, first, first_got), in_order(y, second, second_got)


def send_far(first, second):
    return swap(first, "seq", 2), swap(second, "seq", 1)


def join_far(first, second, first_got, second_got):
    _, y, x = place()
    first = jnp.transpose(in_order(y, first, first_got), (2, 0, 1, 3, 4))
    second = jnp.transpose(in_order(x, second, second_got), (2, 1, 0, 3, 4))
    rows = first.shape[3] * lax.axis_size("seq")
    return first.reshape(rows, -1), second.reshape(rows, -1)


def split_grid(full, cut, axis=4):
    grid = full.reshape(lax.axis_size("seq") // 4, 2, 2, -1, full.shape[1])
    return jnp.split(grid, [cut], axis)


def drop_near(first, second):
    _, y, x = place()
    return pick(first, 1 - x, 2), pick(second, 1 - y, 1)


def keep_near(first, second, first_got, second_got):
    _, y, x = place()
    return add(pick(first, x, 2), first_got), add(pick(second, y, 1), second_got)


def drop_far(first, second):
    _, y, x = place()
    return pick(first, 1 - y, 1), pick(second, 1 - x, 1)


def keep_far(first, second, first_got, second_got, axis=2):
    _, y, x = place()
    parts = [add(pick(first, y, 1), first_got), add(pick(second, x, 1), second_got)]
    return jnp.concatenate(parts, axis)


def swap_near(dropped):
    return swap(dropped[0], "seq", 1), swap(dropped[1], "seq", 2)


def swap_far(dropped):
    return swap(dropped[0], "seq", 2), swap(dropped[1], "seq", 1)


def scatter_line(line):
    z = place()[0]
    size = lax.axis_size("seq")
    layers = size // 4
    got = [
        lax.ppermute(pick(line, (z + k) % layers, 0), "seq", ring_route(size, 4, k))
        for k in range(1, layers)
    ]
    return pick(line, z, 0), got


def sum_line(own, got):
    return sum((g.astype(jnp.float32) for g in got), own.astype(jnp.float32))


def paired():
    return lax.axis_size("batch") == 2 and lax.axis_size("seq") % 4 == 0


def side_index():
    return lax.axis_index("batch") % 2


def halves_of(matrix, groups):
    rows, columns = matrix.shape
    parts = matrix.reshape(rows, groups, 2, columns // (2 * groups))
    return jnp.transpose(parts, (2, 0, 1, 3)).reshape(2, rows, columns // 2)


def whole_of(halves, groups):
    _, rows, columns = halves.shape
    parts = halves.reshape(2, rows, groups, columns // groups)
    return jnp.transpose(parts, (1, 2, 0, 3)).reshape(rows, 2 * columns)


def rows_of_side(total):
    side = side_index()
    total = total.reshape(2, -1, total.shape[1])
    got = swap(pick(total, 1 - side, 0), "batch", 1)
    return in_order(side, pick(total, side, 0), got)


def local(
    inputs, selection, cotangent, ln1_gain, ln1_bias, w_qkv, w_out, ln2_gain, ln2_bias, w_up, w_down
):
    bf16, f32 = jnp.bfloat16, jnp.float32
    tokens = inputs[0]
    chosen = selection[0]
    upstream = cotangent[0]
    count, width = tokens.shape
    hidden = w_up.shape[1]
    blocks = count // BLOCK
    size = lax.axis_size("seq")
    pool_rows = blocks * size
    at = lax.axis_index("seq")
    side = side_index()
    fast = paired()

    half_qkv = halves_of(w_qkv, 3)
    half_uo = jnp.concatenate([halves_of(w_up, 1), halves_of(w_out, 1)], 2)
    vectors = jnp.stack([ln1_gain, ln1_bias, ln2_gain, ln2_bias])
    if fast:
        columns = jnp.pad(vectors.T, ((0, 0), (0, 124)))
        columns = jnp.broadcast_to(columns, (2,) + columns.shape)
        bundle = jnp.concatenate([columns, half_qkv, half_uo], 2)
        got = swap(pick(bundle, 1 - side, 0), "batch", 1)
        slab = in_order(side, pick(bundle, side, 0), got).reshape(-1, bundle.shape[2])
        third = width // 3
        per = slab.shape[0] // 3
        unit_own, pooled = pool(tokens)
        pooled = jnp.transpose(pooled.astype(bf16).reshape(per, 3, third), (1, 0, 2))
        pooled = pooled.reshape(-1, third)
        front = third + 128
        edge = 128 + half_qkv.shape[2]
        slab_q = jnp.concatenate([pooled, slab[:, :edge]], 1)
        slab_u = slab[:, edge:]
        line_got = send_line(slab_q)
        halo = shift_seq(follows(tokens[-BLOCK:], slab), 1)
        line_got_u = send_line(slab_u)
        line_q = join_line(slab_q, follows(line_got, halo))
        near = send_near(line_q, 768)
        wide_q = join_near(*near)
        far = send_far(*wide_q)
        line_u = join_line(slab_u, follows(line_got_u, wide_q))
        near_u = send_near(line_u, 1024)
        first, second = join_far(*wide_q, *follows(far, near_u[0], near_u[1]))
        own_qkv = jnp.concatenate([first[:, front:], second], 1)
        other_qkv = swap(own_qkv, "batch", 1)
        unit_pool = jnp.transpose(first[:, :third].reshape(size, 3, per, third), (0, 2, 1, 3))
        unit_pool = unit_pool.reshape(pool_rows, width)
        vectors = first[:, third : third + 4].T.astype(f32)
    else:
        gathered = lax.all_gather(half_qkv, BOTH, axis=1, tiled=True)
        own_qkv, other_qkv = pick(gathered, side, 0), pick(gathered, 1 - side, 0)
        gathered = lax.all_gather(half_uo, BOTH, axis=1, tiled=True)
        own_uo, other_uo = pick(gathered, side, 0), pick(gathered, 1 - side, 0)
        halo = shift_seq(tokens[-BLOCK:], 1)
        unit_own, pooled = pool(tokens)
        unit_pool = lax.all_gather(pooled.astype(bf16), "seq", axis=0, tiled=True)
        vectors = lax.all_gather(vectors, BOTH, axis=1, tiled=True).astype(f32)
    mat_down = lax.all_gather(w_down, BOTH, axis=0, tiled=True)
    vectors = jnp.pad(vectors, ((0, 4), (0, 0)))

    normed, unit = normal(unit_own, unit_pool, halo, vectors)
    mixed_own = dot_nn(normed, own_qkv).astype(bf16)
    mixed_other = dot_nn(normed, other_qkv).astype(bf16)
    if fast:
        wide_u = join_near(*follows(near_u, mixed_other))
        far_u = send_far(*wide_u)
        mixed_own = follows(mixed_own, wide_u)

    block_ids = at * blocks + jnp.arange(blocks, dtype=jnp.int32)
    flat = chosen.reshape(blocks * TOPK)
    far_bias = jnp.where(chosen < block_ids[:, None], 0.0, NEG).reshape(blocks * TOPK, 1)
    info = jnp.stack([(at == 0).astype(jnp.int32), side])
    attended, probs, picks = attend(
        mixed_own, mixed_other, flat[:, None], far_bias, info, blocks, pool_rows
    )
    if fast:
        own_uo = jnp.concatenate(join_far(*wide_u, *follows(far_u, attended)), 1)
        other_uo = swap(own_uo, "batch", 1)
    output, dafter, dattended, down_own, down_other, uo_own, uo_other, sums_two = mlp(
        attended, tokens, upstream, vectors, own_uo, other_uo, mat_down, info
    )
    if fast:
        down_got = swap(down_other, "batch", 1)
        uo_got = swap(uo_other, "batch", 1)
        grid_d = split_grid(add(down_own, down_got), width)
        drop_d = drop_near(*grid_d)
        near_d = swap_near(drop_d)
        grid_u = split_grid(add(uo_own, follows(uo_got, drop_d)), 1024)
        drop_u = drop_near(*grid_u)
        near_u = swap_near(drop_u)
        dattended = follows(dattended, drop_u)

    dmixed_own, dmixed_other = attend_back(
        mixed_own, mixed_other, flat[None, :], info, picks, probs, dattended, blocks, pool_rows
    )
    if fast:
        kept_d = keep_near(*grid_d, *follows(near_d, dmixed_own))
        drop_d = drop_far(*kept_d)
        far_d = swap_far(drop_d)
        dmixed_other = follows(dmixed_other, drop_d)
    grad_other = dot_tn(normed, dmixed_other).astype(bf16)
    if fast:
        grad_got = swap(grad_other, "batch", 1)
        kept_u = keep_near(*grid_u, *follows(near_u, grad_other))
        drop_u = drop_far(*kept_u)
        far_u = swap_far(drop_u)
        dmixed_own = follows(dmixed_own, drop_u)
    grad_own = dot_tn(normed, dmixed_own).astype(bf16)
    if fast:
        grid_q = split_grid(add(grad_own, grad_got), 512)
        drop_q = drop_near(*grid_q)
        near_q = swap_near(drop_q)
        line_d = keep_far(*kept_d, *follows(far_d, drop_q))
        line_d, got_d = scatter_line(line_d)
        dmixed_own = follows(dmixed_own, line_d)
    dnormed, sums_one = project_back(dmixed_own, dmixed_other, own_qkv, other_qkv, unit)
    vector_grads = jnp.concatenate([sums_one[:2], sums_two[:2]], 0)
    from_next = shift_seq(dnormed[-BLOCK:].astype(bf16), -1)
    dpool = dnormed[count : count + pool_rows].astype(bf16)
    if fast:
        kept_q = keep_near(*grid_q, *follows(near_q, dnormed))
        drop_q = drop_far(*kept_q)
        far_q = swap_far(drop_q)
        spread = jnp.transpose(vector_grads.reshape(4, size, -1), (1, 0, 2)).reshape(size, 1, -1)
        span = spread.shape[2]
        spread = jnp.pad(spread.astype(bf16), ((0, 0), (0, 7), (0, width - span)))
        send = jnp.concatenate([dpool.reshape(size, blocks, width), spread], 1)
        pool_got = lax.all_to_all(send, "seq", 0, 0)
        line_u = keep_far(*kept_u, *follows(far_u, drop_q))
        line_u, got_u = scatter_line(line_u)
        line_q = keep_far(*kept_q, *follows(far_q, send, line_u))
        line_q, got_q = scatter_line(line_q)
        sum_down = sum_line(line_d, follows(got_d, line_q)).reshape(GROUP, 2, -1)
        sum_down = rows_of_side(jnp.transpose(sum_down, (1, 0, 2)).reshape(2 * GROUP, -1))
        sum_down = sum_down.reshape(2, GROUP, 2, -1)
        sum_down = jnp.transpose(sum_down, (2, 1, 0, 3)).reshape(-1, width)
        got = jnp.sum(follows(pool_got, line_q).astype(f32), axis=0)
        from_pool = got[:blocks]
        chip = got[blocks, :span].reshape(4, 2, -1)
        vector_sums = pick(chip, side, 1) + swap(pick(chip, 1 - side, 1), "batch", 1)
        sum_uo = rows_of_side(sum_line(line_u, follows(got_u, line_q)))
    else:
        from_pool = lax.psum_scatter(dpool, "seq", scatter_dimension=0, tiled=True).astype(f32)
        vector_sums = lax.psum_scatter(vector_grads, BOTH, scatter_dimension=1, tiled=True)
    input_grad = input_back(tokens, dnormed, dafter, from_pool, from_next, vectors)
    if fast:
        sum_qkv = rows_of_side(sum_line(line_q, follows(got_q, input_grad)))
    else:

        def scatter(own, other):
            full = in_order(side, own, other)
            sums = lax.psum_scatter(full, BOTH, scatter_dimension=1, tiled=True)
            return sums.astype(f32)

        sum_uo = scatter(uo_own, uo_other)
        sum_qkv = scatter(grad_own, grad_other)
        full = jnp.stack([down_own, down_other]).reshape(2, -1, GROUP, 4, width // 2)
        full = jnp.transpose(full, (1, 3, 2, 0, 4)).reshape(hidden, 2, width // 2)
        full = in_order(side, full[:, 0], full[:, 1])
        full = jnp.transpose(full, (1, 0, 2)).reshape(hidden, width)
        sum_down = lax.psum_scatter(full, BOTH, scatter_dimension=0, tiled=True).astype(f32)

    split = hidden // 2
    return (
        output[None],
        input_grad[None],
        vector_sums[0],
        vector_sums[1],
        whole_of(sum_qkv, 3),
        whole_of(sum_uo[:, :, split:], 1),
        vector_sums[2],
        vector_sums[3],
        whole_of(sum_uo[:, :, :split], 1),
        sum_down,
    )


def solution(mesh):
    tokens = P("batch", "seq", None)
    vector = P(BOTH)
    matrix = P(BOTH, None)
    return jax.shard_map(
        local,
        mesh=mesh,
        in_specs=(
            tokens,
            tokens,
            tokens,
            vector,
            vector,
            matrix,
            matrix,
            vector,
            vector,
            matrix,
            matrix,
        ),
        out_specs=(
            tokens,
            tokens,
            vector,
            vector,
            matrix,
            matrix,
            vector,
            vector,
            matrix,
            matrix,
        ),
        check_vma=False,
    )
```

```python
from functools import partial

import jax
import jax.numpy as jnp
from jax import lax
from jax.experimental import pallas as pl
from jax.experimental.pallas import tpu as pltpu
from jax.sharding import PartitionSpec as P

HEADS = 12
HEAD = 64
BLOCK = 64
TOPK = 16
QUAD = 4 * HEAD
FOLD = BLOCK + TOPK
NEG = -1e30


def dot_nn(a, b):
    return lax.dot_general(a, b, (((1,), (0,)), ((), ())), preferred_element_type=jnp.float32)


def dot_nt(a, b):
    return lax.dot_general(a, b, (((1,), (1,)), ((), ())), preferred_element_type=jnp.float32)


def dot_tn(a, b):
    return lax.dot_general(a, b, (((0,), (0,)), ((), ())), preferred_element_type=jnp.float32)


def spread_heads(rows):
    lane = lax.broadcasted_iota(jnp.int32, rows.shape, 1) // HEAD
    zero = jnp.zeros_like(rows)
    return jnp.concatenate([jnp.where(lane == h, rows, zero) for h in range(4)], 0)


def gather_heads(full):
    lane = lax.broadcasted_iota(jnp.int32, (BLOCK, QUAD), 1) // HEAD
    out = full[:BLOCK]
    for h in range(1, 4):
        out = jnp.where(lane == h, full[h * BLOCK : (h + 1) * BLOCK], out)
    return out


def prev_side():
    k = lax.broadcasted_iota(jnp.int32, (BLOCK, QUAD), 0)
    q = lax.broadcasted_iota(jnp.int32, (BLOCK, QUAD), 1) % BLOCK
    return k > q


def unfold(near, far, prev):
    zero = jnp.zeros_like(near)
    both = [jnp.where(prev, near, zero), jnp.where(prev, zero, near), far]
    return jnp.concatenate(both, 0).astype(jnp.bfloat16)


HALF = HEADS // 2 * HEAD
PAIR = 2 * BLOCK


def load_quad(own_ref, other_ref, rows, part, g):
    at = part * HALF
    if g == 0:
        return own_ref[rows, at : at + QUAD]
    if g == 1:
        return jnp.concatenate(
            [own_ref[rows, at + QUAD : at + HALF], other_ref[rows, at : at + HALF - QUAD]], 1
        )
    return other_ref[rows, at + HALF - QUAD : at + HALF]


def join_quads(quads):
    own = jnp.concatenate([quads[0], quads[1][:, : HALF - QUAD]], 1)
    other = jnp.concatenate([quads[1][:, HALF - QUAD :], quads[2]], 1)
    return own, other


CHAINS = [(b, g) for b in range(2) for g in range(HEADS // 4)]


def load_keys(prev, cur, picks, part, b, g):
    every = slice(None)
    before = load_quad(*prev, every, part, g) if b == 0 else load_quad(*cur, slice(0, BLOCK), part, g)
    here = load_quad(*cur, slice(b * BLOCK, (b + 1) * BLOCK), part, g)
    picked = load_quad(*picks, slice(b * TOPK, (b + 1) * TOPK), part - 1, g)
    return jnp.concatenate([before, here, picked], 0)


def attend_kernel(
    info_ref,
    sel_ref,
    bias_ref,
    pool_own,
    prev_own,
    cur_own,
    pool_other,
    prev_other,
    cur_other,
    att_ref,
    probs_ref,
    picks_ref,
):
    c = pl.program_id(0)
    core = info_ref[1]

    @pl.when(c == 0)
    def _():
        pool_rows = pool_own.shape[0]
        ids = lax.broadcasted_iota(jnp.int32, (sel_ref.shape[0], pool_rows), 1)
        one_hot = (ids == sel_ref[...]).astype(jnp.float32).astype(jnp.bfloat16)
        picks_ref[0] = dot_nn(one_hot, pool_own[:, HALF:]).astype(jnp.bfloat16)
        picks_ref[1] = dot_nn(one_hot, pool_other[:, HALF:]).astype(jnp.bfloat16)

    side = prev_side()
    edge = jnp.where((c == 0) & (info_ref[0] == 1), NEG, 0.0)
    rows = pl.ds(pl.multiple_of(c * 2 * TOPK, 2 * TOPK), 2 * TOPK)
    prev, cur = (prev_own, prev_other), (cur_own, cur_other)
    picks = (picks_ref.at[0, rows], picks_ref.at[1, rows])
    scored, values, fulls, outs = [], [], [], []
    for b, g in CHAINS:
        keys = load_keys(prev, cur, picks, 1, b, g)
        values.append(load_keys(prev, cur, picks, 2, b, g))
        wide_q = spread_heads(load_quad(*cur, slice(b * BLOCK, (b + 1) * BLOCK), 0, g))
        scored.append(dot_nt(keys, wide_q))
    for n, (b, g) in enumerate(CHAINS):
        scores = scored[n] * HEAD ** (-0.5)
        before = scores[:BLOCK] + edge if b == 0 else scores[:BLOCK]
        near = jnp.where(side, before, scores[BLOCK : 2 * BLOCK])
        far = scores[2 * BLOCK :] + bias_ref[b * TOPK : (b + 1) * TOPK]
        folded = jnp.concatenate([near, far], 0)
        top = jnp.max(folded, axis=0, keepdims=True)
        weights = jnp.exp(folded - top)
        probs = weights * (1.0 / jnp.sum(weights, axis=0, keepdims=True))
        probs_ref[b, g] = probs
        fulls.append(unfold(probs[:BLOCK], probs[BLOCK:], side))
    for n, (b, g) in enumerate(CHAINS):
        outs.append(gather_heads(dot_tn(fulls[n], values[n])).astype(jnp.bfloat16))
    for b in range(2):
        own, other = join_quads(outs[b * (HEADS // 4) : (b + 1) * (HEADS // 4)])
        here = slice(b * BLOCK, (b + 1) * BLOCK)
        att_ref[here, pl.ds(pl.multiple_of(core * HALF, 128), HALF)] = own
        att_ref[here, pl.ds(pl.multiple_of((1 - core) * HALF, 128), HALF)] = other


def attend(mixed_own, mixed_other, sel_col, bias_col, info, blocks, pool_rows):
    width = HEADS * HEAD
    halo = mixed_own.shape[0] // BLOCK - 1
    mixed_specs = [
        pl.BlockSpec((pool_rows, 3 * HALF), lambda c, f: (blocks * BLOCK // pool_rows, 0)),
        pl.BlockSpec((BLOCK, 3 * HALF), lambda c, f: (jnp.where(c == 0, halo, 2 * c - 1), 0)),
        pl.BlockSpec((PAIR, 3 * HALF), lambda c, f: (c, 0)),
    ]
    return pl.pallas_call(
        attend_kernel,
        grid_spec=pltpu.PrefetchScalarGridSpec(
            num_scalar_prefetch=1,
            grid=(blocks // 2,),
            in_specs=[
                pl.BlockSpec((blocks * TOPK, 1), lambda c, f: (0, 0)),
                pl.BlockSpec((2 * TOPK, 1), lambda c, f: (c, 0)),
            ]
            + mixed_specs * 2,
            out_specs=[
                pl.BlockSpec((PAIR, width), lambda c, f: (c, 0)),
                pl.BlockSpec((2, HEADS // 4, FOLD, QUAD), lambda c, f: (c, 0, 0, 0)),
                pl.BlockSpec((2, blocks * TOPK, 2 * HALF), lambda c, f: (0, 0, 0)),
            ],
        ),
        out_shape=[
            jax.ShapeDtypeStruct((blocks * BLOCK, width), jnp.bfloat16),
            jax.ShapeDtypeStruct((blocks, HEADS // 4, FOLD, QUAD), jnp.float32),
            jax.ShapeDtypeStruct((2, blocks * TOPK, 2 * HALF), jnp.bfloat16),
        ],
        compiler_params=pltpu.CompilerParams(vmem_limit_bytes=20 * 1024 * 1024),
        cost_estimate=pl.CostEstimate(
            flops=12_000_000_000, bytes_accessed=12_000_000, transcendentals=1_000_000
        ),
        name="attend",
    )(info, sel_col, bias_col, *[mixed_own] * 3, *[mixed_other] * 3)


def attend_back_kernel(
    pairs,
    info_ref,
    sel_ref,
    prev_own,
    cur_own,
    prev_other,
    cur_other,
    picks_ref,
    probs_ref,
    datt_ref,
    out_own,
    out_other,
    carry,
    dpicks,
):
    i = pl.program_id(0)
    core = info_ref[1]
    outs = (out_own, out_other)

    @pl.when(i == 0)
    def _():
        carry[...] = jnp.zeros_like(carry)

    @pl.when(i < pairs)
    def _():
        side = prev_side()
        datt = (
            datt_ref.at[:, pl.ds(pl.multiple_of(core * HALF, 128), HALF)],
            datt_ref.at[:, pl.ds(pl.multiple_of((1 - core) * HALF, 128), HALF)],
        )
        prev, cur = (prev_own, prev_other), (cur_own, cur_other)
        picks = (picks_ref.at[0], picks_ref.at[1])
        wide_qs, wide_ds, firsts, full_ps, full_ds = [], [], [], [], []
        for b, g in CHAINS:
            here = slice(b * BLOCK, (b + 1) * BLOCK)
            wide_qs.append(spread_heads(load_quad(*cur, here, 0, g)))
            wide_ds.append(spread_heads(load_quad(*datt, here, 0, g)))
            firsts.append(dot_nt(load_keys(prev, cur, picks, 2, b, g), wide_ds[-1]))
        for n, (b, g) in enumerate(CHAINS):
            probs, dprobs = probs_ref[b, g], firsts[n]
            near = jnp.where(side, dprobs[:BLOCK], dprobs[BLOCK : 2 * BLOCK])
            folded = jnp.concatenate([near, dprobs[2 * BLOCK :]], 0)
            inner = jnp.sum(probs * folded, axis=0, keepdims=True)
            dscores = probs * (folded - inner) * HEAD ** (-0.5)
            full_ps.append(unfold(probs[:BLOCK], probs[BLOCK:], side))
            full_ds.append(unfold(dscores[:BLOCK], dscores[BLOCK:], side))
        grads = []
        for n, (b, g) in enumerate(CHAINS):
            dvals = dot_nn(full_ps[n], wide_ds[n])
            dkeys = dot_nn(full_ds[n], wide_qs[n])
            dq = gather_heads(dot_tn(full_ds[n], load_keys(prev, cur, picks, 1, b, g)))
            grads.append((dq, dkeys, dvals))
        for part in range(3):
            lanes = slice(part * HALF, (part + 1) * HALF)
            a = join_quads([grad[part] for grad in grads[: HEADS // 4]])
            b = join_quads([grad[part] for grad in grads[HEADS // 4 :]])
            for s, out_ref in enumerate(outs):
                if part == 0:
                    out_ref[:, lanes] = carry[s, :, lanes].astype(jnp.bfloat16)
                    carry[s, :BLOCK, lanes] = a[s]
                    carry[s, BLOCK:, lanes] = b[s]
                else:
                    out_ref[:BLOCK, lanes] = carry[s, :BLOCK, lanes].astype(jnp.bfloat16)
                    low = carry[s, BLOCK:, lanes] + a[s][:BLOCK]
                    out_ref[BLOCK:, lanes] = low.astype(jnp.bfloat16)
                    carry[s, :BLOCK, lanes] = a[s][BLOCK : 2 * BLOCK] + b[s][:BLOCK]
                    carry[s, BLOCK:, lanes] = b[s][BLOCK : 2 * BLOCK]
                    both = jnp.concatenate([a[s][2 * BLOCK :], b[s][2 * BLOCK :]], 0)
                    rows = pl.ds(pl.multiple_of(i * 2 * TOPK, 2 * TOPK), 2 * TOPK)
                    picked = slice((part - 1) * HALF, part * HALF)
                    dpicks[s, rows, picked] = both.astype(jnp.bfloat16)

    @pl.when(i == pairs)
    def _():
        out_own[...] = carry[0].astype(jnp.bfloat16)
        out_other[...] = carry[1].astype(jnp.bfloat16)

    @pl.when(i > pairs)
    def _():
        ids = lax.broadcasted_iota(jnp.int32, (PAIR, 2 * pairs * TOPK), 0) + (i - pairs - 1) * PAIR
        one_hot = (ids == sel_ref[...]).astype(jnp.float32).astype(jnp.bfloat16)
        for s, out_ref in enumerate(outs):
            out_ref[:, :HALF] = jnp.zeros((PAIR, HALF), jnp.bfloat16)
            out_ref[:, HALF:] = dot_nn(one_hot, dpicks[s]).astype(jnp.bfloat16)


def attend_back(mixed_own, mixed_other, sel_row, info, picks, probs, datt, blocks, pool_rows):
    width = HEADS * HEAD
    pairs = blocks // 2
    total = mixed_own.shape[0]
    halo = total // BLOCK - 1

    def pair(i):
        return jnp.minimum(i, pairs - 1)

    def before_block(i, f):
        return (jnp.where(i == 0, halo, 2 * pair(i) - 1), 0)

    def out_block(i, f):
        return (jnp.where(i == 0, total // PAIR - 1, i - 1), 0)

    mixed_specs = [
        pl.BlockSpec((BLOCK, 3 * HALF), before_block),
        pl.BlockSpec((PAIR, 3 * HALF), lambda i, f: (pair(i), 0)),
    ]
    return pl.pallas_call(
        partial(attend_back_kernel, pairs),
        grid_spec=pltpu.PrefetchScalarGridSpec(
            num_scalar_prefetch=1,
            grid=(pairs + 1 + pool_rows // PAIR,),
            in_specs=[pl.BlockSpec((1, blocks * TOPK), lambda i, f: (0, 0))]
            + mixed_specs * 2
            + [
                pl.BlockSpec((2, 2 * TOPK, 2 * HALF), lambda i, f: (0, pair(i), 0)),
                pl.BlockSpec((2, HEADS // 4, FOLD, QUAD), lambda i, f: (pair(i), 0, 0, 0)),
                pl.BlockSpec((PAIR, width), lambda i, f: (pair(i), 0)),
            ],
            out_specs=[pl.BlockSpec((PAIR, 3 * HALF), out_block)] * 2,
            scratch_shapes=[
                pltpu.VMEM((2, PAIR, 3 * HALF), jnp.float32),
                pltpu.VMEM((2, blocks * TOPK, 2 * HALF), jnp.bfloat16),
            ],
        ),
        out_shape=[jax.ShapeDtypeStruct((total, 3 * HALF), jnp.bfloat16)] * 2,
        compiler_params=pltpu.CompilerParams(vmem_limit_bytes=20 * 1024 * 1024),
        cost_estimate=pl.CostEstimate(
            flops=20_000_000_000, bytes_accessed=18_000_000, transcendentals=0
        ),
        name="attend_back",
    )(info, sel_row, *[mixed_own] * 2, *[mixed_other] * 2, picks, probs, datt)


def standardize(values):
    center = values - jnp.mean(values, axis=-1, keepdims=True)
    spread = jnp.mean(center * center, axis=-1, keepdims=True)
    scale = lax.rsqrt(spread + 1e-05)
    return center * scale, scale


def standardize_back(unit, scale, dunit):
    return scale * (
        dunit
        - jnp.mean(dunit, axis=-1, keepdims=True)
        - unit * jnp.mean(dunit * unit, axis=-1, keepdims=True)
    )


ROWS = 256
CHUNK = 768
GROUP = 48
MIB = 1024 * 1024


def params(mib):
    return pltpu.CompilerParams(vmem_limit_bytes=mib * MIB)


def shape(rows, columns, dtype=jnp.bfloat16):
    return jax.ShapeDtypeStruct((rows, columns), dtype)


def cost(flops, moved):
    return pl.CostEstimate(flops=flops, bytes_accessed=moved, transcendentals=0)


def lanes_at(index, size):
    return pl.ds(pl.multiple_of(index * size, 128), size)


def pool_kernel(tokens_ref, unit_ref, out_ref):
    for b in range(out_ref.shape[0]):
        rows = slice(b * BLOCK, (b + 1) * BLOCK)
        unit, _ = standardize(tokens_ref[rows].astype(jnp.float32))
        unit_ref[rows] = unit
        out_ref[b : b + 1] = jnp.mean(unit, axis=0, keepdims=True)


def pool(tokens):
    rows, width = tokens.shape
    return pl.pallas_call(
        pool_kernel,
        out_shape=[shape(rows, width, jnp.float32), shape(rows // BLOCK, width, jnp.float32)],
        compiler_params=params(24),
        cost_estimate=cost(2_000_000_000, 6_000_000),
        name="pool",
    )(tokens)


def normal_kernel(own_ref, pool_ref, halo_ref, vec_ref, normed_ref, unit_ref):
    gain, bias = vec_ref[0:1], vec_ref[1:2]
    start = 0
    for ref in (own_ref, pool_ref, halo_ref):
        for r in range(0, ref.shape[0], BLOCK):
            unit = ref[r : r + BLOCK].astype(jnp.float32)
            if ref is halo_ref:
                unit, _ = standardize(unit)
                rows = slice(start, start + BLOCK)
                unit_ref[rows] = jnp.zeros(unit.shape, jnp.bfloat16)
                normed_ref[rows] = jnp.zeros(unit.shape, jnp.bfloat16)
                start += BLOCK
            rows = slice(start, start + BLOCK)
            unit_ref[rows] = unit.astype(jnp.bfloat16)
            normed_ref[rows] = (unit * gain + bias).astype(jnp.bfloat16)
            start += BLOCK


def normal(unit_own, unit_pool, halo, vectors):
    width = unit_own.shape[1]
    total = unit_own.shape[0] + unit_pool.shape[0] + 2 * halo.shape[0]
    return pl.pallas_call(
        normal_kernel,
        out_shape=[shape(total, width), shape(total, width)],
        compiler_params=params(24),
        cost_estimate=cost(2_000_000_000, 10_000_000),
        name="normal",
    )(unit_own, unit_pool, halo, vectors)


def mlp_kernel(
    info_ref,
    att_ref,
    tokens_ref,
    dy_ref,
    vec_ref,
    out_own,
    out_other,
    up_own,
    up_other,
    down_ref,
    output_ref,
    dafter_ref,
    datt_ref,
    gd_own,
    gd_other,
    gu_own,
    gu_other,
    sums_ref,
    after_ref,
    n2_ref,
    active_ref,
    dh_ref,
    dn2_ref,
    total_ref,
    grad_ref,
    acc,
    low,
):
    i = pl.program_id(0)
    core = info_ref[1]
    side = out_own.shape[1]
    count, width = n2_ref.shape
    row_steps = count // ROWS
    steps = pl.num_programs(0) - 2 * row_steps
    half = steps // 2
    j = i - row_steps

    @pl.when(i < row_steps)
    def _():
        rows = pl.ds(pl.multiple_of(i * ROWS, ROWS), ROWS)
        after_ref[rows, lanes_at(core, side)] = dot_nn(att_ref[rows], out_own[...])
        after_ref[rows, lanes_at(1 - core, side)] = dot_nn(att_ref[rows], out_other[...])
        after = tokens_ref[...].astype(jnp.float32) + after_ref[rows]
        after_ref[rows] = after
        unit, _ = standardize(after)
        n2_ref[rows] = (unit * vec_ref[2:3] + vec_ref[3:4]).astype(jnp.bfloat16)
        dn2_ref[rows] = jnp.zeros((ROWS, width), jnp.float32)
        total_ref[rows] = after

    @pl.when((j >= 0) & (j < steps))
    def _():
        weight = jnp.where(j < half, up_own[...], up_other[...])
        down = down_ref[...]
        root = (2.0 / 3.141592653589793) ** 0.5

        def first(r):
            rows = slice(r, r + ROWS)
            return rows, dot_nn(n2_ref[rows], weight), dot_nt(dy_ref[rows], down)

        def second(rows, u, dactive):
            square = u * u
            t = jnp.tanh(u * (root + (0.044715 * root) * square))
            upper = 0.5 + 0.5 * t
            active = u * upper
            bend = active * ((1.0 - t) * (root + (3.0 * 0.044715 * root) * square))
            active = active.astype(jnp.bfloat16)
            dh = (dactive * (upper + bend)).astype(jnp.bfloat16)
            active_ref[rows] = active
            dh_ref[rows] = dh
            dn2_ref[rows] += dot_nt(dh, weight)
            total_ref[rows] += dot_nn(active, down)

        waiting = first(0)
        for r in range(ROWS, count, ROWS):
            coming = first(r)
            second(*waiting)
            waiting = coming
        second(*waiting)
        grad_ref[...] = dot_tn(active_ref[...], dy_ref[...]).astype(jnp.bfloat16)
        per = gd_own.shape[1] // side
        for s in range(gd_own.shape[0] // GROUP):
            for g in range(per):
                rows = slice((s * per + g) * GROUP, (s * per + g + 1) * GROUP)
                to = (slice(s * GROUP, (s + 1) * GROUP), slice(g * side, (g + 1) * side))
                gd_own[to] = grad_ref[rows, lanes_at(core, side)]
                gd_other[to] = grad_ref[rows, lanes_at(1 - core, side)]
        grad = dot_tn(n2_ref[...], dh_ref[...]).astype(jnp.bfloat16)

        @pl.when(j < half)
        def _():
            gu_own[:, lanes_at(j, CHUNK)] = grad

        @pl.when(j >= half)
        def _():
            gu_other[:, lanes_at(j - half, CHUNK)] = grad

    @pl.when(j == steps)
    def _():
        sums_ref[...] = jnp.zeros_like(sums_ref)
        acc[...] = jnp.zeros_like(acc)

    @pl.when(j >= steps)
    def _():
        rows = pl.ds(pl.multiple_of((j - steps) * ROWS, ROWS), ROWS)
        output_ref[...] = total_ref[rows].astype(jnp.bfloat16)
        unit, scale = standardize(after_ref[rows])
        dn2 = dn2_ref[rows]
        sums_ref[0:1] += jnp.sum(dn2 * unit, axis=0, keepdims=True)
        sums_ref[1:2] += jnp.sum(dn2, axis=0, keepdims=True)
        dafter = dy_ref[rows].astype(jnp.float32)
        dafter += standardize_back(unit, scale, dn2 * vec_ref[2:3])
        dafter_ref[...] = dafter
        low[...] = dafter.astype(jnp.bfloat16)
        datt = dot_nt(low[:, lanes_at(core, side)], out_own[...])
        datt += dot_nt(low[:, lanes_at(1 - core, side)], out_other[...])
        datt_ref[...] = datt.astype(jnp.bfloat16)
        acc[...] += dot_tn(att_ref[rows], low[...])

    @pl.when(i == pl.num_programs(0) - 1)
    def _():
        at = gu_own.shape[1] - side
        gu_own[:, at:] = acc[:, lanes_at(core, side)].astype(jnp.bfloat16)
        gu_other[:, at:] = acc[:, lanes_at(1 - core, side)].astype(jnp.bfloat16)


def ff_maps(hidden, before):
    steps = hidden // CHUNK
    half = steps // 2
    step = lambda i: jnp.clip(i - before, 0, steps - 1)
    own = lambda i, f: (0, jnp.minimum(step(i), half - 1))
    other = lambda i, f: (0, jnp.maximum(step(i) - half, 0))
    place = lambda i, f: lax.rem(f[1] * half + step(i), steps)
    return steps, own, other, place


def out_columns(own):
    width = own.shape[0]
    half = width // 2
    return pl.BlockSpec((width, half), lambda i, f: (0, own.shape[1] // half - 1))


def mlp(attended, tokens, upstream, vectors, own, other, mat_down, info):
    count, width = tokens.shape
    hidden = mat_down.shape[0]
    row_steps = count // ROWS
    steps, first, second, place = ff_maps(hidden, row_steps)
    whole = lambda i, f: (0, 0)
    once = pl.Buffered(1)
    full = pl.BlockSpec((count, width), whole, pipeline_mode=once)
    grads = pl.BlockSpec(own.shape, whole, pipeline_mode=once)
    low_grads = pl.BlockSpec((CHUNK // 4, 2 * width), lambda i, f: (place(i, f), 0))
    row = pl.BlockSpec((ROWS, width), lambda i, f: (jnp.maximum(i - row_steps - steps, 0), 0))
    f32 = jnp.float32
    return pl.pallas_call(
        mlp_kernel,
        grid_spec=pltpu.PrefetchScalarGridSpec(
            num_scalar_prefetch=1,
            grid=(2 * row_steps + steps,),
            in_specs=[
                full,
                pl.BlockSpec((ROWS, width), lambda i, f: (jnp.minimum(i, row_steps - 1), 0)),
                full,
                pl.BlockSpec(vectors.shape, whole),
                out_columns(own),
                out_columns(other),
                pl.BlockSpec((width, CHUNK), first),
                pl.BlockSpec((width, CHUNK), second),
                pl.BlockSpec((CHUNK, width), lambda i, f: (place(i, f), 0)),
            ],
            out_specs=[
                row,
                row,
                row,
                low_grads,
                low_grads,
                grads,
                grads,
                pl.BlockSpec((8, width), whole),
            ],
            scratch_shapes=[
                pltpu.VMEM((count, width), f32),
                pltpu.VMEM((count, width), jnp.bfloat16),
                pltpu.VMEM((count, CHUNK), jnp.bfloat16),
                pltpu.VMEM((count, CHUNK), jnp.bfloat16),
                pltpu.VMEM((count, width), f32),
                pltpu.VMEM((count, width), f32),
                pltpu.VMEM((CHUNK, width), jnp.bfloat16),
                pltpu.VMEM((width, width), f32),
                pltpu.VMEM((ROWS, width), jnp.bfloat16),
            ],
        ),
        out_shape=[
            shape(count, width),
            shape(count, width, f32),
            shape(count, width),
            shape(hidden // 4, 2 * width),
            shape(hidden // 4, 2 * width),
            shape(*own.shape),
            shape(*own.shape),
            shape(8, width, f32),
        ],
        compiler_params=params(58),
        cost_estimate=cost(40_000_000_000, 30_000_000),
        name="mlp",
    )(info, attended, tokens, upstream, vectors, own, other, own, other, mat_down)


def project_back_kernel(dm_own, dm_other, own_ref, other_ref, unit_ref, dn_ref, sums_ref):
    @pl.when(pl.program_id(0) == 0)
    def _():
        sums_ref[...] = jnp.zeros_like(sums_ref)

    dn = dot_nt(dm_own[...], own_ref[...]) + dot_nt(dm_other[...], other_ref[...])
    dn_ref[...] = dn
    sums_ref[0:1] += jnp.sum(dn * unit_ref[...].astype(jnp.float32), axis=0, keepdims=True)
    sums_ref[1:2] += jnp.sum(dn, axis=0, keepdims=True)


def project_back(dm_own, dm_other, own, other, unit):
    total, width = unit.shape
    rows = total // 4
    row = lambda i: (i, 0)
    once = pl.Buffered(1)
    whole = pl.BlockSpec((width, 3 * HALF), lambda i: (0, 0), pipeline_mode=once)
    return pl.pallas_call(
        project_back_kernel,
        grid=(total // rows,),
        in_specs=[
            pl.BlockSpec((rows, 3 * HALF), row),
            pl.BlockSpec((rows, 3 * HALF), row),
            whole,
            whole,
            pl.BlockSpec((rows, width), row),
        ],
        out_specs=[pl.BlockSpec((rows, width), row), pl.BlockSpec((8, width), lambda i: (0, 0))],
        out_shape=[shape(total, width, jnp.float32), shape(8, width, jnp.float32)],
        compiler_params=params(60),
        cost_estimate=cost(6_000_000_000, 16_000_000),
        name="project_back",
    )(dm_own, dm_other, own, other, unit)


def input_kernel(tokens_ref, dn_ref, dafter_ref, pool_ref, next_ref, vec_ref, out_ref):
    i = pl.program_id(0)
    gain = vec_ref[0:1]
    per = tokens_ref.shape[0] // BLOCK
    last = (i == pl.num_programs(0) - 1).astype(jnp.float32)
    for b in range(per):
        rows = slice(b * BLOCK, (b + 1) * BLOCK)
        unit, scale = standardize(tokens_ref[rows].astype(jnp.float32))
        dn = dn_ref[rows] + pool_ref[pl.ds(i * per + b, 1)] * (1.0 / BLOCK)
        if b == per - 1:
            dn += next_ref[...].astype(jnp.float32) * last
        out_ref[rows] = dafter_ref[rows] + standardize_back(unit, scale, dn * gain)


def input_back(tokens, dnormed, dafter, from_pool, from_next, vectors):
    count, width = tokens.shape
    row = pl.BlockSpec((ROWS, width), lambda i: (i, 0))
    whole = lambda i: (0, 0)
    return pl.pallas_call(
        input_kernel,
        grid=(count // ROWS,),
        in_specs=[
            row,
            row,
            row,
            pl.BlockSpec(from_pool.shape, whole),
            pl.BlockSpec(from_next.shape, whole),
            pl.BlockSpec(vectors.shape, whole),
        ],
        out_specs=row,
        out_shape=shape(count, width, jnp.float32),
        compiler_params=params(60),
        cost_estimate=cost(3_000_000_000, 12_000_000),
        name="input_back",
    )(tokens, dnormed, dafter, from_pool, from_next, vectors)


def shift_seq(value, distance):
    size = lax.axis_size("seq")
    route = [(i - distance, i) for i in range(size) if 0 <= i - distance < size]
    return lax.ppermute(value, "seq", route)


BOTH = ("seq", "batch")


def follows(value, *earlier):
    return lax.optimization_barrier((value, earlier))[0]


def flip_route(size, bit):
    return [(i, i ^ bit) for i in range(size)]


def ring_route(size, stride, steps):
    return [(i, (i + stride * steps) % size) for i in range(size)]


def swap(value, axis, bit):
    return lax.ppermute(value, axis, flip_route(lax.axis_size(axis), bit))


def in_order(bit, own, other):
    return jnp.stack([jnp.where(bit == 0, own, other), jnp.where(bit == 0, other, own)])


def pick(value, index, axis):
    return lax.dynamic_index_in_dim(value, index, axis, keepdims=False)


def add(a, b):
    return (a.astype(jnp.float32) + b.astype(jnp.float32)).astype(jnp.bfloat16)


def place():
    at = lax.axis_index("seq")
    return at // 4, at // 2 % 2, at % 2


def send_line(slab):
    size = lax.axis_size("seq")
    return [lax.ppermute(slab, "seq", ring_route(size, 4, k)) for k in range(1, size // 4)]


def join_line(slab, got):
    z = place()[0]
    stack = jnp.stack([slab] + got)
    layers = stack.shape[0]
    parts = [lax.dynamic_slice_in_dim(stack, (z - k) % layers, 1, 0) for k in range(layers)]
    return jnp.concatenate(parts, 0)


def send_near(line, cut):
    first, second = line[:, :, :cut], line[:, :, cut:]
    return first, second, swap(first, "seq", 1), swap(second, "seq", 2)


def join_near(first, second, first_got, second_got):
    _, y, x = place()
    return in_order(x, first, first_got), in_order(y, second, second_got)


def send_far(first, second):
    return swap(first, "seq", 2), swap(second, "seq", 1)


def join_far(first, second, first_got, second_got):
    _, y, x = place()
    first = jnp.transpose(in_order(y, first, first_got), (2, 0, 1, 3, 4))
    second = jnp.transpose(in_order(x, second, second_got), (2, 1, 0, 3, 4))
    rows = first.shape[3] * lax.axis_size("seq")
    return first.reshape(rows, -1), second.reshape(rows, -1)


def split_grid(full, cut, axis=4):
    grid = full.reshape(lax.axis_size("seq") // 4, 2, 2, -1, full.shape[1])
    return jnp.split(grid, [cut], axis)


def drop_near(first, second):
    _, y, x = place()
    return pick(first, 1 - x, 2), pick(second, 1 - y, 1)


def keep_near(first, second, first_got, second_got):
    _, y, x = place()
    return add(pick(first, x, 2), first_got), add(pick(second, y, 1), second_got)


def drop_far(first, second):
    _, y, x = place()
    return pick(first, 1 - y, 1), pick(second, 1 - x, 1)


def keep_far(first, second, first_got, second_got, axis=2):
    _, y, x = place()
    parts = [add(pick(first, y, 1), first_got), add(pick(second, x, 1), second_got)]
    return jnp.concatenate(parts, axis)


def swap_near(dropped):
    return swap(dropped[0], "seq", 1), swap(dropped[1], "seq", 2)


def swap_far(dropped):
    return swap(dropped[0], "seq", 2), swap(dropped[1], "seq", 1)


def spread_line(line):
    size = lax.axis_size("seq")
    groups = [list(range(n, size, 4)) for n in range(4)]
    return lax.all_to_all(line, "seq", 0, 0, axis_index_groups=groups)


def scatter_line(line):
    z = place()[0]
    size = lax.axis_size("seq")
    layers = size // 4
    got = [
        lax.ppermute(pick(line, (z + k) % layers, 0), "seq", ring_route(size, 4, k))
        for k in range(1, layers)
    ]
    return pick(line, z, 0), got


def sum_line(own, got):
    return sum((g.astype(jnp.float32) for g in got), own.astype(jnp.float32))


def paired():
    return lax.axis_size("batch") == 2 and lax.axis_size("seq") % 4 == 0


def side_index():
    return lax.axis_index("batch") % 2


def halves_of(matrix, groups):
    parts = jnp.split(matrix, 2 * groups, 1)
    return jnp.stack([jnp.concatenate(parts[h::2], 1) for h in range(2)])


def whole_of(halves, groups):
    parts = [jnp.split(half, groups, 1) for half in halves]
    return jnp.concatenate([half[g] for g in range(groups) for half in parts], 1)


def local(
    inputs, selection, cotangent, ln1_gain, ln1_bias, w_qkv, w_out, ln2_gain, ln2_bias, w_up, w_down
):
    bf16, f32 = jnp.bfloat16, jnp.float32
    tokens = inputs[0]
    chosen = selection[0]
    upstream = cotangent[0]
    count, width = tokens.shape
    hidden = w_up.shape[1]
    blocks = count // BLOCK
    size = lax.axis_size("seq")
    pool_rows = blocks * size
    at = lax.axis_index("seq")
    side = side_index()
    fast = paired()

    half_qkv = halves_of(w_qkv, 3)
    half_uo = jnp.concatenate([halves_of(w_up, 1), halves_of(w_out, 1)], 2)
    vectors = jnp.stack([ln1_gain, ln1_bias, ln2_gain, ln2_bias])
    if fast:
        columns = jnp.pad(vectors.T, ((0, 0), (0, 124)))
        columns = jnp.broadcast_to(columns, (2,) + columns.shape)
        bundle = jnp.concatenate([columns, half_qkv, half_uo], 2)
        got = swap(pick(bundle, 1 - side, 0), "batch", 1)
        slab = in_order(side, pick(bundle, side, 0), got).reshape(-1, bundle.shape[2])
        third = width // 3
        per = slab.shape[0] // 3
        unit_own, pooled = pool(tokens)
        pooled = jnp.transpose(pooled.astype(bf16).reshape(per, 3, third), (1, 0, 2))
        pooled = pooled.reshape(-1, third)
        front = third + 128
        edge = 128 + half_qkv.shape[2]
        slab_q = jnp.concatenate([pooled, slab[:, :edge]], 1)
        slab_u = slab[:, edge:]
        line_got = send_line(slab_q)
        halo = shift_seq(follows(tokens[-BLOCK:], slab), 1)
        line_got_u = send_line(slab_u)
        line_q = join_line(slab_q, follows(line_got, halo))
        near = send_near(line_q, 768)
        wide_q = join_near(*near)
        far = send_far(*wide_q)
        line_u = join_line(slab_u, follows(line_got_u, wide_q))
        near_u = send_near(line_u, 1024)
        first, second = join_far(*wide_q, *follows(far, near_u[0], near_u[1]))
        own_qkv = jnp.concatenate([first[:, front:], second], 1)
        other_qkv = swap(own_qkv, "batch", 1)
        unit_pool = jnp.transpose(first[:, :third].reshape(size, 3, per, third), (0, 2, 1, 3))
        unit_pool = unit_pool.reshape(pool_rows, width)
        vectors = first[:, third : third + 4].T.astype(f32)
    else:
        gathered = lax.all_gather(half_qkv, BOTH, axis=1, tiled=True)
        own_qkv, other_qkv = pick(gathered, side, 0), pick(gathered, 1 - side, 0)
        gathered = lax.all_gather(half_uo, BOTH, axis=1, tiled=True)
        own_uo, other_uo = pick(gathered, side, 0), pick(gathered, 1 - side, 0)
        halo = shift_seq(tokens[-BLOCK:], 1)
        unit_own, pooled = pool(tokens)
        unit_pool = lax.all_gather(pooled.astype(bf16), "seq", axis=0, tiled=True)
        vectors = lax.all_gather(vectors, BOTH, axis=1, tiled=True).astype(f32)
    mat_down = lax.all_gather(w_down, BOTH, axis=0, tiled=True)
    vectors = jnp.pad(vectors, ((0, 4), (0, 0)))

    normed, unit = normal(unit_own, unit_pool, halo, vectors)
    mixed_own = dot_nn(normed, own_qkv).astype(bf16)
    mixed_other = dot_nn(normed, other_qkv).astype(bf16)
    if fast:
        wide_u = join_near(*follows(near_u, mixed_other))
        far_u = send_far(*wide_u)
        mixed_own = follows(mixed_own, wide_u)

    block_ids = at * blocks + jnp.arange(blocks, dtype=jnp.int32)
    flat = chosen.reshape(blocks * TOPK)
    far_bias = jnp.where(chosen < block_ids[:, None], 0.0, NEG).reshape(blocks * TOPK, 1)
    info = jnp.stack([(at == 0).astype(jnp.int32), side])
    attended, probs, picks = attend(
        mixed_own, mixed_other, flat[:, None], far_bias, info, blocks, pool_rows
    )
    if fast:
        own_uo = jnp.concatenate(join_far(*wide_u, *follows(far_u, attended)), 1)
        other_uo = swap(own_uo, "batch", 1)
    output, dafter, dattended, down_own, down_other, uo_own, uo_other, sums_two = mlp(
        attended, tokens, upstream, vectors, own_uo, other_uo, mat_down, info
    )
    if fast:
        down_got = swap(down_other, "batch", 1)
        uo_got = swap(uo_other, "batch", 1)
        grid_d = split_grid(add(down_own, down_got), width)
        drop_d = drop_near(*grid_d)
        near_d = swap_near(drop_d)
        grid_u = split_grid(add(uo_own, follows(uo_got, drop_d)), 1024)
        drop_u = drop_near(*grid_u)
        near_u = swap_near(drop_u)
        dattended = follows(dattended, drop_u)

    dmixed_own, dmixed_other = attend_back(
        mixed_own, mixed_other, flat[None, :], info, picks, probs, dattended, blocks, pool_rows
    )
    if fast:
        kept_d = keep_near(*grid_d, *follows(near_d, dmixed_own))
        drop_d = drop_far(*kept_d)
        far_d = swap_far(drop_d)
        dmixed_other = follows(dmixed_other, drop_d)
    grad_other = dot_tn(normed, dmixed_other).astype(bf16)
    if fast:
        grad_got = swap(grad_other, "batch", 1)
        kept_u = keep_near(*grid_u, *follows(near_u, grad_other))
        drop_u = drop_far(*kept_u)
        far_u = swap_far(drop_u)
        dmixed_own = follows(dmixed_own, drop_u)
    grad_own = dot_tn(normed, dmixed_own).astype(bf16)
    if fast:
        grid_q = split_grid(add(grad_own, grad_got), 512)
        drop_q = drop_near(*grid_q)
        near_q = swap_near(drop_q)
        line_d = keep_far(*kept_d, *follows(far_d, drop_q))
        got_d = spread_line(line_d)
        dmixed_own = follows(dmixed_own, line_d)
    dnormed, sums_one = project_back(dmixed_own, dmixed_other, own_qkv, other_qkv, unit)
    vector_grads = jnp.concatenate([sums_one[:2], sums_two[:2]], 0)
    from_next = shift_seq(dnormed[-BLOCK:].astype(bf16), -1)
    dpool = dnormed[count : count + pool_rows].astype(bf16)
    if fast:
        got_d, near_q, far_u = follows((got_d, near_q, far_u), dnormed)
        sum_d = jnp.sum(got_d.astype(f32), axis=0)
        kept_q = keep_near(*grid_q, *near_q)
        drop_q = drop_far(*kept_q)
        far_q = swap_far(drop_q)
        spread = jnp.transpose(vector_grads.reshape(4, size, -1), (1, 0, 2)).reshape(size, 1, -1)
        span = spread.shape[2]
        spread = jnp.pad(spread.astype(bf16), ((0, 0), (0, 7), (0, width - span)))
        send = jnp.concatenate([dpool.reshape(size, blocks, width), spread], 1)
        pool_got = lax.all_to_all(send, "seq", 0, 0)
        line_u = keep_far(*kept_u, *follows(far_u, drop_q))
        line_u, got_u = scatter_line(line_u)
        line_q = keep_far(*kept_q, *follows(far_q, send, line_u))
        line_q, got_q = scatter_line(line_q)
        got = jnp.sum(follows(pool_got, line_q).astype(f32), axis=0)
        from_pool = got[:blocks]
        chip = got[blocks, :span].reshape(4, 2, -1)
    else:
        from_pool = lax.psum_scatter(dpool, "seq", scatter_dimension=0, tiled=True).astype(f32)
        vector_sums = lax.psum_scatter(vector_grads, BOTH, scatter_dimension=1, tiled=True)
    input_grad = input_back(tokens, dnormed, dafter, from_pool, from_next, vectors)
    if fast:
        got_u, got_q = follows((got_u, got_q), input_grad)
        total_d = jnp.stack(jnp.split(sum_d, 2, 1))
        got = swap(pick(follows(total_d, line_q), 1 - side, 0), "batch", 1)
        both_d = in_order(side, pick(total_d, side, 0), got)
        sum_down = jnp.concatenate([whole_of(g, 1) for g in jnp.split(both_d, 2, 2)], 0)
        total_u = sum_line(line_u, got_u).reshape(2, GROUP // 2, -1)
        total_q = sum_line(line_q, got_q).reshape(2, GROUP // 2, -1)
        chip = jnp.pad(jnp.transpose(chip, (1, 2, 0)), ((0, 0), (0, 0), (0, 124)))
        bundle = jnp.concatenate([total_u, total_q, chip], 2)
        mine = pick(bundle, side, 0)
        got = swap(pick(bundle, 1 - side, 0), "batch", 1)
        both = in_order(side, mine, got)
        sum_uo, sum_qkv = both[:, :, : total_u.shape[2]], both[:, :, total_u.shape[2] : -128]
        vector_sums = (mine[:, -128:] + got[:, -128:])[:, :4].T
    else:

        def scatter(own, other):
            full = in_order(side, own, other)
            sums = lax.psum_scatter(full, BOTH, scatter_dimension=1, tiled=True)
            return sums.astype(f32)

        sum_uo = scatter(uo_own, uo_other)
        sum_qkv = scatter(grad_own, grad_other)
        full = jnp.stack([down_own, down_other]).reshape(2, -1, GROUP, 4, width // 2)
        full = jnp.transpose(full, (1, 3, 2, 0, 4)).reshape(hidden, 2, width // 2)
        full = in_order(side, full[:, 0], full[:, 1])
        full = jnp.transpose(full, (1, 0, 2)).reshape(hidden, width)
        sum_down = lax.psum_scatter(full, BOTH, scatter_dimension=0, tiled=True).astype(f32)

    split = hidden // 2
    return (
        output[None],
        input_grad[None],
        vector_sums[0],
        vector_sums[1],
        whole_of(sum_qkv, 3),
        whole_of(sum_uo[:, :, split:], 1),
        vector_sums[2],
        vector_sums[3],
        whole_of(sum_uo[:, :, :split], 1),
        sum_down,
    )


def solution(mesh):
    tokens = P("batch", "seq", None)
    vector = P(BOTH)
    matrix = P(BOTH, None)
    return jax.shard_map(
        local,
        mesh=mesh,
        in_specs=(
            tokens,
            tokens,
            tokens,
            vector,
            vector,
            matrix,
            matrix,
            vector,
            vector,
            matrix,
            matrix,
        ),
        out_specs=(
            tokens,
            tokens,
            vector,
            vector,
            matrix,
            matrix,
            vector,
            vector,
            matrix,
            matrix,
        ),
        check_vma=False,
    )
```

```python
from functools import partial

import jax
import jax.numpy as jnp
from jax import lax
from jax.experimental import pallas as pl
from jax.experimental.pallas import tpu as pltpu
from jax.sharding import PartitionSpec as P

HEADS = 12
HEAD = 64
BLOCK = 64
TOPK = 16
QUAD = 4 * HEAD
FOLD = BLOCK + TOPK
NEG = -1e30


def dot_nn(a, b):
    return lax.dot_general(a, b, (((1,), (0,)), ((), ())), preferred_element_type=jnp.float32)


def dot_nt(a, b):
    return lax.dot_general(a, b, (((1,), (1,)), ((), ())), preferred_element_type=jnp.float32)


def dot_tn(a, b):
    return lax.dot_general(a, b, (((0,), (0,)), ((), ())), preferred_element_type=jnp.float32)


def spread_heads(rows):
    lane = lax.broadcasted_iota(jnp.int32, rows.shape, 1) // HEAD
    zero = jnp.zeros_like(rows)
    return jnp.concatenate([jnp.where(lane == h, rows, zero) for h in range(4)], 0)


def gather_heads(full):
    lane = lax.broadcasted_iota(jnp.int32, (BLOCK, QUAD), 1) // HEAD
    out = full[:BLOCK]
    for h in range(1, 4):
        out = jnp.where(lane == h, full[h * BLOCK : (h + 1) * BLOCK], out)
    return out


def prev_side():
    k = lax.broadcasted_iota(jnp.int32, (BLOCK, QUAD), 0)
    q = lax.broadcasted_iota(jnp.int32, (BLOCK, QUAD), 1) % BLOCK
    return k > q


def unfold(near, far, prev):
    zero = jnp.zeros_like(near)
    both = [jnp.where(prev, near, zero), jnp.where(prev, zero, near), far]
    return jnp.concatenate(both, 0).astype(jnp.bfloat16)


HALF = HEADS // 2 * HEAD
PAIR = 2 * BLOCK


def load_quad(own_ref, other_ref, rows, part, g):
    at = part * HALF
    if g == 0:
        return own_ref[rows, at : at + QUAD]
    if g == 1:
        return jnp.concatenate(
            [own_ref[rows, at + QUAD : at + HALF], other_ref[rows, at : at + HALF - QUAD]], 1
        )
    return other_ref[rows, at + HALF - QUAD : at + HALF]


def join_quads(quads):
    own = jnp.concatenate([quads[0], quads[1][:, : HALF - QUAD]], 1)
    other = jnp.concatenate([quads[1][:, HALF - QUAD :], quads[2]], 1)
    return own, other


CHAINS = [(b, g) for b in range(2) for g in range(HEADS // 4)]


def load_keys(prev, cur, picks, part, b, g):
    every = slice(None)
    before = load_quad(*prev, every, part, g) if b == 0 else load_quad(*cur, slice(0, BLOCK), part, g)
    here = load_quad(*cur, slice(b * BLOCK, (b + 1) * BLOCK), part, g)
    picked = load_quad(*picks, slice(b * TOPK, (b + 1) * TOPK), part - 1, g)
    return jnp.concatenate([before, here, picked], 0)


def attend_kernel(
    info_ref,
    sel_ref,
    bias_ref,
    pool_own,
    prev_own,
    cur_own,
    pool_other,
    prev_other,
    cur_other,
    att_ref,
    probs_ref,
    picks_ref,
):
    c = pl.program_id(0)
    core = info_ref[1]

    @pl.when(c == 0)
    def _():
        pool_rows = pool_own.shape[0]
        ids = lax.broadcasted_iota(jnp.int32, (sel_ref.shape[0], pool_rows), 1)
        one_hot = (ids == sel_ref[...]).astype(jnp.float32).astype(jnp.bfloat16)
        picks_ref[0] = dot_nn(one_hot, pool_own[:, HALF:]).astype(jnp.bfloat16)
        picks_ref[1] = dot_nn(one_hot, pool_other[:, HALF:]).astype(jnp.bfloat16)

    side = prev_side()
    edge = jnp.where((c == 0) & (info_ref[0] == 1), NEG, 0.0)
    rows = pl.ds(pl.multiple_of(c * 2 * TOPK, 2 * TOPK), 2 * TOPK)
    prev, cur = (prev_own, prev_other), (cur_own, cur_other)
    picks = (picks_ref.at[0, rows], picks_ref.at[1, rows])
    scored, values, fulls, outs = [], [], [], []
    for b, g in CHAINS:
        keys = load_keys(prev, cur, picks, 1, b, g)
        values.append(load_keys(prev, cur, picks, 2, b, g))
        wide_q = spread_heads(load_quad(*cur, slice(b * BLOCK, (b + 1) * BLOCK), 0, g))
        scored.append(dot_nt(keys, wide_q))
    for n, (b, g) in enumerate(CHAINS):
        scores = scored[n] * HEAD ** (-0.5)
        before = scores[:BLOCK] + edge if b == 0 else scores[:BLOCK]
        near = jnp.where(side, before, scores[BLOCK : 2 * BLOCK])
        far = scores[2 * BLOCK :] + bias_ref[b * TOPK : (b + 1) * TOPK]
        folded = jnp.concatenate([near, far], 0)
        top = jnp.max(folded, axis=0, keepdims=True)
        weights = jnp.exp(folded - top)
        probs = weights * (1.0 / jnp.sum(weights, axis=0, keepdims=True))
        probs_ref[b, g] = probs
        fulls.append(unfold(probs[:BLOCK], probs[BLOCK:], side))
    for n, (b, g) in enumerate(CHAINS):
        outs.append(gather_heads(dot_tn(fulls[n], values[n])).astype(jnp.bfloat16))
    for b in range(2):
        own, other = join_quads(outs[b * (HEADS // 4) : (b + 1) * (HEADS // 4)])
        here = slice(b * BLOCK, (b + 1) * BLOCK)
        att_ref[here, pl.ds(pl.multiple_of(core * HALF, 128), HALF)] = own
        att_ref[here, pl.ds(pl.multiple_of((1 - core) * HALF, 128), HALF)] = other


def attend(mixed_own, mixed_other, sel_col, bias_col, info, blocks, pool_rows):
    width = HEADS * HEAD
    halo = mixed_own.shape[0] // BLOCK - 1
    mixed_specs = [
        pl.BlockSpec((pool_rows, 3 * HALF), lambda c, f: (blocks * BLOCK // pool_rows, 0)),
        pl.BlockSpec((BLOCK, 3 * HALF), lambda c, f: (jnp.where(c == 0, halo, 2 * c - 1), 0)),
        pl.BlockSpec((PAIR, 3 * HALF), lambda c, f: (c, 0)),
    ]
    return pl.pallas_call(
        attend_kernel,
        grid_spec=pltpu.PrefetchScalarGridSpec(
            num_scalar_prefetch=1,
            grid=(blocks // 2,),
            in_specs=[
                pl.BlockSpec((blocks * TOPK, 1), lambda c, f: (0, 0)),
                pl.BlockSpec((2 * TOPK, 1), lambda c, f: (c, 0)),
            ]
            + mixed_specs * 2,
            out_specs=[
                pl.BlockSpec((PAIR, width), lambda c, f: (c, 0)),
                pl.BlockSpec((2, HEADS // 4, FOLD, QUAD), lambda c, f: (c, 0, 0, 0)),
                pl.BlockSpec((2, blocks * TOPK, 2 * HALF), lambda c, f: (0, 0, 0)),
            ],
        ),
        out_shape=[
            jax.ShapeDtypeStruct((blocks * BLOCK, width), jnp.bfloat16),
            jax.ShapeDtypeStruct((blocks, HEADS // 4, FOLD, QUAD), jnp.float32),
            jax.ShapeDtypeStruct((2, blocks * TOPK, 2 * HALF), jnp.bfloat16),
        ],
        compiler_params=pltpu.CompilerParams(vmem_limit_bytes=20 * 1024 * 1024),
        cost_estimate=pl.CostEstimate(
            flops=12_000_000_000, bytes_accessed=12_000_000, transcendentals=1_000_000
        ),
        name="attend",
    )(info, sel_col, bias_col, *[mixed_own] * 3, *[mixed_other] * 3)


def attend_back_kernel(
    pairs,
    info_ref,
    sel_ref,
    prev_own,
    cur_own,
    prev_other,
    cur_other,
    picks_ref,
    probs_ref,
    datt_ref,
    out_own,
    out_other,
    carry,
    dpicks,
):
    i = pl.program_id(0)
    core = info_ref[1]
    outs = (out_own, out_other)

    @pl.when(i == 0)
    def _():
        carry[...] = jnp.zeros_like(carry)

    @pl.when(i < pairs)
    def _():
        side = prev_side()
        datt = (
            datt_ref.at[:, pl.ds(pl.multiple_of(core * HALF, 128), HALF)],
            datt_ref.at[:, pl.ds(pl.multiple_of((1 - core) * HALF, 128), HALF)],
        )
        prev, cur = (prev_own, prev_other), (cur_own, cur_other)
        picks = (picks_ref.at[0], picks_ref.at[1])
        wide_qs, wide_ds, firsts, full_ps, full_ds = [], [], [], [], []
        for b, g in CHAINS:
            here = slice(b * BLOCK, (b + 1) * BLOCK)
            wide_qs.append(spread_heads(load_quad(*cur, here, 0, g)))
            wide_ds.append(spread_heads(load_quad(*datt, here, 0, g)))
            firsts.append(dot_nt(load_keys(prev, cur, picks, 2, b, g), wide_ds[-1]))
        for n, (b, g) in enumerate(CHAINS):
            probs, dprobs = probs_ref[b, g], firsts[n]
            near = jnp.where(side, dprobs[:BLOCK], dprobs[BLOCK : 2 * BLOCK])
            folded = jnp.concatenate([near, dprobs[2 * BLOCK :]], 0)
            inner = jnp.sum(probs * folded, axis=0, keepdims=True)
            dscores = probs * (folded - inner) * HEAD ** (-0.5)
            full_ps.append(unfold(probs[:BLOCK], probs[BLOCK:], side))
            full_ds.append(unfold(dscores[:BLOCK], dscores[BLOCK:], side))
        grads = []
        for n, (b, g) in enumerate(CHAINS):
            dvals = dot_nn(full_ps[n], wide_ds[n])
            dkeys = dot_nn(full_ds[n], wide_qs[n])
            dq = gather_heads(dot_tn(full_ds[n], load_keys(prev, cur, picks, 1, b, g)))
            grads.append((dq, dkeys, dvals))
        for part in range(3):
            lanes = slice(part * HALF, (part + 1) * HALF)
            a = join_quads([grad[part] for grad in grads[: HEADS // 4]])
            b = join_quads([grad[part] for grad in grads[HEADS // 4 :]])
            for s, out_ref in enumerate(outs):
                if part == 0:
                    out_ref[:, lanes] = carry[s, :, lanes].astype(jnp.bfloat16)
                    carry[s, :BLOCK, lanes] = a[s]
                    carry[s, BLOCK:, lanes] = b[s]
                else:
                    out_ref[:BLOCK, lanes] = carry[s, :BLOCK, lanes].astype(jnp.bfloat16)
                    low = carry[s, BLOCK:, lanes] + a[s][:BLOCK]
                    out_ref[BLOCK:, lanes] = low.astype(jnp.bfloat16)
                    carry[s, :BLOCK, lanes] = a[s][BLOCK : 2 * BLOCK] + b[s][:BLOCK]
                    carry[s, BLOCK:, lanes] = b[s][BLOCK : 2 * BLOCK]
                    both = jnp.concatenate([a[s][2 * BLOCK :], b[s][2 * BLOCK :]], 0)
                    rows = pl.ds(pl.multiple_of(i * 2 * TOPK, 2 * TOPK), 2 * TOPK)
                    picked = slice((part - 1) * HALF, part * HALF)
                    dpicks[s, rows, picked] = both.astype(jnp.bfloat16)

    @pl.when(i == pairs)
    def _():
        out_own[...] = carry[0].astype(jnp.bfloat16)
        out_other[...] = carry[1].astype(jnp.bfloat16)

    @pl.when(i > pairs)
    def _():
        ids = lax.broadcasted_iota(jnp.int32, (PAIR, 2 * pairs * TOPK), 0) + (i - pairs - 1) * PAIR
        one_hot = (ids == sel_ref[...]).astype(jnp.float32).astype(jnp.bfloat16)
        for s, out_ref in enumerate(outs):
            out_ref[:, :HALF] = jnp.zeros((PAIR, HALF), jnp.bfloat16)
            out_ref[:, HALF:] = dot_nn(one_hot, dpicks[s]).astype(jnp.bfloat16)


def attend_back(mixed_own, mixed_other, sel_row, info, picks, probs, datt, blocks, pool_rows):
    width = HEADS * HEAD
    pairs = blocks // 2
    total = mixed_own.shape[0]
    halo = total // BLOCK - 1

    def pair(i):
        return jnp.minimum(i, pairs - 1)

    def before_block(i, f):
        return (jnp.where(i == 0, halo, 2 * pair(i) - 1), 0)

    def out_block(i, f):
        return (jnp.where(i == 0, total // PAIR - 1, i - 1), 0)

    mixed_specs = [
        pl.BlockSpec((BLOCK, 3 * HALF), before_block),
        pl.BlockSpec((PAIR, 3 * HALF), lambda i, f: (pair(i), 0)),
    ]
    return pl.pallas_call(
        partial(attend_back_kernel, pairs),
        grid_spec=pltpu.PrefetchScalarGridSpec(
            num_scalar_prefetch=1,
            grid=(pairs + 1 + pool_rows // PAIR,),
            in_specs=[pl.BlockSpec((1, blocks * TOPK), lambda i, f: (0, 0))]
            + mixed_specs * 2
            + [
                pl.BlockSpec((2, 2 * TOPK, 2 * HALF), lambda i, f: (0, pair(i), 0)),
                pl.BlockSpec((2, HEADS // 4, FOLD, QUAD), lambda i, f: (pair(i), 0, 0, 0)),
                pl.BlockSpec((PAIR, width), lambda i, f: (pair(i), 0)),
            ],
            out_specs=[pl.BlockSpec((PAIR, 3 * HALF), out_block)] * 2,
            scratch_shapes=[
                pltpu.VMEM((2, PAIR, 3 * HALF), jnp.float32),
                pltpu.VMEM((2, blocks * TOPK, 2 * HALF), jnp.bfloat16),
            ],
        ),
        out_shape=[jax.ShapeDtypeStruct((total, 3 * HALF), jnp.bfloat16)] * 2,
        compiler_params=pltpu.CompilerParams(vmem_limit_bytes=20 * 1024 * 1024),
        cost_estimate=pl.CostEstimate(
            flops=20_000_000_000, bytes_accessed=18_000_000, transcendentals=0
        ),
        name="attend_back",
    )(info, sel_row, *[mixed_own] * 2, *[mixed_other] * 2, picks, probs, datt)


def standardize(values):
    center = values - jnp.mean(values, axis=-1, keepdims=True)
    spread = jnp.mean(center * center, axis=-1, keepdims=True)
    scale = lax.rsqrt(spread + 1e-05)
    return center * scale, scale


def standardize_back(unit, scale, dunit):
    return scale * (
        dunit
        - jnp.mean(dunit, axis=-1, keepdims=True)
        - unit * jnp.mean(dunit * unit, axis=-1, keepdims=True)
    )


ROWS = 256
CHUNK = 768
GROUP = 48
MIB = 1024 * 1024


def params(mib):
    return pltpu.CompilerParams(vmem_limit_bytes=mib * MIB)


def shape(rows, columns, dtype=jnp.bfloat16):
    return jax.ShapeDtypeStruct((rows, columns), dtype)


def cost(flops, moved):
    return pl.CostEstimate(flops=flops, bytes_accessed=moved, transcendentals=0)


def lanes_at(index, size):
    return pl.ds(pl.multiple_of(index * size, 128), size)


def pool_kernel(tokens_ref, unit_ref, out_ref):
    for b in range(out_ref.shape[0]):
        rows = slice(b * BLOCK, (b + 1) * BLOCK)
        unit, _ = standardize(tokens_ref[rows].astype(jnp.float32))
        unit_ref[rows] = unit
        out_ref[b : b + 1] = jnp.mean(unit, axis=0, keepdims=True)


def pool(tokens):
    rows, width = tokens.shape
    return pl.pallas_call(
        pool_kernel,
        out_shape=[shape(rows, width, jnp.float32), shape(rows // BLOCK, width, jnp.float32)],
        compiler_params=params(24),
        cost_estimate=cost(2_000_000_000, 6_000_000),
        name="pool",
    )(tokens)


def normal_kernel(own_ref, pool_ref, halo_ref, vec_ref, normed_ref, unit_ref):
    gain, bias = vec_ref[0:1], vec_ref[1:2]
    start = 0
    for ref in (own_ref, pool_ref, halo_ref):
        for r in range(0, ref.shape[0], BLOCK):
            unit = ref[r : r + BLOCK].astype(jnp.float32)
            if ref is halo_ref:
                unit, _ = standardize(unit)
                rows = slice(start, start + BLOCK)
                unit_ref[rows] = jnp.zeros(unit.shape, jnp.bfloat16)
                normed_ref[rows] = jnp.zeros(unit.shape, jnp.bfloat16)
                start += BLOCK
            rows = slice(start, start + BLOCK)
            unit_ref[rows] = unit.astype(jnp.bfloat16)
            normed_ref[rows] = (unit * gain + bias).astype(jnp.bfloat16)
            start += BLOCK


def normal(unit_own, unit_pool, halo, vectors):
    width = unit_own.shape[1]
    total = unit_own.shape[0] + unit_pool.shape[0] + 2 * halo.shape[0]
    return pl.pallas_call(
        normal_kernel,
        out_shape=[shape(total, width), shape(total, width)],
        compiler_params=params(24),
        cost_estimate=cost(2_000_000_000, 10_000_000),
        name="normal",
    )(unit_own, unit_pool, halo, vectors)


def mlp_kernel(
    info_ref,
    att_ref,
    tokens_ref,
    dy_ref,
    vec_ref,
    out_own,
    out_other,
    up_own,
    up_other,
    down_ref,
    output_ref,
    dafter_ref,
    datt_ref,
    gd_own,
    gd_other,
    gu_own,
    gu_other,
    sums_ref,
    after_ref,
    n2_ref,
    active_ref,
    dh_ref,
    dn2_ref,
    total_ref,
    grad_ref,
    acc,
    low,
):
    i = pl.program_id(0)
    core = info_ref[1]
    side = out_own.shape[1]
    count, width = n2_ref.shape
    row_steps = count // ROWS
    steps = pl.num_programs(0) - 2 * row_steps
    half = steps // 2
    j = i - row_steps

    @pl.when(i < row_steps)
    def _():
        rows = pl.ds(pl.multiple_of(i * ROWS, ROWS), ROWS)
        after_ref[rows, lanes_at(core, side)] = dot_nn(att_ref[rows], out_own[...])
        after_ref[rows, lanes_at(1 - core, side)] = dot_nn(att_ref[rows], out_other[...])
        after = tokens_ref[...].astype(jnp.float32) + after_ref[rows]
        after_ref[rows] = after
        unit, _ = standardize(after)
        n2_ref[rows] = (unit * vec_ref[2:3] + vec_ref[3:4]).astype(jnp.bfloat16)
        dn2_ref[rows] = jnp.zeros((ROWS, width), jnp.float32)
        total_ref[rows] = after

    @pl.when((j >= 0) & (j < steps))
    def _():
        weight = jnp.where(j < half, up_own[...], up_other[...])
        down = down_ref[...]
        root = (2.0 / 3.141592653589793) ** 0.5

        def first(r):
            rows = slice(r, r + ROWS)
            return rows, dot_nn(n2_ref[rows], weight), dot_nt(dy_ref[rows], down)

        def second(rows, u, dactive):
            square = u * u
            t = jnp.tanh(u * (root + (0.044715 * root) * square))
            upper = 0.5 + 0.5 * t
            active = u * upper
            bend = active * ((1.0 - t) * (root + (3.0 * 0.044715 * root) * square))
            active = active.astype(jnp.bfloat16)
            dh = (dactive * (upper + bend)).astype(jnp.bfloat16)
            active_ref[rows] = active
            dh_ref[rows] = dh
            dn2_ref[rows] += dot_nt(dh, weight)
            total_ref[rows] += dot_nn(active, down)

        waiting = first(0)
        for r in range(ROWS, count, ROWS):
            coming = first(r)
            second(*waiting)
            waiting = coming
        second(*waiting)
        grad_ref[...] = dot_tn(active_ref[...], dy_ref[...]).astype(jnp.bfloat16)
        per = gd_own.shape[1] // side
        for s in range(gd_own.shape[0] // GROUP):
            for g in range(per):
                rows = slice((s * per + g) * GROUP, (s * per + g + 1) * GROUP)
                to = (slice(s * GROUP, (s + 1) * GROUP), slice(g * side, (g + 1) * side))
                gd_own[to] = grad_ref[rows, lanes_at(core, side)]
                gd_other[to] = grad_ref[rows, lanes_at(1 - core, side)]
        grad = dot_tn(n2_ref[...], dh_ref[...]).astype(jnp.bfloat16)

        @pl.when(j < half)
        def _():
            gu_own[:, lanes_at(j, CHUNK)] = grad

        @pl.when(j >= half)
        def _():
            gu_other[:, lanes_at(j - half, CHUNK)] = grad

    @pl.when(j == steps)
    def _():
        sums_ref[...] = jnp.zeros_like(sums_ref)
        acc[...] = jnp.zeros_like(acc)

    @pl.when(j >= steps)
    def _():
        rows = pl.ds(pl.multiple_of((j - steps) * ROWS, ROWS), ROWS)
        output_ref[...] = total_ref[rows].astype(jnp.bfloat16)
        unit, scale = standardize(after_ref[rows])
        dn2 = dn2_ref[rows]
        sums_ref[0:1] += jnp.sum(dn2 * unit, axis=0, keepdims=True)
        sums_ref[1:2] += jnp.sum(dn2, axis=0, keepdims=True)
        dafter = dy_ref[rows].astype(jnp.float32)
        dafter += standardize_back(unit, scale, dn2 * vec_ref[2:3])
        dafter_ref[...] = dafter
        low[...] = dafter.astype(jnp.bfloat16)
        datt = dot_nt(low[:, lanes_at(core, side)], out_own[...])
        datt += dot_nt(low[:, lanes_at(1 - core, side)], out_other[...])
        datt_ref[...] = datt.astype(jnp.bfloat16)
        acc[...] += dot_tn(att_ref[rows], low[...])

    @pl.when(i == pl.num_programs(0) - 1)
    def _():
        at = gu_own.shape[1] - side
        gu_own[:, at:] = acc[:, lanes_at(core, side)].astype(jnp.bfloat16)
        gu_other[:, at:] = acc[:, lanes_at(1 - core, side)].astype(jnp.bfloat16)


def ff_maps(hidden, before):
    steps = hidden // CHUNK
    half = steps // 2
    step = lambda i: jnp.clip(i - before, 0, steps - 1)
    own = lambda i, f: (0, jnp.minimum(step(i), half - 1))
    other = lambda i, f: (0, jnp.maximum(step(i) - half, 0))
    place = lambda i, f: lax.rem(f[1] * half + step(i), steps)
    return steps, own, other, place


def out_columns(own):
    width = own.shape[0]
    half = width // 2
    return pl.BlockSpec((width, half), lambda i, f: (0, own.shape[1] // half - 1))


def mlp(attended, tokens, upstream, vectors, own, other, mat_down, info):
    count, width = tokens.shape
    hidden = mat_down.shape[0]
    row_steps = count // ROWS
    steps, first, second, place = ff_maps(hidden, row_steps)
    whole = lambda i, f: (0, 0)
    once = pl.Buffered(1)
    full = pl.BlockSpec((count, width), whole, pipeline_mode=once)
    grads = pl.BlockSpec(own.shape, whole, pipeline_mode=once)
    low_grads = pl.BlockSpec((CHUNK // 4, 2 * width), lambda i, f: (place(i, f), 0))
    row = pl.BlockSpec((ROWS, width), lambda i, f: (jnp.maximum(i - row_steps - steps, 0), 0))
    f32 = jnp.float32
    return pl.pallas_call(
        mlp_kernel,
        grid_spec=pltpu.PrefetchScalarGridSpec(
            num_scalar_prefetch=1,
            grid=(2 * row_steps + steps,),
            in_specs=[
                full,
                pl.BlockSpec((ROWS, width), lambda i, f: (jnp.minimum(i, row_steps - 1), 0)),
                full,
                pl.BlockSpec(vectors.shape, whole),
                out_columns(own),
                out_columns(other),
                pl.BlockSpec((width, CHUNK), first),
                pl.BlockSpec((width, CHUNK), second),
                pl.BlockSpec((CHUNK, width), lambda i, f: (place(i, f), 0)),
            ],
            out_specs=[
                row,
                row,
                row,
                low_grads,
                low_grads,
                grads,
                grads,
                pl.BlockSpec((8, width), whole),
            ],
            scratch_shapes=[
                pltpu.VMEM((count, width), f32),
                pltpu.VMEM((count, width), jnp.bfloat16),
                pltpu.VMEM((count, CHUNK), jnp.bfloat16),
                pltpu.VMEM((count, CHUNK), jnp.bfloat16),
                pltpu.VMEM((count, width), f32),
                pltpu.VMEM((count, width), f32),
                pltpu.VMEM((CHUNK, width), jnp.bfloat16),
                pltpu.VMEM((width, width), f32),
                pltpu.VMEM((ROWS, width), jnp.bfloat16),
            ],
        ),
        out_shape=[
            shape(count, width),
            shape(count, width, f32),
            shape(count, width),
            shape(hidden // 4, 2 * width),
            shape(hidden // 4, 2 * width),
            shape(*own.shape),
            shape(*own.shape),
            shape(8, width, f32),
        ],
        compiler_params=params(58),
        cost_estimate=cost(40_000_000_000, 30_000_000),
        name="mlp",
    )(info, attended, tokens, upstream, vectors, own, other, own, other, mat_down)


def project_back_kernel(dm_own, dm_other, own_ref, other_ref, unit_ref, dn_ref, sums_ref):
    @pl.when(pl.program_id(0) == 0)
    def _():
        sums_ref[...] = jnp.zeros_like(sums_ref)

    dn = dot_nt(dm_own[...], own_ref[...]) + dot_nt(dm_other[...], other_ref[...])
    dn_ref[...] = dn.astype(jnp.bfloat16)
    sums_ref[0:1] += jnp.sum(dn * unit_ref[...].astype(jnp.float32), axis=0, keepdims=True)
    sums_ref[1:2] += jnp.sum(dn, axis=0, keepdims=True)


def project_back(dm_own, dm_other, own, other, unit):
    total, width = unit.shape
    rows = total // 4
    row = lambda i: (i, 0)
    once = pl.Buffered(1)
    whole = pl.BlockSpec((width, 3 * HALF), lambda i: (0, 0), pipeline_mode=once)
    return pl.pallas_call(
        project_back_kernel,
        grid=(total // rows,),
        in_specs=[
            pl.BlockSpec((rows, 3 * HALF), row),
            pl.BlockSpec((rows, 3 * HALF), row),
            whole,
            whole,
            pl.BlockSpec((rows, width), row),
        ],
        out_specs=[pl.BlockSpec((rows, width), row), pl.BlockSpec((8, width), lambda i: (0, 0))],
        out_shape=[shape(total, width), shape(8, width, jnp.float32)],
        compiler_params=params(60),
        cost_estimate=cost(6_000_000_000, 16_000_000),
        name="project_back",
    )(dm_own, dm_other, own, other, unit)


def input_kernel(tokens_ref, dn_ref, dafter_ref, pool_ref, next_ref, vec_ref, out_ref):
    i = pl.program_id(0)
    gain = vec_ref[0:1]
    per = tokens_ref.shape[0] // BLOCK
    last = (i == pl.num_programs(0) - 1).astype(jnp.float32)
    for b in range(per):
        rows = slice(b * BLOCK, (b + 1) * BLOCK)
        unit, scale = standardize(tokens_ref[rows].astype(jnp.float32))
        dn = dn_ref[rows].astype(jnp.float32) + pool_ref[pl.ds(i * per + b, 1)] * (1.0 / BLOCK)
        if b == per - 1:
            dn += next_ref[...].astype(jnp.float32) * last
        out_ref[rows] = dafter_ref[rows] + standardize_back(unit, scale, dn * gain)


def input_back(tokens, dnormed, dafter, from_pool, from_next, vectors):
    count, width = tokens.shape
    row = pl.BlockSpec((ROWS, width), lambda i: (i, 0))
    whole = lambda i: (0, 0)
    return pl.pallas_call(
        input_kernel,
        grid=(count // ROWS,),
        in_specs=[
            row,
            row,
            row,
            pl.BlockSpec(from_pool.shape, whole),
            pl.BlockSpec(from_next.shape, whole),
            pl.BlockSpec(vectors.shape, whole),
        ],
        out_specs=row,
        out_shape=shape(count, width, jnp.float32),
        compiler_params=params(60),
        cost_estimate=cost(3_000_000_000, 12_000_000),
        name="input_back",
    )(tokens, dnormed, dafter, from_pool, from_next, vectors)


def shift_seq(value, distance):
    size = lax.axis_size("seq")
    route = [(i - distance, i) for i in range(size) if 0 <= i - distance < size]
    return lax.ppermute(value, "seq", route)


BOTH = ("seq", "batch")


def follows(value, *earlier):
    return lax.optimization_barrier((value, earlier))[0]


def flip_route(size, bit):
    return [(i, i ^ bit) for i in range(size)]


def ring_route(size, stride, steps):
    return [(i, (i + stride * steps) % size) for i in range(size)]


def swap(value, axis, bit):
    return lax.ppermute(value, axis, flip_route(lax.axis_size(axis), bit))


def in_order(bit, own, other):
    return jnp.stack([jnp.where(bit == 0, own, other), jnp.where(bit == 0, other, own)])


def pick(value, index, axis):
    return lax.dynamic_index_in_dim(value, index, axis, keepdims=False)


def add(a, b):
    return (a.astype(jnp.float32) + b.astype(jnp.float32)).astype(jnp.bfloat16)


def place():
    at = lax.axis_index("seq")
    return at // 4, at // 2 % 2, at % 2


def send_line(slab):
    size = lax.axis_size("seq")
    return [lax.ppermute(slab, "seq", ring_route(size, 4, k)) for k in range(1, size // 4)]


def join_line(slab, got):
    z = place()[0]
    stack = jnp.stack([slab] + got)
    layers = stack.shape[0]
    parts = [lax.dynamic_slice_in_dim(stack, (z - k) % layers, 1, 0) for k in range(layers)]
    return jnp.concatenate(parts, 0)


def send_near(line, cut):
    first, second = line[:, :, :cut], line[:, :, cut:]
    return first, second, swap(first, "seq", 1), swap(second, "seq", 2)


def join_near(first, second, first_got, second_got):
    _, y, x = place()
    return in_order(x, first, first_got), in_order(y, second, second_got)


def send_far(first, second):
    return swap(first, "seq", 2), swap(second, "seq", 1)


def join_far(first, second, first_got, second_got):
    _, y, x = place()
    first = jnp.transpose(in_order(y, first, first_got), (2, 0, 1, 3, 4))
    second = jnp.transpose(in_order(x, second, second_got), (2, 1, 0, 3, 4))
    rows = first.shape[3] * lax.axis_size("seq")
    return first.reshape(rows, -1), second.reshape(rows, -1)


def split_grid(full, cut, axis=4):
    grid = full.reshape(lax.axis_size("seq") // 4, 2, 2, -1, full.shape[1])
    return jnp.split(grid, [cut], axis)


def drop_near(first, second):
    _, y, x = place()
    return pick(first, 1 - x, 2), pick(second, 1 - y, 1)


def keep_near(first, second, first_got, second_got):
    _, y, x = place()
    return add(pick(first, x, 2), first_got), add(pick(second, y, 1), second_got)


def drop_far(first, second):
    _, y, x = place()
    return pick(first, 1 - y, 1), pick(second, 1 - x, 1)


def keep_far(first, second, first_got, second_got, axis=2):
    _, y, x = place()
    parts = [add(pick(first, y, 1), first_got), add(pick(second, x, 1), second_got)]
    return jnp.concatenate(parts, axis)


def swap_near(dropped):
    return swap(dropped[0], "seq", 1), swap(dropped[1], "seq", 2)


def swap_far(dropped):
    return swap(dropped[0], "seq", 2), swap(dropped[1], "seq", 1)


def spread_line(line):
    size = lax.axis_size("seq")
    groups = [list(range(n, size, 4)) for n in range(4)]
    return lax.all_to_all(line, "seq", 0, 0, axis_index_groups=groups)


def scatter_line(line):
    z = place()[0]
    size = lax.axis_size("seq")
    layers = size // 4
    got = [
        lax.ppermute(pick(line, (z + k) % layers, 0), "seq", ring_route(size, 4, k))
        for k in range(1, layers)
    ]
    return pick(line, z, 0), got


def sum_line(own, got):
    return sum((g.astype(jnp.float32) for g in got), own.astype(jnp.float32))


def paired():
    return lax.axis_size("batch") == 2 and lax.axis_size("seq") % 4 == 0


def side_index():
    return lax.axis_index("batch") % 2


def halves_of(matrix, groups):
    parts = jnp.split(matrix, 2 * groups, 1)
    return jnp.stack([jnp.concatenate(parts[h::2], 1) for h in range(2)])


def whole_of(halves, groups):
    parts = [jnp.split(half, groups, 1) for half in halves]
    return jnp.concatenate([half[g] for g in range(groups) for half in parts], 1)


def local(
    inputs, selection, cotangent, ln1_gain, ln1_bias, w_qkv, w_out, ln2_gain, ln2_bias, w_up, w_down
):
    bf16, f32 = jnp.bfloat16, jnp.float32
    tokens = inputs[0]
    chosen = selection[0]
    upstream = cotangent[0]
    count, width = tokens.shape
    hidden = w_up.shape[1]
    blocks = count // BLOCK
    size = lax.axis_size("seq")
    pool_rows = blocks * size
    at = lax.axis_index("seq")
    side = side_index()
    fast = paired()

    half_qkv = halves_of(w_qkv, 3)
    half_uo = jnp.concatenate([halves_of(w_up, 1), halves_of(w_out, 1)], 2)
    vectors = jnp.stack([ln1_gain, ln1_bias, ln2_gain, ln2_bias])
    if fast:
        columns = jnp.pad(vectors.T, ((0, 0), (0, 124)))
        columns = jnp.broadcast_to(columns, (2,) + columns.shape)
        bundle = jnp.concatenate([columns, half_qkv, half_uo], 2)
        got = swap(pick(bundle, 1 - side, 0), "batch", 1)
        slab = in_order(side, pick(bundle, side, 0), got).reshape(-1, bundle.shape[2])
        third = width // 3
        per = slab.shape[0] // 3
        unit_own, pooled = pool(tokens)
        pooled = jnp.transpose(pooled.astype(bf16).reshape(per, 3, third), (1, 0, 2))
        pooled = pooled.reshape(-1, third)
        front = third + 128
        edge = 128 + half_qkv.shape[2]
        slab_q = jnp.concatenate([pooled, slab[:, :edge]], 1)
        slab_u = slab[:, edge:]
        line_got = send_line(slab_q)
        halo = shift_seq(follows(tokens[-BLOCK:], slab), 1)
        line_got_u = send_line(slab_u)
        line_q = join_line(slab_q, follows(line_got, halo))
        near = send_near(line_q, 768)
        wide_q = join_near(*near)
        far = send_far(*wide_q)
        line_u = join_line(slab_u, follows(line_got_u, wide_q))
        near_u = send_near(line_u, 1024)
        first, second = join_far(*wide_q, *follows(far, near_u[0], near_u[1]))
        own_qkv = jnp.concatenate([first[:, front:], second], 1)
        other_qkv = swap(own_qkv, "batch", 1)
        unit_pool = jnp.transpose(first[:, :third].reshape(size, 3, per, third), (0, 2, 1, 3))
        unit_pool = unit_pool.reshape(pool_rows, width)
        vectors = first[:, third : third + 4].T.astype(f32)
    else:
        gathered = lax.all_gather(half_qkv, BOTH, axis=1, tiled=True)
        own_qkv, other_qkv = pick(gathered, side, 0), pick(gathered, 1 - side, 0)
        gathered = lax.all_gather(half_uo, BOTH, axis=1, tiled=True)
        own_uo, other_uo = pick(gathered, side, 0), pick(gathered, 1 - side, 0)
        halo = shift_seq(tokens[-BLOCK:], 1)
        unit_own, pooled = pool(tokens)
        unit_pool = lax.all_gather(pooled.astype(bf16), "seq", axis=0, tiled=True)
        vectors = lax.all_gather(vectors, BOTH, axis=1, tiled=True).astype(f32)
    mat_down = lax.all_gather(w_down, BOTH, axis=0, tiled=True)
    vectors = jnp.pad(vectors, ((0, 4), (0, 0)))

    normed, unit = normal(unit_own, unit_pool, halo, vectors)
    mixed_own = dot_nn(normed, own_qkv).astype(bf16)
    mixed_other = dot_nn(normed, other_qkv).astype(bf16)
    if fast:
        wide_u = join_near(*follows(near_u, mixed_other))
        far_u = send_far(*wide_u)
        mixed_own = follows(mixed_own, wide_u)

    block_ids = at * blocks + jnp.arange(blocks, dtype=jnp.int32)
    flat = chosen.reshape(blocks * TOPK)
    far_bias = jnp.where(chosen < block_ids[:, None], 0.0, NEG).reshape(blocks * TOPK, 1)
    info = jnp.stack([(at == 0).astype(jnp.int32), side])
    attended, probs, picks = attend(
        mixed_own, mixed_other, flat[:, None], far_bias, info, blocks, pool_rows
    )
    if fast:
        own_uo = jnp.concatenate(join_far(*wide_u, *follows(far_u, attended)), 1)
        other_uo = swap(own_uo, "batch", 1)
    output, dafter, dattended, down_own, down_other, uo_own, uo_other, sums_two = mlp(
        attended, tokens, upstream, vectors, own_uo, other_uo, mat_down, info
    )
    if fast:
        down_got = swap(down_other, "batch", 1)
        uo_got = swap(uo_other, "batch", 1)
        grid_d = split_grid(add(down_own, down_got), width)
        drop_d = drop_near(*grid_d)
        near_d = swap_near(drop_d)
        grid_u = split_grid(add(uo_own, follows(uo_got, drop_d)), 1024)
        drop_u = drop_near(*grid_u)
        near_u = swap_near(drop_u)
        dattended = follows(dattended, drop_u)

    dmixed_own, dmixed_other = attend_back(
        mixed_own, mixed_other, flat[None, :], info, picks, probs, dattended, blocks, pool_rows
    )
    if fast:
        kept_d = keep_near(*grid_d, *follows(near_d, dmixed_own))
        drop_d = drop_far(*kept_d)
        far_d = swap_far(drop_d)
        dmixed_other = follows(dmixed_other, drop_d)
    grad_other = dot_tn(normed, dmixed_other).astype(bf16)
    if fast:
        grad_got = swap(grad_other, "batch", 1)
        kept_u = keep_near(*grid_u, *follows(near_u, grad_other))
        drop_u = drop_far(*kept_u)
        far_u = swap_far(drop_u)
        dmixed_own = follows(dmixed_own, drop_u)
    grad_own = dot_tn(normed, dmixed_own).astype(bf16)
    if fast:
        grid_q = split_grid(add(grad_own, grad_got), 512)
        drop_q = drop_near(*grid_q)
        near_q = swap_near(drop_q)
        line_d = keep_far(*kept_d, *follows(far_d, drop_q))
        got_d = spread_line(line_d)
        dmixed_own = follows(dmixed_own, line_d)
    dnormed, sums_one = project_back(dmixed_own, dmixed_other, own_qkv, other_qkv, unit)
    vector_grads = jnp.concatenate([sums_one[:2], sums_two[:2]], 0)
    from_next = shift_seq(dnormed[-BLOCK:], -1)
    dpool = dnormed[count : count + pool_rows]
    if fast:
        got_d, near_q, far_u = follows((got_d, near_q, far_u), dnormed)
        sum_d = jnp.sum(got_d.astype(f32), axis=0)
        kept_q = keep_near(*grid_q, *near_q)
        drop_q = drop_far(*kept_q)
        far_q = swap_far(drop_q)
        spread = jnp.transpose(vector_grads.reshape(4, size, -1), (1, 0, 2)).reshape(size, 1, -1)
        span = spread.shape[2]
        spread = jnp.pad(spread.astype(bf16), ((0, 0), (0, 7), (0, width - span)))
        send = jnp.concatenate([dpool.reshape(size, blocks, width), spread], 1)
        pool_got = lax.all_to_all(send, "seq", 0, 0)
        line_u = keep_far(*kept_u, *follows(far_u, drop_q))
        line_u, got_u = scatter_line(line_u)
        line_q = keep_far(*kept_q, *follows(far_q, send, line_u))
        line_q, got_q = scatter_line(line_q)
        got = jnp.sum(follows(pool_got, line_q).astype(f32), axis=0)
        from_pool = got[:blocks]
        chip = got[blocks, :span].reshape(4, 2, -1)
    else:
        from_pool = lax.psum_scatter(dpool, "seq", scatter_dimension=0, tiled=True).astype(f32)
        vector_sums = lax.psum_scatter(vector_grads, BOTH, scatter_dimension=1, tiled=True)
    input_grad = input_back(tokens, dnormed, dafter, from_pool, from_next, vectors)
    if fast:
        got_u, got_q = follows((got_u, got_q), input_grad)
        total_d = jnp.stack(jnp.split(sum_d, 2, 1))
        got = swap(pick(follows(total_d, line_q), 1 - side, 0), "batch", 1)
        both_d = in_order(side, pick(total_d, side, 0), got)
        sum_down = jnp.concatenate([whole_of(g, 1) for g in jnp.split(both_d, 2, 2)], 0)
        total_u = sum_line(line_u, got_u).reshape(2, GROUP // 2, -1)
        total_q = sum_line(line_q, got_q).reshape(2, GROUP // 2, -1)
        chip = jnp.pad(jnp.transpose(chip, (1, 2, 0)), ((0, 0), (0, 0), (0, 124)))
        bundle = jnp.concatenate([total_u, total_q, chip], 2)
        mine = pick(bundle, side, 0)
        got = swap(pick(bundle, 1 - side, 0), "batch", 1)
        both = in_order(side, mine, got)
        sum_uo, sum_qkv = both[:, :, : total_u.shape[2]], both[:, :, total_u.shape[2] : -128]
        vector_sums = (mine[:, -128:] + got[:, -128:])[:, :4].T
    else:

        def scatter(own, other):
            full = in_order(side, own, other)
            sums = lax.psum_scatter(full, BOTH, scatter_dimension=1, tiled=True)
            return sums.astype(f32)

        sum_uo = scatter(uo_own, uo_other)
        sum_qkv = scatter(grad_own, grad_other)
        full = jnp.stack([down_own, down_other]).reshape(2, -1, GROUP, 4, width // 2)
        full = jnp.transpose(full, (1, 3, 2, 0, 4)).reshape(hidden, 2, width // 2)
        full = in_order(side, full[:, 0], full[:, 1])
        full = jnp.transpose(full, (1, 0, 2)).reshape(hidden, width)
        sum_down = lax.psum_scatter(full, BOTH, scatter_dimension=0, tiled=True).astype(f32)

    split = hidden // 2
    return (
        output[None],
        input_grad[None],
        vector_sums[0],
        vector_sums[1],
        whole_of(sum_qkv, 3),
        whole_of(sum_uo[:, :, split:], 1),
        vector_sums[2],
        vector_sums[3],
        whole_of(sum_uo[:, :, :split], 1),
        sum_down,
    )


def solution(mesh):
    tokens = P("batch", "seq", None)
    vector = P(BOTH)
    matrix = P(BOTH, None)
    return jax.shard_map(
        local,
        mesh=mesh,
        in_specs=(
            tokens,
            tokens,
            tokens,
            vector,
            vector,
            matrix,
            matrix,
            vector,
            vector,
            matrix,
            matrix,
        ),
        out_specs=(
            tokens,
            tokens,
            vector,
            vector,
            matrix,
            matrix,
            vector,
            vector,
            matrix,
            matrix,
        ),
        check_vma=False,
    )
```

```python
from functools import partial

import jax
import jax.numpy as jnp
from jax import lax
from jax.experimental import pallas as pl
from jax.experimental.pallas import tpu as pltpu
from jax.sharding import PartitionSpec as P

HEADS = 12
HEAD = 64
BLOCK = 64
TOPK = 16
QUAD = 4 * HEAD
FOLD = BLOCK + TOPK
NEG = -1e30


def dot_nn(a, b):
    return lax.dot_general(a, b, (((1,), (0,)), ((), ())), preferred_element_type=jnp.float32)


def dot_nt(a, b):
    return lax.dot_general(a, b, (((1,), (1,)), ((), ())), preferred_element_type=jnp.float32)


def dot_tn(a, b):
    return lax.dot_general(a, b, (((0,), (0,)), ((), ())), preferred_element_type=jnp.float32)


def spread_heads(rows):
    lane = lax.broadcasted_iota(jnp.int32, rows.shape, 1) // HEAD
    zero = jnp.zeros_like(rows)
    return jnp.concatenate([jnp.where(lane == h, rows, zero) for h in range(4)], 0)


def gather_heads(full):
    lane = lax.broadcasted_iota(jnp.int32, (BLOCK, QUAD), 1) // HEAD
    out = full[:BLOCK]
    for h in range(1, 4):
        out = jnp.where(lane == h, full[h * BLOCK : (h + 1) * BLOCK], out)
    return out


def prev_side():
    k = lax.broadcasted_iota(jnp.int32, (BLOCK, QUAD), 0)
    q = lax.broadcasted_iota(jnp.int32, (BLOCK, QUAD), 1) % BLOCK
    return k > q


def unfold(near, far, prev):
    zero = jnp.zeros_like(near)
    both = [jnp.where(prev, near, zero), jnp.where(prev, zero, near), far]
    return jnp.concatenate(both, 0).astype(jnp.bfloat16)


HALF = HEADS // 2 * HEAD
PAIR = 2 * BLOCK


def load_quad(own_ref, other_ref, rows, part, g):
    at = part * HALF
    if g == 0:
        return own_ref[rows, at : at + QUAD]
    if g == 1:
        return jnp.concatenate(
            [own_ref[rows, at + QUAD : at + HALF], other_ref[rows, at : at + HALF - QUAD]], 1
        )
    return other_ref[rows, at + HALF - QUAD : at + HALF]


def join_quads(quads):
    own = jnp.concatenate([quads[0], quads[1][:, : HALF - QUAD]], 1)
    other = jnp.concatenate([quads[1][:, HALF - QUAD :], quads[2]], 1)
    return own, other


CHAINS = [(b, g) for b in range(2) for g in range(HEADS // 4)]


def load_keys(prev, cur, picks, part, b, g):
    every = slice(None)
    before = load_quad(*prev, every, part, g) if b == 0 else load_quad(*cur, slice(0, BLOCK), part, g)
    here = load_quad(*cur, slice(b * BLOCK, (b + 1) * BLOCK), part, g)
    picked = load_quad(*picks, slice(b * TOPK, (b + 1) * TOPK), part - 1, g)
    return jnp.concatenate([before, here, picked], 0)


def attend_kernel(
    info_ref,
    sel_ref,
    bias_ref,
    pool_own,
    prev_own,
    cur_own,
    pool_other,
    prev_other,
    cur_other,
    att_ref,
    probs_ref,
    picks_ref,
):
    c = pl.program_id(0)
    core = info_ref[1]

    @pl.when(c == 0)
    def _():
        pool_rows = pool_own.shape[0]
        ids = lax.broadcasted_iota(jnp.int32, (sel_ref.shape[0], pool_rows), 1)
        one_hot = (ids == sel_ref[...]).astype(jnp.float32).astype(jnp.bfloat16)
        picks_ref[0] = dot_nn(one_hot, pool_own[:, HALF:]).astype(jnp.bfloat16)
        picks_ref[1] = dot_nn(one_hot, pool_other[:, HALF:]).astype(jnp.bfloat16)

    side = prev_side()
    edge = jnp.where((c == 0) & (info_ref[0] == 1), NEG, 0.0)
    rows = pl.ds(pl.multiple_of(c * 2 * TOPK, 2 * TOPK), 2 * TOPK)
    prev, cur = (prev_own, prev_other), (cur_own, cur_other)
    picks = (picks_ref.at[0, rows], picks_ref.at[1, rows])
    scored, values, fulls, outs = [], [], [], []
    for b, g in CHAINS:
        keys = load_keys(prev, cur, picks, 1, b, g)
        values.append(load_keys(prev, cur, picks, 2, b, g))
        wide_q = spread_heads(load_quad(*cur, slice(b * BLOCK, (b + 1) * BLOCK), 0, g))
        scored.append(dot_nt(keys, wide_q))
    for n, (b, g) in enumerate(CHAINS):
        scores = scored[n] * HEAD ** (-0.5)
        before = scores[:BLOCK] + edge if b == 0 else scores[:BLOCK]
        near = jnp.where(side, before, scores[BLOCK : 2 * BLOCK])
        far = scores[2 * BLOCK :] + bias_ref[b * TOPK : (b + 1) * TOPK]
        folded = jnp.concatenate([near, far], 0)
        top = jnp.max(folded, axis=0, keepdims=True)
        weights = jnp.exp(folded - top)
        probs = weights * (1.0 / jnp.sum(weights, axis=0, keepdims=True))
        probs_ref[b, g] = probs
        fulls.append(unfold(probs[:BLOCK], probs[BLOCK:], side))
    for n, (b, g) in enumerate(CHAINS):
        outs.append(gather_heads(dot_tn(fulls[n], values[n])).astype(jnp.bfloat16))
    for b in range(2):
        own, other = join_quads(outs[b * (HEADS // 4) : (b + 1) * (HEADS // 4)])
        here = slice(b * BLOCK, (b + 1) * BLOCK)
        att_ref[here, pl.ds(pl.multiple_of(core * HALF, 128), HALF)] = own
        att_ref[here, pl.ds(pl.multiple_of((1 - core) * HALF, 128), HALF)] = other


def attend(mixed_own, mixed_other, sel_col, bias_col, info, blocks, pool_rows):
    width = HEADS * HEAD
    halo = mixed_own.shape[0] // BLOCK - 1
    mixed_specs = [
        pl.BlockSpec((pool_rows, 3 * HALF), lambda c, f: (blocks * BLOCK // pool_rows, 0)),
        pl.BlockSpec((BLOCK, 3 * HALF), lambda c, f: (jnp.where(c == 0, halo, 2 * c - 1), 0)),
        pl.BlockSpec((PAIR, 3 * HALF), lambda c, f: (c, 0)),
    ]
    return pl.pallas_call(
        attend_kernel,
        grid_spec=pltpu.PrefetchScalarGridSpec(
            num_scalar_prefetch=1,
            grid=(blocks // 2,),
            in_specs=[
                pl.BlockSpec((blocks * TOPK, 1), lambda c, f: (0, 0)),
                pl.BlockSpec((2 * TOPK, 1), lambda c, f: (c, 0)),
            ]
            + mixed_specs * 2,
            out_specs=[
                pl.BlockSpec((PAIR, width), lambda c, f: (c, 0)),
                pl.BlockSpec((2, HEADS // 4, FOLD, QUAD), lambda c, f: (c, 0, 0, 0)),
                pl.BlockSpec((2, blocks * TOPK, 2 * HALF), lambda c, f: (0, 0, 0)),
            ],
        ),
        out_shape=[
            jax.ShapeDtypeStruct((blocks * BLOCK, width), jnp.bfloat16),
            jax.ShapeDtypeStruct((blocks, HEADS // 4, FOLD, QUAD), jnp.float32),
            jax.ShapeDtypeStruct((2, blocks * TOPK, 2 * HALF), jnp.bfloat16),
        ],
        compiler_params=pltpu.CompilerParams(vmem_limit_bytes=20 * 1024 * 1024),
        cost_estimate=pl.CostEstimate(
            flops=12_000_000_000, bytes_accessed=12_000_000, transcendentals=1_000_000
        ),
        name="attend",
    )(info, sel_col, bias_col, *[mixed_own] * 3, *[mixed_other] * 3)


def attend_back_kernel(
    pairs,
    info_ref,
    sel_ref,
    prev_own,
    cur_own,
    prev_other,
    cur_other,
    picks_ref,
    probs_ref,
    datt_ref,
    out_own,
    out_other,
    carry,
    dpicks,
):
    i = pl.program_id(0)
    core = info_ref[1]
    outs = (out_own, out_other)

    @pl.when(i == 0)
    def _():
        carry[...] = jnp.zeros_like(carry)

    @pl.when(i < pairs)
    def _():
        side = prev_side()
        datt = (
            datt_ref.at[:, pl.ds(pl.multiple_of(core * HALF, 128), HALF)],
            datt_ref.at[:, pl.ds(pl.multiple_of((1 - core) * HALF, 128), HALF)],
        )
        prev, cur = (prev_own, prev_other), (cur_own, cur_other)
        picks = (picks_ref.at[0], picks_ref.at[1])
        wide_qs, wide_ds, firsts, full_ps, full_ds = [], [], [], [], []
        for b, g in CHAINS:
            here = slice(b * BLOCK, (b + 1) * BLOCK)
            wide_qs.append(spread_heads(load_quad(*cur, here, 0, g)))
            wide_ds.append(spread_heads(load_quad(*datt, here, 0, g)))
            firsts.append(dot_nt(load_keys(prev, cur, picks, 2, b, g), wide_ds[-1]))
        for n, (b, g) in enumerate(CHAINS):
            probs, dprobs = probs_ref[b, g], firsts[n]
            near = jnp.where(side, dprobs[:BLOCK], dprobs[BLOCK : 2 * BLOCK])
            folded = jnp.concatenate([near, dprobs[2 * BLOCK :]], 0)
            inner = jnp.sum(probs * folded, axis=0, keepdims=True)
            dscores = probs * (folded - inner) * HEAD ** (-0.5)
            full_ps.append(unfold(probs[:BLOCK], probs[BLOCK:], side))
            full_ds.append(unfold(dscores[:BLOCK], dscores[BLOCK:], side))
        grads = []
        for n, (b, g) in enumerate(CHAINS):
            dvals = dot_nn(full_ps[n], wide_ds[n])
            dkeys = dot_nn(full_ds[n], wide_qs[n])
            dq = gather_heads(dot_tn(full_ds[n], load_keys(prev, cur, picks, 1, b, g)))
            grads.append((dq, dkeys, dvals))
        for part in range(3):
            lanes = slice(part * HALF, (part + 1) * HALF)
            a = join_quads([grad[part] for grad in grads[: HEADS // 4]])
            b = join_quads([grad[part] for grad in grads[HEADS // 4 :]])
            for s, out_ref in enumerate(outs):
                if part == 0:
                    out_ref[:, lanes] = carry[s, :, lanes].astype(jnp.bfloat16)
                    carry[s, :BLOCK, lanes] = a[s]
                    carry[s, BLOCK:, lanes] = b[s]
                else:
                    out_ref[:BLOCK, lanes] = carry[s, :BLOCK, lanes].astype(jnp.bfloat16)
                    low = carry[s, BLOCK:, lanes] + a[s][:BLOCK]
                    out_ref[BLOCK:, lanes] = low.astype(jnp.bfloat16)
                    carry[s, :BLOCK, lanes] = a[s][BLOCK : 2 * BLOCK] + b[s][:BLOCK]
                    carry[s, BLOCK:, lanes] = b[s][BLOCK : 2 * BLOCK]
                    both = jnp.concatenate([a[s][2 * BLOCK :], b[s][2 * BLOCK :]], 0)
                    rows = pl.ds(pl.multiple_of(i * 2 * TOPK, 2 * TOPK), 2 * TOPK)
                    picked = slice((part - 1) * HALF, part * HALF)
                    dpicks[s, rows, picked] = both.astype(jnp.bfloat16)

    @pl.when(i == pairs)
    def _():
        out_own[...] = carry[0].astype(jnp.bfloat16)
        out_other[...] = carry[1].astype(jnp.bfloat16)

    @pl.when(i > pairs)
    def _():
        ids = lax.broadcasted_iota(jnp.int32, (PAIR, 2 * pairs * TOPK), 0) + (i - pairs - 1) * PAIR
        one_hot = (ids == sel_ref[...]).astype(jnp.float32).astype(jnp.bfloat16)
        for s, out_ref in enumerate(outs):
            out_ref[:, :HALF] = jnp.zeros((PAIR, HALF), jnp.bfloat16)
            out_ref[:, HALF:] = dot_nn(one_hot, dpicks[s]).astype(jnp.bfloat16)


def attend_back(mixed_own, mixed_other, sel_row, info, picks, probs, datt, blocks, pool_rows):
    width = HEADS * HEAD
    pairs = blocks // 2
    total = mixed_own.shape[0]
    halo = total // BLOCK - 1

    def pair(i):
        return jnp.minimum(i, pairs - 1)

    def before_block(i, f):
        return (jnp.where(i == 0, halo, 2 * pair(i) - 1), 0)

    def out_block(i, f):
        return (jnp.where(i == 0, total // PAIR - 1, i - 1), 0)

    mixed_specs = [
        pl.BlockSpec((BLOCK, 3 * HALF), before_block),
        pl.BlockSpec((PAIR, 3 * HALF), lambda i, f: (pair(i), 0)),
    ]
    return pl.pallas_call(
        partial(attend_back_kernel, pairs),
        grid_spec=pltpu.PrefetchScalarGridSpec(
            num_scalar_prefetch=1,
            grid=(pairs + 1 + pool_rows // PAIR,),
            in_specs=[pl.BlockSpec((1, blocks * TOPK), lambda i, f: (0, 0))]
            + mixed_specs * 2
            + [
                pl.BlockSpec((2, 2 * TOPK, 2 * HALF), lambda i, f: (0, pair(i), 0)),
                pl.BlockSpec((2, HEADS // 4, FOLD, QUAD), lambda i, f: (pair(i), 0, 0, 0)),
                pl.BlockSpec((PAIR, width), lambda i, f: (pair(i), 0)),
            ],
            out_specs=[pl.BlockSpec((PAIR, 3 * HALF), out_block)] * 2,
            scratch_shapes=[
                pltpu.VMEM((2, PAIR, 3 * HALF), jnp.float32),
                pltpu.VMEM((2, blocks * TOPK, 2 * HALF), jnp.bfloat16),
            ],
        ),
        out_shape=[jax.ShapeDtypeStruct((total, 3 * HALF), jnp.bfloat16)] * 2,
        compiler_params=pltpu.CompilerParams(vmem_limit_bytes=20 * 1024 * 1024),
        cost_estimate=pl.CostEstimate(
            flops=20_000_000_000, bytes_accessed=18_000_000, transcendentals=0
        ),
        name="attend_back",
    )(info, sel_row, *[mixed_own] * 2, *[mixed_other] * 2, picks, probs, datt)


def standardize(values):
    center = values - jnp.mean(values, axis=-1, keepdims=True)
    spread = jnp.mean(center * center, axis=-1, keepdims=True)
    scale = lax.rsqrt(spread + 1e-05)
    return center * scale, scale


def standardize_back(unit, scale, dunit):
    return scale * (
        dunit
        - jnp.mean(dunit, axis=-1, keepdims=True)
        - unit * jnp.mean(dunit * unit, axis=-1, keepdims=True)
    )


ROWS = 256
CHUNK = 768
GROUP = 48
MIB = 1024 * 1024


def params(mib):
    return pltpu.CompilerParams(vmem_limit_bytes=mib * MIB)


def shape(rows, columns, dtype=jnp.bfloat16):
    return jax.ShapeDtypeStruct((rows, columns), dtype)


def cost(flops, moved):
    return pl.CostEstimate(flops=flops, bytes_accessed=moved, transcendentals=0)


def lanes_at(index, size):
    return pl.ds(pl.multiple_of(index * size, 128), size)


def pool_kernel(tokens_ref, unit_ref, out_ref):
    for b in range(out_ref.shape[0]):
        rows = slice(b * BLOCK, (b + 1) * BLOCK)
        unit, _ = standardize(tokens_ref[rows].astype(jnp.float32))
        unit_ref[rows] = unit
        out_ref[b : b + 1] = jnp.mean(unit, axis=0, keepdims=True)


def pool(tokens):
    rows, width = tokens.shape
    return pl.pallas_call(
        pool_kernel,
        out_shape=[shape(rows, width, jnp.float32), shape(rows // BLOCK, width, jnp.float32)],
        compiler_params=params(24),
        cost_estimate=cost(2_000_000_000, 6_000_000),
        name="pool",
    )(tokens)


def normal_kernel(own_ref, pool_ref, halo_ref, vec_ref, normed_ref, unit_ref):
    gain, bias = vec_ref[0:1], vec_ref[1:2]
    start = 0
    for ref in (own_ref, pool_ref, halo_ref):
        for r in range(0, ref.shape[0], BLOCK):
            unit = ref[r : r + BLOCK].astype(jnp.float32)
            if ref is halo_ref:
                unit, _ = standardize(unit)
                rows = slice(start, start + BLOCK)
                unit_ref[rows] = jnp.zeros(unit.shape, jnp.bfloat16)
                normed_ref[rows] = jnp.zeros(unit.shape, jnp.bfloat16)
                start += BLOCK
            rows = slice(start, start + BLOCK)
            unit_ref[rows] = unit.astype(jnp.bfloat16)
            normed_ref[rows] = (unit * gain + bias).astype(jnp.bfloat16)
            start += BLOCK


def normal(unit_own, unit_pool, halo, vectors):
    width = unit_own.shape[1]
    total = unit_own.shape[0] + unit_pool.shape[0] + 2 * halo.shape[0]
    return pl.pallas_call(
        normal_kernel,
        out_shape=[shape(total, width), shape(total, width)],
        compiler_params=params(24),
        cost_estimate=cost(2_000_000_000, 10_000_000),
        name="normal",
    )(unit_own, unit_pool, halo, vectors)


def mlp_kernel(
    info_ref,
    att_ref,
    tokens_ref,
    dy_ref,
    vec_ref,
    out_own,
    out_other,
    up_own,
    up_other,
    down_ref,
    output_ref,
    dafter_ref,
    datt_ref,
    gd_own,
    gd_other,
    gu_own,
    gu_other,
    sums_ref,
    after_ref,
    n2_ref,
    active_ref,
    dh_ref,
    dn2_ref,
    total_ref,
    grad_ref,
    acc,
    low,
):
    i = pl.program_id(0)
    core = info_ref[1]
    side = out_own.shape[1]
    count, width = n2_ref.shape
    row_steps = count // ROWS
    steps = pl.num_programs(0) - 2 * row_steps
    half = steps // 2
    j = i - row_steps

    @pl.when(i < row_steps)
    def _():
        rows = pl.ds(pl.multiple_of(i * ROWS, ROWS), ROWS)
        after_ref[rows, lanes_at(core, side)] = dot_nn(att_ref[rows], out_own[...])
        after_ref[rows, lanes_at(1 - core, side)] = dot_nn(att_ref[rows], out_other[...])
        after = tokens_ref[...].astype(jnp.float32) + after_ref[rows]
        after_ref[rows] = after
        unit, _ = standardize(after)
        n2_ref[rows] = (unit * vec_ref[2:3] + vec_ref[3:4]).astype(jnp.bfloat16)
        dn2_ref[rows] = jnp.zeros((ROWS, width), jnp.float32)
        total_ref[rows] = after

    @pl.when((j >= 0) & (j < steps))
    def _():
        weight = jnp.where(j < half, up_own[...], up_other[...])
        down = down_ref[...]
        root = (2.0 / 3.141592653589793) ** 0.5

        def first(r):
            rows = slice(r, r + ROWS)
            return rows, dot_nn(n2_ref[rows], weight), dot_nt(dy_ref[rows], down)

        def second(rows, u, dactive):
            square = u * u
            t = jnp.tanh(u * (root + (0.044715 * root) * square))
            upper = 0.5 + 0.5 * t
            active = u * upper
            bend = active * ((1.0 - t) * (root + (3.0 * 0.044715 * root) * square))
            active = active.astype(jnp.bfloat16)
            dh = (dactive * (upper + bend)).astype(jnp.bfloat16)
            active_ref[rows] = active
            dh_ref[rows] = dh
            dn2_ref[rows] += dot_nt(dh, weight)
            total_ref[rows] += dot_nn(active, down)

        waiting = first(0)
        for r in range(ROWS, count, ROWS):
            coming = first(r)
            second(*waiting)
            waiting = coming
        second(*waiting)
        grad_ref[...] = dot_tn(active_ref[...], dy_ref[...]).astype(jnp.bfloat16)
        per = gd_own.shape[1] // side
        for s in range(gd_own.shape[0] // GROUP):
            for g in range(per):
                rows = slice((s * per + g) * GROUP, (s * per + g + 1) * GROUP)
                to = (slice(s * GROUP, (s + 1) * GROUP), slice(g * side, (g + 1) * side))
                gd_own[to] = grad_ref[rows, lanes_at(core, side)]
                gd_other[to] = grad_ref[rows, lanes_at(1 - core, side)]
        grad = dot_tn(n2_ref[...], dh_ref[...]).astype(jnp.bfloat16)

        @pl.when(j < half)
        def _():
            gu_own[:, lanes_at(j, CHUNK)] = grad

        @pl.when(j >= half)
        def _():
            gu_other[:, lanes_at(j - half, CHUNK)] = grad

    @pl.when(j == steps)
    def _():
        sums_ref[...] = jnp.zeros_like(sums_ref)
        acc[...] = jnp.zeros_like(acc)

    @pl.when(j >= steps)
    def _():
        rows = pl.ds(pl.multiple_of((j - steps) * ROWS, ROWS), ROWS)
        output_ref[...] = total_ref[rows].astype(jnp.bfloat16)
        unit, scale = standardize(after_ref[rows])
        dn2 = dn2_ref[rows]
        sums_ref[0:1] += jnp.sum(dn2 * unit, axis=0, keepdims=True)
        sums_ref[1:2] += jnp.sum(dn2, axis=0, keepdims=True)
        dafter = dy_ref[rows].astype(jnp.float32)
        dafter += standardize_back(unit, scale, dn2 * vec_ref[2:3])
        dafter_ref[...] = dafter
        low[...] = dafter.astype(jnp.bfloat16)
        datt = dot_nt(low[:, lanes_at(core, side)], out_own[...])
        datt += dot_nt(low[:, lanes_at(1 - core, side)], out_other[...])
        datt_ref[...] = datt.astype(jnp.bfloat16)
        acc[...] += dot_tn(att_ref[rows], low[...])

    @pl.when(i == pl.num_programs(0) - 1)
    def _():
        at = gu_own.shape[1] - side
        gu_own[:, at:] = acc[:, lanes_at(core, side)].astype(jnp.bfloat16)
        gu_other[:, at:] = acc[:, lanes_at(1 - core, side)].astype(jnp.bfloat16)


def ff_maps(hidden, before):
    steps = hidden // CHUNK
    half = steps // 2
    step = lambda i: jnp.clip(i - before, 0, steps - 1)
    own = lambda i, f: (0, jnp.minimum(step(i), half - 1))
    other = lambda i, f: (0, jnp.maximum(step(i) - half, 0))
    place = lambda i, f: lax.rem(f[1] * half + step(i), steps)
    return steps, own, other, place


def out_columns(own):
    width = own.shape[0]
    half = width // 2
    return pl.BlockSpec((width, half), lambda i, f: (0, own.shape[1] // half - 1))


def mlp(attended, tokens, upstream, vectors, own, other, mat_down, info):
    count, width = tokens.shape
    hidden = mat_down.shape[0]
    row_steps = count // ROWS
    steps, first, second, place = ff_maps(hidden, row_steps)
    whole = lambda i, f: (0, 0)
    once = pl.Buffered(1)
    full = pl.BlockSpec((count, width), whole, pipeline_mode=once)
    grads = pl.BlockSpec(own.shape, whole, pipeline_mode=once)
    low_grads = pl.BlockSpec((CHUNK // 4, 2 * width), lambda i, f: (place(i, f), 0))
    row = pl.BlockSpec((ROWS, width), lambda i, f: (jnp.maximum(i - row_steps - steps, 0), 0))
    f32 = jnp.float32
    return pl.pallas_call(
        mlp_kernel,
        grid_spec=pltpu.PrefetchScalarGridSpec(
            num_scalar_prefetch=1,
            grid=(2 * row_steps + steps,),
            in_specs=[
                full,
                pl.BlockSpec((ROWS, width), lambda i, f: (jnp.minimum(i, row_steps - 1), 0)),
                full,
                pl.BlockSpec(vectors.shape, whole),
                out_columns(own),
                out_columns(other),
                pl.BlockSpec((width, CHUNK), first),
                pl.BlockSpec((width, CHUNK), second),
                pl.BlockSpec((CHUNK, width), lambda i, f: (place(i, f), 0)),
            ],
            out_specs=[
                row,
                row,
                row,
                low_grads,
                low_grads,
                grads,
                grads,
                pl.BlockSpec((8, width), whole),
            ],
            scratch_shapes=[
                pltpu.VMEM((count, width), f32),
                pltpu.VMEM((count, width), jnp.bfloat16),
                pltpu.VMEM((count, CHUNK), jnp.bfloat16),
                pltpu.VMEM((count, CHUNK), jnp.bfloat16),
                pltpu.VMEM((count, width), f32),
                pltpu.VMEM((count, width), f32),
                pltpu.VMEM((CHUNK, width), jnp.bfloat16),
                pltpu.VMEM((width, width), f32),
                pltpu.VMEM((ROWS, width), jnp.bfloat16),
            ],
        ),
        out_shape=[
            shape(count, width),
            shape(count, width, f32),
            shape(count, width),
            shape(hidden // 4, 2 * width),
            shape(hidden // 4, 2 * width),
            shape(*own.shape),
            shape(*own.shape),
            shape(8, width, f32),
        ],
        compiler_params=params(58),
        cost_estimate=cost(40_000_000_000, 30_000_000),
        name="mlp",
    )(info, attended, tokens, upstream, vectors, own, other, own, other, mat_down)


def project_back_kernel(dm_own, dm_other, own_ref, other_ref, unit_ref, dn_ref, sums_ref):
    @pl.when(pl.program_id(0) == 0)
    def _():
        sums_ref[...] = jnp.zeros_like(sums_ref)

    dn = dot_nt(dm_own[...], own_ref[...]) + dot_nt(dm_other[...], other_ref[...])
    dn_ref[...] = dn.astype(jnp.bfloat16)
    sums_ref[0:1] += jnp.sum(dn * unit_ref[...].astype(jnp.float32), axis=0, keepdims=True)
    sums_ref[1:2] += jnp.sum(dn, axis=0, keepdims=True)


def project_back(dm_own, dm_other, own, other, unit):
    total, width = unit.shape
    rows = total // 4
    row = lambda i: (i, 0)
    once = pl.Buffered(1)
    whole = pl.BlockSpec((width, 3 * HALF), lambda i: (0, 0), pipeline_mode=once)
    return pl.pallas_call(
        project_back_kernel,
        grid=(total // rows,),
        in_specs=[
            pl.BlockSpec((rows, 3 * HALF), row),
            pl.BlockSpec((rows, 3 * HALF), row),
            whole,
            whole,
            pl.BlockSpec((rows, width), row),
        ],
        out_specs=[pl.BlockSpec((rows, width), row), pl.BlockSpec((8, width), lambda i: (0, 0))],
        out_shape=[shape(total, width), shape(8, width, jnp.float32)],
        compiler_params=params(60),
        cost_estimate=cost(6_000_000_000, 16_000_000),
        name="project_back",
    )(dm_own, dm_other, own, other, unit)


def input_kernel(tokens_ref, dn_ref, dafter_ref, pool_ref, next_ref, vec_ref, out_ref):
    i = pl.program_id(0)
    gain = vec_ref[0:1]
    per = tokens_ref.shape[0] // BLOCK
    last = (i == pl.num_programs(0) - 1).astype(jnp.float32)
    for b in range(per):
        rows = slice(b * BLOCK, (b + 1) * BLOCK)
        unit, scale = standardize(tokens_ref[rows].astype(jnp.float32))
        dn = dn_ref[rows].astype(jnp.float32) + pool_ref[pl.ds(i * per + b, 1)] * (1.0 / BLOCK)
        if b == per - 1:
            dn += next_ref[...].astype(jnp.float32) * last
        out_ref[rows] = dafter_ref[rows] + standardize_back(unit, scale, dn * gain)


def input_back(tokens, dnormed, dafter, from_pool, from_next, vectors):
    count, width = tokens.shape
    row = pl.BlockSpec((ROWS, width), lambda i: (i, 0))
    whole = lambda i: (0, 0)
    return pl.pallas_call(
        input_kernel,
        grid=(count // ROWS,),
        in_specs=[
            row,
            row,
            row,
            pl.BlockSpec(from_pool.shape, whole),
            pl.BlockSpec(from_next.shape, whole),
            pl.BlockSpec(vectors.shape, whole),
        ],
        out_specs=row,
        out_shape=shape(count, width, jnp.float32),
        compiler_params=params(60),
        cost_estimate=cost(3_000_000_000, 12_000_000),
        name="input_back",
    )(tokens, dnormed, dafter, from_pool, from_next, vectors)


def shift_seq(value, distance):
    size = lax.axis_size("seq")
    route = [(i - distance, i) for i in range(size) if 0 <= i - distance < size]
    return lax.ppermute(value, "seq", route)


BOTH = ("seq", "batch")


def follows(value, *earlier):
    return lax.optimization_barrier((value, earlier))[0]


def flip_route(size, bit):
    return [(i, i ^ bit) for i in range(size)]


def ring_route(size, stride, steps):
    return [(i, (i + stride * steps) % size) for i in range(size)]


def swap(value, axis, bit):
    return lax.ppermute(value, axis, flip_route(lax.axis_size(axis), bit))


def in_order(bit, own, other):
    return jnp.stack([jnp.where(bit == 0, own, other), jnp.where(bit == 0, other, own)])


def pick(value, index, axis):
    return lax.dynamic_index_in_dim(value, index, axis, keepdims=False)


def add(a, b):
    return (a.astype(jnp.float32) + b.astype(jnp.float32)).astype(jnp.bfloat16)


def place():
    at = lax.axis_index("seq")
    return at // 4, at // 2 % 2, at % 2


def send_line(slab):
    size = lax.axis_size("seq")
    return [lax.ppermute(slab, "seq", ring_route(size, 4, k)) for k in range(1, size // 4)]


def join_line(slab, got):
    z = place()[0]
    stack = jnp.stack([slab] + got)
    layers = stack.shape[0]
    parts = [lax.dynamic_slice_in_dim(stack, (z - k) % layers, 1, 0) for k in range(layers)]
    return jnp.concatenate(parts, 0)


def send_near(line, cut):
    first, second = line[:, :, :cut], line[:, :, cut:]
    return first, second, swap(first, "seq", 1), swap(second, "seq", 2)


def join_near(first, second, first_got, second_got):
    _, y, x = place()
    return in_order(x, first, first_got), in_order(y, second, second_got)


def send_far(first, second):
    return swap(first, "seq", 2), swap(second, "seq", 1)


def join_far(first, second, first_got, second_got):
    _, y, x = place()
    first = jnp.transpose(in_order(y, first, first_got), (2, 0, 1, 3, 4))
    second = jnp.transpose(in_order(x, second, second_got), (2, 1, 0, 3, 4))
    rows = first.shape[3] * lax.axis_size("seq")
    return first.reshape(rows, -1), second.reshape(rows, -1)


def sum_grids(a, b, cut):
    cuts = (slice(None, cut), slice(cut, None))
    sums = [add(a[:, columns], b[:, columns]) for columns in cuts]
    layers = lax.axis_size("seq") // 4
    return [part.reshape(layers, 2, 2, -1, part.shape[1]) for part in sums]


def drop_near(first, second):
    _, y, x = place()
    return pick(first, 1 - x, 2), pick(second, 1 - y, 1)


def keep_near(first, second, first_got, second_got):
    _, y, x = place()
    return add(pick(first, x, 2), first_got), add(pick(second, y, 1), second_got)


def drop_far(first, second):
    _, y, x = place()
    return pick(first, 1 - y, 1), pick(second, 1 - x, 1)


def keep_far(first, second, first_got, second_got, axis=2):
    _, y, x = place()
    parts = [add(pick(first, y, 1), first_got), add(pick(second, x, 1), second_got)]
    return jnp.concatenate(parts, axis)


def swap_near(dropped):
    return swap(dropped[0], "seq", 1), swap(dropped[1], "seq", 2)


def swap_far(dropped):
    return swap(dropped[0], "seq", 2), swap(dropped[1], "seq", 1)


def spread_line(line):
    size = lax.axis_size("seq")
    groups = [list(range(n, size, 4)) for n in range(4)]
    return lax.all_to_all(line, "seq", 0, 0, axis_index_groups=groups)


def scatter_line(line):
    z = place()[0]
    size = lax.axis_size("seq")
    layers = size // 4
    got = [
        lax.ppermute(pick(line, (z + k) % layers, 0), "seq", ring_route(size, 4, k))
        for k in range(1, layers)
    ]
    return pick(line, z, 0), got


def sum_line(own, got):
    return sum((g.astype(jnp.float32) for g in got), own.astype(jnp.float32))


def paired():
    return lax.axis_size("batch") == 2 and lax.axis_size("seq") % 4 == 0


def side_index():
    return lax.axis_index("batch") % 2


def halves_of(matrix, groups):
    parts = jnp.split(matrix, 2 * groups, 1)
    return jnp.stack([jnp.concatenate(parts[h::2], 1) for h in range(2)])


def whole_of(halves, groups):
    parts = [jnp.split(half, groups, 1) for half in halves]
    return jnp.concatenate([half[g] for g in range(groups) for half in parts], 1)


def local(
    inputs, selection, cotangent, ln1_gain, ln1_bias, w_qkv, w_out, ln2_gain, ln2_bias, w_up, w_down
):
    bf16, f32 = jnp.bfloat16, jnp.float32
    tokens = inputs[0]
    chosen = selection[0]
    upstream = cotangent[0]
    count, width = tokens.shape
    hidden = w_up.shape[1]
    blocks = count // BLOCK
    size = lax.axis_size("seq")
    pool_rows = blocks * size
    at = lax.axis_index("seq")
    side = side_index()
    fast = paired()

    half_qkv = halves_of(w_qkv, 3)
    half_uo = jnp.concatenate([halves_of(w_up, 1), halves_of(w_out, 1)], 2)
    vectors = jnp.stack([ln1_gain, ln1_bias, ln2_gain, ln2_bias])
    if fast:
        columns = jnp.pad(vectors.T, ((0, 0), (0, 124)))
        columns = jnp.broadcast_to(columns, (2,) + columns.shape)
        bundle = jnp.concatenate([columns, half_qkv, half_uo], 2)
        got = swap(pick(bundle, 1 - side, 0), "batch", 1)
        slab = in_order(side, pick(bundle, side, 0), got).reshape(-1, bundle.shape[2])
        third = width // 3
        per = slab.shape[0] // 3
        unit_own, pooled = pool(tokens)
        pooled = jnp.transpose(pooled.astype(bf16).reshape(per, 3, third), (1, 0, 2))
        pooled = pooled.reshape(-1, third)
        front = third + 128
        edge = 128 + half_qkv.shape[2]
        slab_q = jnp.concatenate([pooled, slab[:, :edge]], 1)
        slab_u = slab[:, edge:]
        line_got = send_line(slab_q)
        halo = shift_seq(follows(tokens[-BLOCK:], slab), 1)
        line_got_u = send_line(slab_u)
        line_q = join_line(slab_q, follows(line_got, halo))
        near = send_near(line_q, 768)
        wide_q = join_near(*near)
        far = send_far(*wide_q)
        line_u = join_line(slab_u, follows(line_got_u, wide_q))
        near_u = send_near(line_u, 1024)
        first, second = join_far(*wide_q, *follows(far, near_u[0], near_u[1]))
        own_qkv = jnp.concatenate([first[:, front:], second], 1)
        other_qkv = swap(own_qkv, "batch", 1)
        unit_pool = jnp.transpose(first[:, :third].reshape(size, 3, per, third), (0, 2, 1, 3))
        unit_pool = unit_pool.reshape(pool_rows, width)
        vectors = first[:, third : third + 4].T.astype(f32)
    else:
        gathered = lax.all_gather(half_qkv, BOTH, axis=1, tiled=True)
        own_qkv, other_qkv = pick(gathered, side, 0), pick(gathered, 1 - side, 0)
        gathered = lax.all_gather(half_uo, BOTH, axis=1, tiled=True)
        own_uo, other_uo = pick(gathered, side, 0), pick(gathered, 1 - side, 0)
        halo = shift_seq(tokens[-BLOCK:], 1)
        unit_own, pooled = pool(tokens)
        unit_pool = lax.all_gather(pooled.astype(bf16), "seq", axis=0, tiled=True)
        vectors = lax.all_gather(vectors, BOTH, axis=1, tiled=True).astype(f32)
    mat_down = lax.all_gather(w_down, BOTH, axis=0, tiled=True)
    vectors = jnp.pad(vectors, ((0, 4), (0, 0)))

    normed, unit = normal(unit_own, unit_pool, halo, vectors)
    mixed_own = dot_nn(normed, own_qkv).astype(bf16)
    mixed_other = dot_nn(normed, other_qkv).astype(bf16)
    if fast:
        wide_u = join_near(*follows(near_u, mixed_other))
        far_u = send_far(*wide_u)
        mixed_own = follows(mixed_own, wide_u)

    block_ids = at * blocks + jnp.arange(blocks, dtype=jnp.int32)
    flat = chosen.reshape(blocks * TOPK)
    far_bias = jnp.where(chosen < block_ids[:, None], 0.0, NEG).reshape(blocks * TOPK, 1)
    info = jnp.stack([(at == 0).astype(jnp.int32), side])
    attended, probs, picks = attend(
        mixed_own, mixed_other, flat[:, None], far_bias, info, blocks, pool_rows
    )
    if fast:
        own_uo = jnp.concatenate(join_far(*wide_u, *follows(far_u, attended)), 1)
        other_uo = swap(own_uo, "batch", 1)
    output, dafter, dattended, down_own, down_other, uo_own, uo_other, sums_two = mlp(
        attended, tokens, upstream, vectors, own_uo, other_uo, mat_down, info
    )
    if fast:
        down_got = swap(down_other, "batch", 1)
        uo_got = swap(uo_other, "batch", 1)
        grid_d = sum_grids(down_own, down_got, width)
        drop_d = drop_near(*grid_d)
        near_d = swap_near(drop_d)
        grid_u = sum_grids(uo_own, follows(uo_got, drop_d), 1024)
        drop_u = drop_near(*grid_u)
        near_u = swap_near(drop_u)
        dattended = follows(dattended, drop_u)

    dmixed_own, dmixed_other = attend_back(
        mixed_own, mixed_other, flat[None, :], info, picks, probs, dattended, blocks, pool_rows
    )
    if fast:
        kept_d = keep_near(*grid_d, *follows(near_d, dmixed_own))
        drop_d = drop_far(*kept_d)
        far_d = swap_far(drop_d)
        dmixed_other = follows(dmixed_other, drop_d)
    grad_other = dot_tn(normed, dmixed_other).astype(bf16)
    if fast:
        grad_got = swap(grad_other, "batch", 1)
        kept_u = keep_near(*grid_u, *follows(near_u, grad_other))
        drop_u = drop_far(*kept_u)
        far_u = swap_far(drop_u)
        dmixed_own = follows(dmixed_own, drop_u)
    grad_own = dot_tn(normed, dmixed_own).astype(bf16)
    if fast:
        grid_q = sum_grids(grad_own, grad_got, 512)
        drop_q = drop_near(*grid_q)
        near_q = swap_near(drop_q)
        line_d = keep_far(*kept_d, *follows(far_d, drop_q))
        got_d = spread_line(line_d)
        dmixed_own = follows(dmixed_own, line_d)
    dnormed, sums_one = project_back(dmixed_own, dmixed_other, own_qkv, other_qkv, unit)
    vector_grads = jnp.concatenate([sums_one[:2], sums_two[:2]], 0)
    from_next = shift_seq(dnormed[-BLOCK:], -1)
    dpool = dnormed[count : count + pool_rows]
    if fast:
        got_d, near_q, far_u = follows((got_d, near_q, far_u), dnormed)
        sum_d = jnp.sum(got_d.astype(f32), axis=0)
        kept_q = keep_near(*grid_q, *near_q)
        drop_q = drop_far(*kept_q)
        far_q = swap_far(drop_q)
        spread = jnp.transpose(vector_grads.reshape(4, size, -1), (1, 0, 2)).reshape(size, 1, -1)
        span = spread.shape[2]
        spread = jnp.pad(spread.astype(bf16), ((0, 0), (0, 7), (0, width - span)))
        send = jnp.concatenate([dpool.reshape(size, blocks, width), spread], 1)
        pool_got = lax.all_to_all(send, "seq", 0, 0)
        line_u = keep_far(*kept_u, *follows(far_u, drop_q))
        line_u, got_u = scatter_line(line_u)
        line_q = keep_far(*kept_q, *follows(far_q, send, line_u))
        line_q, got_q = scatter_line(line_q)
        got = jnp.sum(follows(pool_got, line_q).astype(f32), axis=0)
        from_pool = got[:blocks]
        chip = got[blocks, :span].reshape(4, 2, -1)
    else:
        from_pool = lax.psum_scatter(dpool, "seq", scatter_dimension=0, tiled=True).astype(f32)
        vector_sums = lax.psum_scatter(vector_grads, BOTH, scatter_dimension=1, tiled=True)
    input_grad = input_back(tokens, dnormed, dafter, from_pool, from_next, vectors)
    if fast:
        got_u, got_q = follows((got_u, got_q), input_grad)
        total_d = jnp.stack(jnp.split(sum_d, 2, 1))
        got = swap(pick(follows(total_d, line_q), 1 - side, 0), "batch", 1)
        both_d = in_order(side, pick(total_d, side, 0), got)
        sum_down = jnp.concatenate([whole_of(g, 1) for g in jnp.split(both_d, 2, 2)], 0)
        total_u = sum_line(line_u, got_u).reshape(2, GROUP // 2, -1)
        total_q = sum_line(line_q, got_q).reshape(2, GROUP // 2, -1)
        chip = jnp.pad(jnp.transpose(chip, (1, 2, 0)), ((0, 0), (0, 0), (0, 124)))
        bundle = jnp.concatenate([total_u, total_q, chip], 2)
        mine = pick(bundle, side, 0)
        got = swap(pick(bundle, 1 - side, 0), "batch", 1)
        both = in_order(side, mine, got)
        sum_uo, sum_qkv = both[:, :, : total_u.shape[2]], both[:, :, total_u.shape[2] : -128]
        vector_sums = (mine[:, -128:] + got[:, -128:])[:, :4].T
    else:

        def scatter(own, other):
            full = in_order(side, own, other)
            sums = lax.psum_scatter(full, BOTH, scatter_dimension=1, tiled=True)
            return sums.astype(f32)

        sum_uo = scatter(uo_own, uo_other)
        sum_qkv = scatter(grad_own, grad_other)
        full = jnp.stack([down_own, down_other]).reshape(2, -1, GROUP, 4, width // 2)
        full = jnp.transpose(full, (1, 3, 2, 0, 4)).reshape(hidden, 2, width // 2)
        full = in_order(side, full[:, 0], full[:, 1])
        full = jnp.transpose(full, (1, 0, 2)).reshape(hidden, width)
        sum_down = lax.psum_scatter(full, BOTH, scatter_dimension=0, tiled=True).astype(f32)

    split = hidden // 2
    return (
        output[None],
        input_grad[None],
        vector_sums[0],
        vector_sums[1],
        whole_of(sum_qkv, 3),
        whole_of(sum_uo[:, :, split:], 1),
        vector_sums[2],
        vector_sums[3],
        whole_of(sum_uo[:, :, :split], 1),
        sum_down,
    )


def solution(mesh):
    tokens = P("batch", "seq", None)
    vector = P(BOTH)
    matrix = P(BOTH, None)
    return jax.shard_map(
        local,
        mesh=mesh,
        in_specs=(
            tokens,
            tokens,
            tokens,
            vector,
            vector,
            matrix,
            matrix,
            vector,
            vector,
            matrix,
            matrix,
        ),
        out_specs=(
            tokens,
            tokens,
            vector,
            vector,
            matrix,
            matrix,
            vector,
            vector,
            matrix,
            matrix,
        ),
        check_vma=False,
    )
```
